32 devices in a mesh: wall: 2 (over x), stream: 4 (over y, core), span: 4 (over z).
Axes of the slice: x: 2, y: 2, z: 4, core: 2. Of those that a mesh axis runs over, the one named last changes fastest.
Arguments:
- potential: float32 [64, 64, 512], P('wall', 'span', 'stream'), may hold values from -1.2 to 1.2
- concentration: float32 [3, 64, 64, 512], P(None, 'wall', 'span', 'stream'), may hold values from 0.2 to 3
- permittivity: float32 [64, 64, 512], P('wall', 'span', 'stream'), may hold values from 0.5 to 2
- fixed_charge: float32 [64, 64, 512], P('wall', 'span', 'stream'), may hold values from -6 to 6
Outputs:
- update: float32 [4, 64, 64, 512], P(None, 'wall', 'span', 'stream')
The draws below stay inside these ranges and needn't reach their ends.
All inputs are finite; a program needn't handle non-finite values.
Results may differ from the reference program's by a relative error of at most 0.0003.
Values sent between devices are 32-bit elements; how exact they have to be, the bound alone decides.
No kernel may reach another device: no remote copies, remote signals or barrier semaphores. Data moves between devices by JAX's collectives and lax.ppermute only.
A program may use at most 128 MiB of HBM per device.

```python
import math
import jax
import jax.numpy as jnp
from jax import lax

NW = 64
NP = 64
NS = 512


def steps_of(own_key, dims, pieces, least, top_value):
    def one(dim, blocks):
        draws = jax.random.uniform(jax.random.fold_in(jax.random.fold_in(own_key, 6), dim), (blocks,), jnp.float32, least / len(pieces), top_value / len(pieces))
        return jnp.repeat(jnp.exp(draws), dims[dim] // blocks).reshape((-1,) + (1,) * (len(dims) - dim - 1))

    loudness = one(*pieces[0])
    for cut in pieces[1:]:
        loudness = loudness * one(*cut)
    return loudness


def centred(key, shape, scale, limit, split=(), kind=jnp.bfloat16):
    gain = steps_of(key, shape, split, -0.22, 0.18) if split else 1.0
    values = jax.random.normal(key, shape, jnp.float32) * scale * gain
    return jnp.minimum(jnp.maximum(values, -limit), limit).astype(kind)


def setup_inputs(seed: int = 0) -> dict:
    keys = jax.random.split(jax.random.key(seed), 5)
    potential = centred(keys[0], (NW, NP, NS), 0.3, 1.2, ((0, 2), (1, 4), (2, 4)), jnp.float32)
    concentration = jnp.clip(jnp.exp(math.log(3.0) - 2.7080502 * jax.random.uniform(keys[1], (3, NW, NP, NS), jnp.float32) ** steps_of(keys[1], (3, NW, NP, NS), ((1, 2), (2, 4), (3, 4)), -0.2, 0.2)), 0.2, 3.0)
    permittivity = jnp.clip(jnp.exp(math.log(2.0) - 1.3862944 * jax.random.uniform(keys[2], (NW, NP, NS), jnp.float32) ** steps_of(keys[2], (NW, NP, NS), ((0, 2), (1, 4), (2, 4)), -0.2, 0.2)), 0.5, 2.0)
    fixed_charge = centred(keys[3], (NW, NP, NS), 1.0, 6.0, ((0, 2), (1, 4), (2, 4)), jnp.float32)
    return dict(potential=potential, concentration=concentration, permittivity=permittivity, fixed_charge=fixed_charge)


VALENCE = (1.0, -1.0, 2.0)
MOBILITY = (1.0, 1.5, 0.7)
PLANE_WEIGHT = 0.01


def bernoulli(values):
    near_zero = jnp.abs(values) < 1e-3
    safe_values = jnp.where(near_zero, 1.0, values)
    series = 1.0 - 0.5 * values + values * values / 12.0
    return jnp.where(near_zero, series, safe_values / jnp.expm1(safe_values))


def block_mul(left_block, right_block):
    return jnp.sum(left_block[:, :, None] * right_block[None, :, :], axis=1)


def invert_small(matrix):
    order_size = matrix.shape[0]
    left_rows = [[matrix[i, j] for j in range(order_size)] for i in range(order_size)]
    blank_entry = jnp.zeros_like(matrix[0, 0])
    right_rows = [[blank_entry + (1.0 if i == j else 0.0) for j in range(order_size)] for i in range(order_size)]
    for k in range(order_size):
        pivot_inv = 1.0 / left_rows[k][k]
        left_rows[k] = [v * pivot_inv for v in left_rows[k]]
        right_rows[k] = [v * pivot_inv for v in right_rows[k]]
        for i in range(order_size):
            if i != k:
                factor = left_rows[i][k]
                left_rows[i] = [a - factor * b for a, b in zip(left_rows[i], left_rows[k])]
                right_rows[i] = [a - factor * b for a, b in zip(right_rows[i], right_rows[k])]
    return jnp.stack([jnp.stack(r, 0) for r in right_rows], 0)


def block_thomas(lower, diagonal, upper, right_side):
    def forward(carried, row_blocks):
        coupled_prev, solved_prev = carried
        lower_row, diag_row, upper_row, side_row = row_blocks
        reduced = diag_row - block_mul(lower_row, coupled_prev)
        inverse = invert_small(reduced)
        coupled = block_mul(inverse, upper_row)
        solved = block_mul(inverse, side_row - block_mul(lower_row, solved_prev))
        return (coupled, solved), (coupled, solved)

    initial = (jnp.zeros_like(diagonal[0]), jnp.zeros_like(right_side[0]))
    ignored_end, (coupled_all, solved_all) = lax.scan(forward, initial, (lower, diagonal, upper, right_side))

    def backward(following, row_blocks):
        coupled, solved = row_blocks
        current = solved - block_mul(coupled, following)
        return current, current

    ignored_start, result = lax.scan(backward, jnp.zeros_like(right_side[0]), (coupled_all, solved_all), reverse=True)
    return result


def stack_blocks(entries, shape):
    stacked = jnp.stack([jnp.stack([jnp.broadcast_to(e, shape) for e in r], 0) for r in entries], 0)
    return jnp.moveaxis(stacked, 2, 0)


def assemble(center, neighbours, fixed_charge):
    potential, concentration, permittivity = center
    shape = potential.shape
    blank_entry = jnp.zeros_like(potential)
    charge = fixed_charge
    for k in range(3):
        charge = charge + VALENCE[k] * concentration[k]
    residual = [-charge, blank_entry, blank_entry, blank_entry]
    jacobian = [[blank_entry] * 4 for i in range(4)]
    lower = [[blank_entry] * 4 for i in range(4)]
    upper = [[blank_entry] * 4 for i in range(4)]
    for k in range(3):
        jacobian[0][k + 1] = blank_entry - VALENCE[k]
    for nearby, inside, weight, position in neighbours:
        near_potential, near_conc, near_perm = nearby
        harmonic = 2.0 * permittivity * near_perm / (permittivity + near_perm)
        face_perm = weight * (inside * harmonic + (1.0 - inside) * permittivity)
        residual[0] = residual[0] + face_perm * (potential - near_potential)
        jacobian[0][0] = jacobian[0][0] + face_perm
        offdiag = lower if position == "lower" else (upper if position == "upper" else None)
        if offdiag is not None:
            offdiag[0][0] = -inside * face_perm
        for k in range(3):
            drift = VALENCE[k] * (near_potential - potential)
            face_coef = inside * weight * MOBILITY[k]
            weight_out = bernoulli(drift)
            weight_in = bernoulli(-drift)
            mean_conc = 0.5 * (concentration[k] + near_conc[k])
            residual[k + 1] = residual[k + 1] + face_coef * (weight_out * concentration[k] - weight_in * near_conc[k])
            jacobian[k + 1][k + 1] = jacobian[k + 1][k + 1] + face_coef * weight_out
            jacobian[k + 1][0] = jacobian[k + 1][0] + face_coef * VALENCE[k] * mean_conc
            if offdiag is not None:
                offdiag[k + 1][k + 1] = -face_coef * weight_in
                offdiag[k + 1][0] = -face_coef * VALENCE[k] * mean_conc
    residual_all = jnp.moveaxis(jnp.stack([jnp.broadcast_to(e, shape) for e in residual], 0), 1, 0)
    return residual_all, stack_blocks(jacobian, shape), stack_blocks(lower, shape), stack_blocks(upper, shape)


def along_wall(array, wall_axis, from_below):
    length = array.shape[wall_axis]
    edge = jnp.zeros_like(lax.slice_in_dim(array, 0, 1, axis=wall_axis))
    if from_below:
        return jnp.concatenate([edge, lax.slice_in_dim(array, 0, length - 1, axis=wall_axis)], wall_axis)
    return jnp.concatenate([lax.slice_in_dim(array, 1, length, axis=wall_axis), edge], wall_axis)


def reference(potential, concentration, permittivity, fixed_charge):
    wall_rows = jnp.arange(NW, dtype=jnp.int32)
    inside_lower = (wall_rows > 0).astype(potential.dtype)[:, None]
    inside_upper = (wall_rows < NW - 1).astype(potential.dtype)[:, None]

    def one_plane(plane_index):
        def plane_fields(offset):
            where_plane = ((plane_index + offset) % NP).astype(jnp.int32)
            return (lax.dynamic_index_in_dim(potential, where_plane, 1, False),
                    lax.dynamic_index_in_dim(concentration, where_plane, 2, False),
                    lax.dynamic_index_in_dim(permittivity, where_plane, 1, False))

        center = plane_fields(0)
        below = tuple(along_wall(a, w, True) for a, w in zip(center, (0, 1, 0)))
        above = tuple(along_wall(a, w, False) for a, w in zip(center, (0, 1, 0)))
        behind = tuple(jnp.roll(a, 1, axis=-1) for a in center)
        ahead = tuple(jnp.roll(a, -1, axis=-1) for a in center)
        neighbours = [(below, inside_lower, 1.0, "lower"), (above, inside_upper, 1.0, "upper"),
                      (plane_fields(-1), 1.0, PLANE_WEIGHT, "plane"), (plane_fields(1), 1.0, PLANE_WEIGHT, "plane"),
                      (behind, 1.0, PLANE_WEIGHT, "plane"), (ahead, 1.0, PLANE_WEIGHT, "plane")]
        charge_here = lax.dynamic_index_in_dim(fixed_charge, plane_index.astype(jnp.int32), 1, False)
        residual, diagonal, lower, upper = assemble(center, neighbours, charge_here)
        solved = block_thomas(lower, diagonal, upper, -residual[:, :, None])
        return solved[:, :, 0]

    planes = lax.map(one_plane, jnp.arange(NP, dtype=jnp.int32))
    return jnp.transpose(planes, (2, 1, 0, 3))
```

```python
import functools

import jax
import jax.numpy as jnp
from jax import lax
from jax.experimental import pallas as pl
from jax.experimental.pallas import tpu as pltpu
from jax.sharding import PartitionSpec as P

VALENCE = (1.0, -1.0, 2.0)
MOBILITY = (1.0, 1.5, 0.7)
HALF_ZD = tuple(0.5 * z * d for z, d in zip(VALENCE, MOBILITY))
PLANE_WEIGHT = 0.01
LANES = 128
SUB = 8
NQ = 11

VMEM = pl.BlockSpec(memory_space=pltpu.VMEM)
SMEM = pl.BlockSpec(memory_space=pltpu.SMEM)


def sds(*shape):
    return jax.ShapeDtypeStruct(shape, jnp.float32)


def params(mib=8):
    return pltpu.CompilerParams(vmem_limit_bytes=mib * 1024 * 1024)


def face(phi, eps, conc, phi_m, eps_m, conc_m, weight):
    x = phi_m - phi
    y = 0.5 * x
    y = jnp.where(y == 0.0, 1e-20, y)
    t = jnp.tanh(y)
    h = y * pl.reciprocal(t, approx=True)
    e = (eps * eps_m) * pl.reciprocal(eps + eps_m, approx=True)
    if weight is None:
        e = e + e
        h2 = h + y * t
        xw, yw, hw = x, y, h
    else:
        e = e * (weight + weight)
        hw = h * weight
        yw = y * weight
        xw = yw + yw
        h2 = hw + yw * t
    p1 = hw - yw
    m1 = hw + yw
    out = (p1, 1.5 * m1, 0.7 * (h2 - xw))
    into = (m1, 1.5 * p1, 0.7 * (h2 + xw))
    g = e * x
    flux = tuple(out[k] * conc[k] - into[k] * conc_m[k] for k in range(3))
    return e, g, out, into, flux


def inv2(a, b, c, d):
    r = pl.reciprocal(a * d - b * c, approx=True)
    return d * r, b * r, c * r, a * r


def inverse4(D):
    a0, a1, a2, a3 = inv2(D[0][0], D[0][1], D[1][0], D[1][1])
    A = ((a0, -a1), (-a2, a3))
    E = [[D[2 + i][0] * A[0][j] + D[2 + i][1] * A[1][j] for j in range(2)] for i in range(2)]
    S = [
        [D[2 + i][2 + j] - (E[i][0] * D[0][2 + j] + E[i][1] * D[1][2 + j]) for j in range(2)]
        for i in range(2)
    ]
    s0, s1, s2, s3 = inv2(S[0][0], S[0][1], S[1][0], S[1][1])
    I = ((s0, -s1), (-s2, s3))
    F = [[A[i][0] * D[0][2 + j] + A[i][1] * D[1][2 + j] for j in range(2)] for i in range(2)]
    X = [[I[i][0] * E[0][j] + I[i][1] * E[1][j] for j in range(2)] for i in range(2)]
    Y = [[F[i][0] * I[0][j] + F[i][1] * I[1][j] for j in range(2)] for i in range(2)]
    Z = [[A[i][j] + (F[i][0] * X[0][j] + F[i][1] * X[1][j]) for j in range(2)] for i in range(2)]
    return [
        [Z[0][0], Z[0][1], -Y[0][0], -Y[0][1]],
        [Z[1][0], Z[1][1], -Y[1][0], -Y[1][1]],
        [-X[0][0], -X[0][1], I[0][0], I[0][1]],
        [-X[1][0], -X[1][1], I[1][0], I[1][1]],
    ]


def mat_vec(G, v):
    return [(G[i][0] * v[0] + G[i][1] * v[1]) + (G[i][2] * v[2] + G[i][3] * v[3]) for i in range(4)]


def couple(D, r, e, m, f, T, s):
    Dn = [[D[0][j] - e * T[0][j] for j in range(4)]]
    rn = [r[0] + e * s[0]]
    for k in range(3):
        Dn.append([D[k + 1][j] - (m[k] * T[0][j] + f[k] * T[k + 1][j]) for j in range(4)])
        rn.append(r[k + 1] + (m[k] * s[0] + f[k] * s[k + 1]))
    return Dn, rn


def solve_block(D, r, e, m, f):
    G = inverse4(D)
    first = mat_vec(G, [e] + list(m))
    T = [[first[i]] + [G[i][k + 1] * f[k] for k in range(3)] for i in range(4)]
    return T, mat_vec(G, r)


def pack_kernel(
    rows, planes, where_ref, phi_hbm, conc_hbm, eps_hbm, charge_hbm,
    phi_ref, conc_ref, eps_ref, charge_ref, near_ref, far_ref, cols_ref, sems,
):
    copies = [
        pltpu.make_async_copy(src, dst, sems.at[i])
        for i, (src, dst) in enumerate(
            (
                (conc_hbm, conc_ref),
                (phi_hbm, phi_ref),
                (eps_hbm, eps_ref),
                (charge_hbm, charge_ref),
            )
        )
    ]
    for copy in copies:
        copy.start()
    for copy in copies:
        copy.wait()
    odd = where_ref[1] > 0
    views = [phi_ref, conc_ref.at[0], conc_ref.at[1], conc_ref.at[2], eps_ref]
    even_lane = lax.broadcasted_iota(jnp.int32, (SUB, LANES), 1)
    for f, ref in enumerate(views):
        low = ref[pl.ds(0, rows, stride=planes), :]
        high = ref[pl.ds(planes - 1, rows, stride=planes), :]
        near_ref[f] = jnp.where(odd, low, high)
        far_ref[f] = jnp.where(odd, high, low)
    for f, ref in enumerate(views):
        packed = jnp.zeros((SUB, LANES), jnp.float32)
        for j in range(rows * planes // SUB):
            moved = pltpu.roll(ref[SUB * j : SUB * (j + 1), :], 2 * j + 1, 1)
            packed = jnp.where((even_lane // 2) == j, moved, packed)
        cols_ref[f] = packed


def assemble_kernel(
    rows, planes, where_ref, phi_ref, conc_ref, eps_ref, charge_ref,
    acc_ref, fe_ref, fu_ref, span_ref,
):
    wall = where_ref[0]
    first_wall = (wall == 0).astype(jnp.float32)
    last_wall = 1.0 - first_wall

    def cell(p, row0):
        at = pl.ds(row0 * planes + p, SUB, stride=planes)
        return phi_ref[at, :], eps_ref[at, :], [conc_ref[k, at, :] for k in range(3)]

    for row0 in range(0, rows, SUB):
        zero = jnp.zeros((SUB, LANES), jnp.float32)
        carry = [zero] * NQ
        phi, eps, conc = cell(0, row0)
        for p in range(planes):
            total = list(carry)
            if p + 1 < planes:
                phi_m, eps_m, conc_m = cell(p + 1, row0)
                e, g, out, into, flux = face(phi, eps, conc, phi_m, eps_m, conc_m, PLANE_WEIGHT)
                mine = [e, g, *out, *flux, *conc_m]
                total = [a + b for a, b in zip(total, mine)]
                carry = [e, -g, *into, *[-v for v in flux], *conc]
                phi, eps, conc = phi_m, eps_m, conc_m
            for q in range(NQ):
                span_ref[q, p * rows + row0 : p * rows + row0 + SUB, :] = total[q]

    lane = lax.broadcasted_iota(jnp.int32, (planes, LANES), 1)
    weight = jnp.where(lane < LANES - 1, PLANE_WEIGHT, 0.0).astype(jnp.float32)

    def load(r):
        at = pl.ds(pl.multiple_of(r * planes, planes), planes)
        return phi_ref[at, :], eps_ref[at, :], [conc_ref[k, at, :] for k in range(3)]

    def finish(r, phi, eps, conc, lower, upper):
        at = pl.ds(pl.multiple_of(r * planes, planes), planes)

        def fwd(v):
            return pltpu.roll(v, LANES - 1, 1)

        def back(v):
            return pltpu.roll(v, 1, 1)

        conc_m = [fwd(c) for c in conc]
        e, g, out, into, flux = face(phi, eps, conc, fwd(phi), fwd(eps), conc_m, weight)
        span = [span_ref[q, pl.ds(r, planes, stride=rows), :] for q in range(NQ)]
        total_e = (e + back(e)) + (lower[0] + upper[0]) + span[0]
        total_g = (g - back(g)) + (lower[1] + upper[1]) + span[1]
        charge = charge_ref[at, :] + conc[0] - conc[1] + 2.0 * conc[2]
        acc_ref[0, at, :] = total_e
        acc_ref[1, at, :] = total_g + charge
        for k in range(3):
            acc_ref[2 + k, at, :] = (out[k] + back(into[k])) + (lower[2][k] + upper[2][k]) + span[2 + k]
            acc_ref[5 + k, at, :] = -(
                (flux[k] - back(flux[k])) + (lower[3][k] + upper[3][k]) + span[5 + k]
            )
            near = conc_m[k] + back(conc[k]) + span[8 + k] + 4.0 * conc[k]
            acc_ref[8 + k, at, :] = (HALF_ZD[k] * PLANE_WEIGHT) * near + HALF_ZD[k] * (
                lower[4][k] + upper[4][k]
            )

    zero = jnp.zeros((planes, LANES), jnp.float32)
    zeros = [zero] * 3

    phi, eps, conc = load(0)
    e = first_wall * eps
    lower = (e, -e * phi, zeros, zeros, zeros)

    def step(r, carry):
        phi, eps, conc, lower = carry
        phi_m, eps_m, conc_m = load(r + 1)
        e, g, out, into, flux = face(phi, eps, conc, phi_m, eps_m, conc_m, None)
        at = pl.ds(pl.multiple_of(r * planes, planes), planes)
        fe_ref[at, :] = e
        for k in range(3):
            fu_ref[wall, k, at, :] = into[k]
            fu_ref[1 - wall, k, at, :] = out[k]
        both = [conc[k] + conc_m[k] for k in range(3)]
        upper = (e, g, out, flux, both)
        finish(r, phi, eps, conc, lower, upper)
        lower = (e, -g, list(into), [-v for v in flux], both)
        return phi_m, eps_m, conc_m, lower

    phi, eps, conc, lower = lax.fori_loop(0, rows - 1, step, (phi, eps, conc, lower))
    e = last_wall * eps
    upper = (e, -e * phi, zeros, zeros, zeros)
    finish(rows - 1, phi, eps, conc, lower, upper)


def halo_terms(own, near, wrapped):
    e, g, out, _, flux = face(own[0], own[4], own[1:4], near[0], near[4], near[1:4], PLANE_WEIGHT)
    c = [near[1 + k] if wrapped is None else near[1 + k] - wrapped[1 + k] for k in range(3)]
    return [e, g, *out, *[-v for v in flux], *[(HALF_ZD[k] * PLANE_WEIGHT) * c[k] for k in range(3)]]


def eliminate_kernel(
    rows, planes, where_ref, phi_ref, conc_ref, eps_ref, acc_ref, fe_ref, fu_ref,
    near_ref, far_ref, near_halo_ref, far_halo_ref, cols_ref, even_halo_ref, odd_halo_ref,
    t_ref, s_ref, tip_ref, side_ref, rim_ref,
):
    wall = where_ref[0]
    span_odd = where_ref[1]
    stream_odd = where_ref[2] > 0

    for own_ref, halo_ref, side in (
        (near_ref, near_halo_ref, 1 - span_odd),
        (far_ref, far_halo_ref, span_odd),
    ):
        own = [own_ref[f] for f in range(5)]
        near = [halo_ref[f] for f in range(5)]
        for q, v in enumerate(halo_terms(own, near, None)):
            rim_ref[q, side] = v

    odd = lax.broadcasted_iota(jnp.int32, (SUB, LANES), 1) % 2 == 1
    own, near, wrapped = [], [], []
    for f in range(5):
        mine, a, b = cols_ref[f], even_halo_ref[f], odd_halo_ref[f]
        right = jnp.where(stream_odd, b, a)
        left = jnp.where(stream_odd, a, b)
        own.append(mine)
        near.append(jnp.where(odd, pltpu.roll(left, 1, 1), pltpu.roll(right, LANES - 1, 1)))
        wrapped.append(jnp.where(odd, pltpu.roll(mine, 1, 1), pltpu.roll(mine, LANES - 1, 1)))
    for q, v in enumerate(halo_terms(own, near, wrapped)):
        side_ref[q] = v

    lane = lax.broadcasted_iota(jnp.int32, (planes, LANES), 1)
    edge = (lane == 0) | (lane == LANES - 1)
    plane = lax.broadcasted_iota(jnp.int32, (planes, LANES), 0)
    low_plane, high_plane = plane == 0, plane == planes - 1

    def place(i):
        return jnp.where(wall == 0, i, rows - 1 - i)

    def own_block(i):
        r = place(i)
        at = pl.ds(pl.multiple_of(r * planes, planes), planes)
        q_all = []
        for q in range(NQ):
            side = side_ref[q]
            parts = [
                pltpu.roll(side, LANES - 1 - 2 * ((planes // SUB) * r + part), 1)
                for part in range(planes // SUB)
            ]
            moved = jnp.where(edge, jnp.concatenate(parts, 0), 0.0)
            low = jnp.broadcast_to(rim_ref[q, 0, pl.ds(r, 1), :], (planes, LANES))
            high = jnp.broadcast_to(rim_ref[q, 1, pl.ds(r, 1), :], (planes, LANES))
            rim = jnp.where(low_plane, low, jnp.where(high_plane, high, 0.0))
            q_all.append(acc_ref[q, at, :] + (moved + rim))
        a, d, b = q_all[0], q_all[2:5], q_all[8:11]
        one = jnp.ones_like(a)
        zero = jnp.zeros_like(a)
        D = [
            [a, -one, one, -2.0 * one],
            [b[0], d[0], zero, zero],
            [b[1], zero, d[1], zero],
            [b[2], zero, zero, d[2]],
        ]
        return at, D, [q_all[1], *q_all[5:8]]

    def next_face(i):
        r = place(i)
        r_next = place(i + 1)
        at = pl.ds(pl.multiple_of(r * planes, planes), planes)
        at_next = pl.ds(pl.multiple_of(r_next * planes, planes), planes)
        at_face = pl.ds(pl.multiple_of(jnp.minimum(r, r_next) * planes, planes), planes)
        m = [HALF_ZD[k] * (conc_ref[k, at, :] + conc_ref[k, at_next, :]) for k in range(3)]
        up = [fu_ref[0, k, at_face, :] for k in range(3)]
        low = [fu_ref[1, k, at_face, :] for k in range(3)]
        return fe_ref[at_face, :], m, up, low

    def reduce_row(i, carry):
        at, D, r = own_block(i)
        if carry is not None:
            T, s, e, m, low = carry
            D, r = couple(D, r, e, m, low, T, s)
        return at, D, r

    def step(i, carry):
        at, D, r = reduce_row(i, carry)
        e, m, up, low = next_face(i)
        T, s = solve_block(D, r, e, m, up)
        for a in range(4):
            for b in range(4):
                t_ref[4 * a + b, at, :] = T[a][b]
            s_ref[a, at, :] = s[a]
        return T, s, e, m, low

    carry = step(0, None)
    carry = lax.fori_loop(1, rows - 1, step, carry)
    at, D, r = reduce_row(rows - 1, carry)
    for a in range(4):
        for b in range(4):
            tip_ref[4 * a + b] = D[a][b]
        tip_ref[16 + a] = r[a]
    tip_ref[20] = phi_ref[at, :]
    for k in range(3):
        tip_ref[21 + k] = conc_ref[k, at, :]
    tip_ref[24] = eps_ref[at, :]


def tip_block(ref):
    D = [[ref[4 * a + b] for b in range(4)] for a in range(4)]
    r = [ref[16 + a] for a in range(4)]
    return D, r, ref[20], [ref[21 + k] for k in range(3)], ref[24]


def with_face(D, r, e, g, m, out, flux):
    D = [list(row) for row in D]
    r = list(r)
    D[0][0] = D[0][0] + e
    r[0] = r[0] + g
    for k in range(3):
        D[k + 1][k + 1] = D[k + 1][k + 1] + out[k]
        D[k + 1][0] = D[k + 1][0] + m[k]
        r[k + 1] = r[k + 1] - flux[k]
    return D, r


def substitute_kernel(rows, planes, where_ref, own_ref, near_ref, t_ref, s_ref, out_ref):
    wall = where_ref[0]
    D, r, phi, conc, eps = tip_block(own_ref)
    Dm, rm, phi_m, conc_m, eps_m = tip_block(near_ref)
    e, g, out, into, flux = face(phi, eps, conc, phi_m, eps_m, conc_m, None)
    m = [HALF_ZD[k] * (conc[k] + conc_m[k]) for k in range(3)]
    Dm, rm = with_face(Dm, rm, e, -g, m, into, [-v for v in flux])
    T, s = solve_block(Dm, rm, e, m, out)
    D, r = with_face(D, r, e, g, m, out, flux)
    D, r = couple(D, r, e, m, into, T, s)
    x = mat_vec(inverse4(D), r)

    def put(i, x):
        row = jnp.where(wall == 0, i, rows - 1 - i)
        at = pl.ds(pl.multiple_of(row * planes, planes), planes)
        for a in range(4):
            out_ref[a, at, :] = x[a]

    put(rows - 1, x)

    def step(j, x):
        i = rows - 2 - j
        row = jnp.where(wall == 0, i, rows - 1 - i)
        at = pl.ds(pl.multiple_of(row * planes, planes), planes)
        T = [[t_ref[4 * a + b, at, :] for b in range(4)] for a in range(4)]
        x = [v + s_ref[a, at, :] for a, v in enumerate(mat_vec(T, x))]
        put(i, x)
        return x

    lax.fori_loop(0, rows - 1, step, x)


def swap_pairs(count, first):
    pairs = []
    for i in range(first, count + first, 2):
        a, b = i % count, (i + 1) % count
        pairs += [(a, b), (b, a)]
    return pairs


def on_device_pair(potential, concentration, permittivity, fixed_charge):
    rows, planes, cols = potential.shape
    cells = rows * planes
    phi = potential.reshape(cells, cols)
    conc = concentration.reshape(3, cells, cols)
    eps = permittivity.reshape(cells, cols)
    charge = fixed_charge.reshape(cells, cols)
    n_span, n_stream = lax.axis_size("span"), lax.axis_size("stream")
    where = jnp.stack(
        [lax.axis_index("wall"), lax.axis_index("span") % 2, lax.axis_index("stream") % 2]
    ).astype(jnp.int32)

    phi, conc, eps, charge, near, far, edge_cols = pl.pallas_call(
        functools.partial(pack_kernel, rows, planes),
        out_shape=(
            sds(cells, cols), sds(3, cells, cols), sds(cells, cols), sds(cells, cols),
            sds(5, rows, cols), sds(5, rows, cols), sds(5, SUB, LANES),
        ),
        in_specs=[SMEM] + [pl.BlockSpec(memory_space=pltpu.HBM)] * 4,
        out_specs=(VMEM,) * 7,
        scratch_shapes=[pltpu.SemaphoreType.DMA((4,))],
        compiler_params=params(),
    )(where, *(pltpu.with_memory_space_constraint(v, pltpu.HBM) for v in (phi, conc, eps, charge)))

    far_halo = lax.ppermute(far, "span", swap_pairs(n_span, 1))
    near_halo = lax.ppermute(near, "span", swap_pairs(n_span, 0))
    odd_halo = lax.ppermute(edge_cols, "stream", swap_pairs(n_stream, 1))
    even_halo = lax.ppermute(edge_cols, "stream", swap_pairs(n_stream, 0))

    acc, fe, fu = pl.pallas_call(
        functools.partial(assemble_kernel, rows, planes),
        out_shape=(sds(NQ, cells, cols), sds(cells, cols), sds(2, 3, cells, cols)),
        in_specs=[SMEM] + [VMEM] * 4,
        out_specs=(VMEM,) * 3,
        scratch_shapes=[pltpu.VMEM((NQ, cells, cols), jnp.float32)],
        compiler_params=params(),
        cost_estimate=pl.CostEstimate(flops=12_000_000, bytes_accessed=6_000_000, transcendentals=0),
    )(where, phi, conc, eps, charge)

    T, s, tip = pl.pallas_call(
        functools.partial(eliminate_kernel, rows, planes),
        out_shape=(
            sds(16, cells, cols), sds(4, cells, cols), sds(25, planes, cols)
        ),
        in_specs=[SMEM] + [VMEM] * 13,
        out_specs=(VMEM,) * 3,
        scratch_shapes=[
            pltpu.VMEM((NQ, SUB, LANES), jnp.float32),
            pltpu.VMEM((NQ, 2, rows, LANES), jnp.float32),
        ],
        compiler_params=params(),
    )(
        where, phi, conc, eps, acc, fe, fu, near, far, near_halo, far_halo, edge_cols,
        even_halo, odd_halo,
    )

    tip_m = lax.ppermute(tip, "wall", [(0, 1), (1, 0)])

    update = pl.pallas_call(
        functools.partial(substitute_kernel, rows, planes),
        out_shape=sds(4, cells, cols),
        in_specs=[SMEM] + [VMEM] * 4,
        out_specs=VMEM,
        compiler_params=params(),
    )(where, tip, tip_m, T, s)
    return update.reshape(4, rows, planes, cols)


def with_halo(block, sides, width, periodic):
    for axis, dim in sides:
        count = lax.axis_size(axis)
        forward = [(i, i + 1) for i in range(count - 1)]
        if periodic:
            forward.append((count - 1, 0))
        backward = [(target, source) for source, target in forward]
        low = lax.ppermute(
            lax.slice_in_dim(block, block.shape[dim] - width, None, axis=dim), axis, forward
        )
        high = lax.ppermute(lax.slice_in_dim(block, 0, width, axis=dim), axis, backward)
        block = jnp.concatenate([low, block, high], axis=dim)
    return block


def bernoulli(values):
    near_zero = jnp.abs(values) < 0.001
    safe_values = jnp.where(near_zero, 1.0, values)
    series = 1.0 - 0.5 * values + values * values / 12.0
    return jnp.where(near_zero, series, safe_values / jnp.expm1(safe_values))


def block_mul(left_block, right_block):
    return jnp.sum(left_block[:, :, None] * right_block[None, :, :], axis=1)


def invert_small(matrix):
    order_size = matrix.shape[0]
    left_rows = [[matrix[i, j] for j in range(order_size)] for i in range(order_size)]
    blank_entry = jnp.zeros_like(matrix[0, 0])
    right_rows = [
        [blank_entry + (1.0 if i == j else 0.0) for j in range(order_size)]
        for i in range(order_size)
    ]
    for k in range(order_size):
        pivot_inv = 1.0 / left_rows[k][k]
        left_rows[k] = [v * pivot_inv for v in left_rows[k]]
        right_rows[k] = [v * pivot_inv for v in right_rows[k]]
        for i in range(order_size):
            if i != k:
                factor = left_rows[i][k]
                left_rows[i] = [a - factor * b for a, b in zip(left_rows[i], left_rows[k])]
                right_rows[i] = [a - factor * b for a, b in zip(right_rows[i], right_rows[k])]
    return jnp.stack([jnp.stack(r, 0) for r in right_rows], 0)


def block_thomas(lower, diagonal, upper, right_side):

    def forward(carried, row_blocks):
        coupled_prev, solved_prev = carried
        lower_row, diag_row, upper_row, side_row = row_blocks
        reduced = diag_row - block_mul(lower_row, coupled_prev)
        inverse = invert_small(reduced)
        coupled = block_mul(inverse, upper_row)
        solved = block_mul(inverse, side_row - block_mul(lower_row, solved_prev))
        return ((coupled, solved), (coupled, solved))

    initial = (jnp.zeros_like(diagonal[0]), jnp.zeros_like(right_side[0]))
    ignored_end, (coupled_all, solved_all) = lax.scan(
        forward, initial, (lower, diagonal, upper, right_side)
    )

    def backward(following, row_blocks):
        coupled, solved = row_blocks
        current = solved - block_mul(coupled, following)
        return (current, current)

    ignored_start, result = lax.scan(
        backward, jnp.zeros_like(right_side[0]), (coupled_all, solved_all), reverse=True
    )
    return result


def stack_blocks(entries):
    stacked = jnp.stack([jnp.stack([e for e in r], 0) for r in entries], 0)
    return jnp.moveaxis(stacked, 2, 0)


def assemble(center, neighbours, fixed_charge):
    potential, concentration, permittivity = center
    blank_entry = jnp.zeros_like(potential)
    charge = fixed_charge
    for k in range(3):
        charge = charge + VALENCE[k] * concentration[k]
    residual = [-charge, blank_entry, blank_entry, blank_entry]
    jacobian = [[blank_entry] * 4 for i in range(4)]
    lower = [[blank_entry] * 4 for i in range(4)]
    upper = [[blank_entry] * 4 for i in range(4)]
    for k in range(3):
        jacobian[0][k + 1] = blank_entry - VALENCE[k]
    for nearby, inside, weight, position in neighbours:
        near_potential, near_conc, near_perm = nearby
        harmonic = 2.0 * permittivity * near_perm / (permittivity + near_perm)
        face_perm = weight * (inside * harmonic + (1.0 - inside) * permittivity)
        residual[0] = residual[0] + face_perm * (potential - near_potential)
        jacobian[0][0] = jacobian[0][0] + face_perm
        offdiag = lower if position == "lower" else upper if position == "upper" else None
        if offdiag is not None:
            offdiag[0][0] = -inside * face_perm
        for k in range(3):
            drift = VALENCE[k] * (near_potential - potential)
            face_coef = inside * weight * MOBILITY[k]
            weight_out = bernoulli(drift)
            weight_in = bernoulli(-drift)
            mean_conc = 0.5 * (concentration[k] + near_conc[k])
            residual[k + 1] = residual[k + 1] + face_coef * (
                weight_out * concentration[k] - weight_in * near_conc[k]
            )
            jacobian[k + 1][k + 1] = jacobian[k + 1][k + 1] + face_coef * weight_out
            jacobian[k + 1][0] = jacobian[k + 1][0] + face_coef * VALENCE[k] * mean_conc
            if offdiag is not None:
                offdiag[k + 1][k + 1] = -face_coef * weight_in
                offdiag[k + 1][0] = -face_coef * VALENCE[k] * mean_conc
    residual_all = jnp.moveaxis(jnp.stack([e for e in residual], 0), 1, 0)
    return (residual_all, stack_blocks(jacobian), stack_blocks(lower), stack_blocks(upper))


def split_fields(block):
    return (block[0], block[1:4], block[4])


def partition_forward(previous_vec, previous_map, first_tip, last_tip):
    identity = jnp.eye(4, dtype=first_tip.dtype).reshape((4, 4) + (1,) * (first_tip.ndim - 2))
    start_vec = first_tip[:, 0:1]
    start_left = first_tip[:, 1:5]
    start_right = first_tip[:, 5:9]
    end_vec = last_tip[:, 0:1]
    end_left = last_tip[:, 1:5]
    end_right = last_tip[:, 5:9]
    schur_block = identity - block_mul(start_left, previous_map)
    inverse = invert_small(schur_block)
    offset = block_mul(inverse, start_vec + block_mul(start_left, previous_vec))
    reach_map = block_mul(inverse, start_right)
    next_vec = end_vec + block_mul(end_left, previous_vec + block_mul(previous_map, offset))
    next_map = block_mul(end_left, block_mul(previous_map, reach_map)) + end_right
    return (next_vec, next_map, offset, reach_map)


def reduced_sweep(every_tip, zero_vec, zero_map):

    def sweep_forward(carried, tip_pair):
        previous_vec, previous_map = carried
        next_vec, next_map, offset, reach_map = partition_forward(
            previous_vec, previous_map, tip_pair[0], tip_pair[1]
        )
        return ((next_vec, next_map), (previous_vec, previous_map, offset, reach_map))

    ignored_e, (vec_all, map_all, offset_all, reach_all) = lax.scan(
        sweep_forward, (zero_vec, zero_map), every_tip
    )

    def sweep_backward(right_value, pieces):
        offset, reach_map = pieces
        return (offset + block_mul(reach_map, right_value), right_value)

    ignored_f, right_all = lax.scan(sweep_backward, zero_vec, (offset_all, reach_all), reverse=True)
    return (vec_all, map_all, offset_all, reach_all, right_all)


def on_device(potential, concentration, permittivity, fixed_charge):
    cells_wall = potential.shape[0]
    stacked = jnp.concatenate([potential[None], concentration, permittivity[None]], 0)
    walled = with_halo(stacked, (("wall", 1),), 1, False)
    planed = with_halo(stacked, (("stream", 3), ("span", 2)), 1, True)
    center = split_fields(stacked)
    wall_index = lax.axis_index("wall")
    global_row = wall_index * cells_wall + jnp.arange(cells_wall, dtype=jnp.int32)
    line_length = lax.axis_size("wall") * cells_wall
    inside_lower = (global_row > 0).astype(jnp.float32)[:, None, None]
    inside_upper = (global_row < line_length - 1).astype(jnp.float32)[:, None, None]
    neighbours = [
        (split_fields(walled[:, :-2]), inside_lower, 1.0, "lower"),
        (split_fields(walled[:, 2:]), inside_upper, 1.0, "upper"),
        (split_fields(planed[:, :, :-2, 1:-1]), 1.0, PLANE_WEIGHT, "plane"),
        (split_fields(planed[:, :, 2:, 1:-1]), 1.0, PLANE_WEIGHT, "plane"),
        (split_fields(planed[:, :, 1:-1, :-2]), 1.0, PLANE_WEIGHT, "plane"),
        (split_fields(planed[:, :, 1:-1, 2:]), 1.0, PLANE_WEIGHT, "plane"),
    ]
    residual, diagonal, lower, upper = assemble(center, neighbours, fixed_charge)
    row_ids = jnp.arange(cells_wall, dtype=jnp.int32)
    first_mask = (row_ids == 0).astype(jnp.float32)[:, None, None, None, None]
    last_mask = (row_ids == cells_wall - 1).astype(jnp.float32)[:, None, None, None, None]
    right_side = jnp.concatenate(
        [-residual[:, :, None], -lower * first_mask, -upper * last_mask], 2
    )
    solved = block_thomas(lower, diagonal, upper, right_side)
    first_tip = solved[0]
    last_tip = solved[-1]
    lines_shape = first_tip.shape[2:]
    zero_vec = jnp.zeros((4, 1) + lines_shape, jnp.float32)
    zero_map = jnp.zeros((4, 4) + lines_shape, jnp.float32)
    line_tips = jnp.stack([first_tip, last_tip], 0)[None]
    every_tip = lax.all_gather(line_tips, "wall", axis=0, tiled=True)
    vec_all, map_all, offset_all, reach_all, right_all = reduced_sweep(
        every_tip, zero_vec, zero_map
    )

    def choose_own(stacked_all):
        return lax.dynamic_index_in_dim(stacked_all, wall_index, 0, False)

    previous_vec = choose_own(vec_all)
    previous_map = choose_own(map_all)
    offset = choose_own(offset_all)
    reach_map = choose_own(reach_all)
    right_value = choose_own(right_all)
    local_first = offset + block_mul(reach_map, right_value)
    left_value = previous_vec + block_mul(previous_map, local_first)
    update = solved[:, :, 0]
    update = update + jnp.sum(solved[:, :, 1:5] * left_value[None, None, :, 0], axis=2)
    update = update + jnp.sum(solved[:, :, 5:9] * right_value[None, None, :, 0], axis=2)
    return jnp.moveaxis(update, 1, 0)


def on_any(potential, concentration, permittivity, fixed_charge):
    rows, planes, cols = potential.shape
    pair = (
        lax.axis_size("wall") == 2
        and lax.axis_size("span") % 2 == 0
        and lax.axis_size("stream") % 2 == 0
        and cols == LANES
        and rows % SUB == 0
        and planes % SUB == 0
        and rows * planes // SUB * 2 <= LANES
    )
    chosen = on_device_pair if pair else on_device
    return chosen(potential, concentration, permittivity, fixed_charge)


def solution(mesh):
    return jax.shard_map(
        on_any,
        mesh=mesh,
        in_specs=(
            P("wall", "span", "stream"),
            P(None, "wall", "span", "stream"),
            P("wall", "span", "stream"),
            P("wall", "span", "stream"),
        ),
        out_specs=P(None, "wall", "span", "stream"),
        check_vma=False,
    )
```

```python
import functools

import jax
import jax.numpy as jnp
from jax import lax
from jax.experimental import pallas as pl
from jax.experimental.pallas import tpu as pltpu
from jax.sharding import PartitionSpec as P

VALENCE = (1.0, -1.0, 2.0)
MOBILITY = (1.0, 1.5, 0.7)
HALF_ZD = tuple(0.5 * z * d for z, d in zip(VALENCE, MOBILITY))
PLANE_WEIGHT = 0.01
LANES = 128
SUB = 8
NQ = 11
ASSEMBLE_GROUP = 4
ELIMINATE_GROUP = 30
SUBSTITUTE_GROUP = 31
OUT_ROWS = 8

VMEM = pl.BlockSpec(memory_space=pltpu.VMEM)
SMEM = pl.BlockSpec(memory_space=pltpu.SMEM)


def sds(*shape):
    return jax.ShapeDtypeStruct(shape, jnp.float32)


def params(mib=8):
    return pltpu.CompilerParams(vmem_limit_bytes=mib * 1024 * 1024)


def unrolled(start, stop, step, carry, group):
    full = (stop - start) // group if stop - start > group else 0

    def body(j, carry):
        for u in range(group):
            carry = step(start + group * j + u, carry)
        return carry

    if full:
        carry = lax.fori_loop(0, full, body, carry)
    for i in range(start + group * full, stop):
        carry = step(i, carry)
    return carry


def face(phi, eps, conc, phi_m, eps_m, conc_m, weight):
    x = phi_m - phi
    y = 0.5 * x
    y = jnp.where(y == 0.0, 1e-20, y)
    t = jnp.tanh(y)
    h = y * pl.reciprocal(t, approx=True)
    e = (eps * eps_m) * pl.reciprocal(eps + eps_m, approx=True)
    if weight is None:
        e = e + e
        h2 = h + y * t
        xw, yw, hw = x, y, h
    else:
        e = e * (weight + weight)
        hw = h * weight
        yw = y * weight
        xw = yw + yw
        h2 = hw + yw * t
    p1 = hw - yw
    m1 = hw + yw
    out = (p1, 1.5 * m1, 0.7 * (h2 - xw))
    into = (m1, 1.5 * p1, 0.7 * (h2 + xw))
    g = e * x
    flux = tuple(out[k] * conc[k] - into[k] * conc_m[k] for k in range(3))
    return e, g, out, into, flux


def inv2(a, b, c, d):
    r = pl.reciprocal(a * d - b * c, approx=True)
    return d * r, b * r, c * r, a * r


def inverse4(D):
    a0, a1, a2, a3 = inv2(D[0][0], D[0][1], D[1][0], D[1][1])
    A = ((a0, -a1), (-a2, a3))
    E = [[D[2 + i][0] * A[0][j] + D[2 + i][1] * A[1][j] for j in range(2)] for i in range(2)]
    S = [
        [D[2 + i][2 + j] - (E[i][0] * D[0][2 + j] + E[i][1] * D[1][2 + j]) for j in range(2)]
        for i in range(2)
    ]
    s0, s1, s2, s3 = inv2(S[0][0], S[0][1], S[1][0], S[1][1])
    I = ((s0, -s1), (-s2, s3))
    F = [[A[i][0] * D[0][2 + j] + A[i][1] * D[1][2 + j] for j in range(2)] for i in range(2)]
    X = [[I[i][0] * E[0][j] + I[i][1] * E[1][j] for j in range(2)] for i in range(2)]
    Y = [[F[i][0] * I[0][j] + F[i][1] * I[1][j] for j in range(2)] for i in range(2)]
    Z = [[A[i][j] + (F[i][0] * X[0][j] + F[i][1] * X[1][j]) for j in range(2)] for i in range(2)]
    return [
        [Z[0][0], Z[0][1], -Y[0][0], -Y[0][1]],
        [Z[1][0], Z[1][1], -Y[1][0], -Y[1][1]],
        [-X[0][0], -X[0][1], I[0][0], I[0][1]],
        [-X[1][0], -X[1][1], I[1][0], I[1][1]],
    ]


def mat_vec(G, v):
    return [(G[i][0] * v[0] + G[i][1] * v[1]) + (G[i][2] * v[2] + G[i][3] * v[3]) for i in range(4)]


def couple(D, r, e, m, f, T, s):
    Dn = [[D[0][j] - e * T[0][j] for j in range(4)]]
    rn = [r[0] + e * s[0]]
    for k in range(3):
        Dn.append([D[k + 1][j] - (m[k] * T[0][j] + f[k] * T[k + 1][j]) for j in range(4)])
        rn.append(r[k + 1] + (m[k] * s[0] + f[k] * s[k + 1]))
    return Dn, rn


def solve_block(D, r, e, m, f):
    G = inverse4(D)
    first = mat_vec(G, [e] + list(m))
    T = [[first[i]] + [G[i][k + 1] * f[k] for k in range(3)] for i in range(4)]
    return T, mat_vec(G, r)


def pack_kernel(
    rows, planes, where_ref, phi_hbm, conc_hbm, eps_hbm, charge_hbm,
    phi_ref, conc_ref, eps_ref, charge_ref, near_ref, far_ref, cols_ref, sems,
):
    fields = [
        (phi_hbm, phi_ref),
        *((conc_hbm.at[k], conc_ref.at[k]) for k in range(3)),
        (eps_hbm, eps_ref),
        (charge_hbm, charge_ref),
    ]
    copies = [pltpu.make_async_copy(*pair, sems.at[i]) for i, pair in enumerate(fields)]
    for copy in copies:
        copy.start()
    odd = where_ref[1] > 0
    pair_of_lane = lax.broadcasted_iota(jnp.int32, (SUB, LANES), 1) // 2
    for f in range(5):
        copies[f].wait()
        ref = fields[f][1]
        low = ref[pl.ds(0, rows, stride=planes), :]
        high = ref[pl.ds(planes - 1, rows, stride=planes), :]
        near_ref[f] = jnp.where(odd, low, high)
        far_ref[f] = jnp.where(odd, high, low)
        packed = jnp.zeros((SUB, LANES), jnp.float32)
        for j in range(rows * planes // SUB):
            moved = pltpu.roll(ref[SUB * j : SUB * (j + 1), :], 2 * j + 1, 1)
            packed = jnp.where(pair_of_lane == j, moved, packed)
        cols_ref[f] = packed
    copies[5].wait()


def assemble_kernel(
    rows, planes, where_ref, phi_ref, conc_ref, eps_ref, charge_ref,
    acc_ref, fe_ref, fu_ref, span_ref,
):
    wall = where_ref[0]
    first_wall = (wall == 0).astype(jnp.float32)
    last_wall = 1.0 - first_wall

    def cell(p, row0):
        at = pl.ds(row0 * planes + p, SUB, stride=planes)
        return phi_ref[at, :], eps_ref[at, :], [conc_ref[k, at, :] for k in range(3)]

    for row0 in range(0, rows, SUB):
        zero = jnp.zeros((SUB, LANES), jnp.float32)
        carry = [zero] * NQ
        phi, eps, conc = cell(0, row0)
        for p in range(planes):
            total = list(carry)
            if p + 1 < planes:
                phi_m, eps_m, conc_m = cell(p + 1, row0)
                e, g, out, into, flux = face(phi, eps, conc, phi_m, eps_m, conc_m, PLANE_WEIGHT)
                mine = [e, g, *out, *flux, *conc_m]
                total = [a + b for a, b in zip(total, mine)]
                carry = [e, -g, *into, *[-v for v in flux], *conc]
                phi, eps, conc = phi_m, eps_m, conc_m
            for q in range(NQ):
                span_ref[q, p * (rows + 1) + row0 : p * (rows + 1) + row0 + SUB, :] = total[q]

    lane = lax.broadcasted_iota(jnp.int32, (planes, LANES), 1)
    weight = jnp.where(lane < LANES - 1, PLANE_WEIGHT, 0.0).astype(jnp.float32)

    def load(r):
        at = pl.ds(pl.multiple_of(r * planes, planes), planes)
        return phi_ref[at, :], eps_ref[at, :], [conc_ref[k, at, :] for k in range(3)]

    def finish(r, phi, eps, conc, lower, upper):
        at = pl.ds(pl.multiple_of(r * planes, planes), planes)

        def fwd(v):
            return pltpu.roll(v, LANES - 1, 1)

        def back(v):
            return pltpu.roll(v, 1, 1)

        conc_m = [fwd(c) for c in conc]
        e, g, out, into, flux = face(phi, eps, conc, fwd(phi), fwd(eps), conc_m, weight)
        span = [span_ref[q, pl.ds(r, planes, stride=rows + 1), :] for q in range(NQ)]
        total_e = (e + back(e)) + (lower[0] + upper[0]) + span[0]
        total_g = (g - back(g)) + (lower[1] + upper[1]) + span[1]
        charge = charge_ref[at, :] + conc[0] - conc[1] + 2.0 * conc[2]
        acc_ref[0, at, :] = total_e
        acc_ref[1, at, :] = total_g + charge
        for k in range(3):
            acc_ref[2 + k, at, :] = (out[k] + back(into[k])) + (lower[2][k] + upper[2][k]) + span[2 + k]
            acc_ref[5 + k, at, :] = -(
                (flux[k] - back(flux[k])) + (lower[3][k] + upper[3][k]) + span[5 + k]
            )
            near = conc_m[k] + back(conc[k]) + span[8 + k] + 4.0 * conc[k]
            acc_ref[8 + k, at, :] = (HALF_ZD[k] * PLANE_WEIGHT) * near + HALF_ZD[k] * (
                lower[4][k] + upper[4][k]
            )

    zero = jnp.zeros((planes, LANES), jnp.float32)
    zeros = [zero] * 3

    phi, eps, conc = load(0)
    e = first_wall * eps
    lower = (e, -e * phi, zeros, zeros, zeros)

    def step(r, carry):
        phi, eps, conc, lower = carry
        phi_m, eps_m, conc_m = load(r + 1)
        e, g, out, into, flux = face(phi, eps, conc, phi_m, eps_m, conc_m, None)
        at = pl.ds(pl.multiple_of(r * planes, planes), planes)
        fe_ref[at, :] = e
        for k in range(3):
            fu_ref[wall, k, at, :] = into[k]
            fu_ref[1 - wall, k, at, :] = out[k]
        both = [conc[k] + conc_m[k] for k in range(3)]
        upper = (e, g, out, flux, both)
        finish(r, phi, eps, conc, lower, upper)
        lower = (e, -g, list(into), [-v for v in flux], both)
        return phi_m, eps_m, conc_m, lower

    phi, eps, conc, lower = unrolled(0, rows - 1, step, (phi, eps, conc, lower), ASSEMBLE_GROUP)
    e = last_wall * eps
    upper = (e, -e * phi, zeros, zeros, zeros)
    finish(rows - 1, phi, eps, conc, lower, upper)


def halo_terms(own, near, wrapped):
    e, g, out, _, flux = face(own[0], own[4], own[1:4], near[0], near[4], near[1:4], PLANE_WEIGHT)
    c = [near[1 + k] if wrapped is None else near[1 + k] - wrapped[1 + k] for k in range(3)]
    return [e, g, *out, *[-v for v in flux], *[(HALF_ZD[k] * PLANE_WEIGHT) * c[k] for k in range(3)]]


def first_eliminate_kernel(
    rows, planes, where_ref, phi_ref, conc_ref, eps_ref, acc_ref, fe_ref, fu_ref,
    near_ref, far_ref, near_halo_ref, far_halo_ref, cols_ref, even_halo_ref, odd_halo_ref,
    t_ref, s_ref, tip_ref, side_ref, rim_ref,
):
    span_odd = where_ref[1]
    stream_odd = where_ref[2] > 0

    for own_ref, halo_ref, side in (
        (near_ref, near_halo_ref, 1 - span_odd),
        (far_ref, far_halo_ref, span_odd),
    ):
        own = [own_ref[f] for f in range(5)]
        near = [halo_ref[f] for f in range(5)]
        for q, v in enumerate(halo_terms(own, near, None)):
            rim_ref[q, side] = v

    odd = lax.broadcasted_iota(jnp.int32, (SUB, LANES), 1) % 2 == 1
    own, near, wrapped = [], [], []
    for f in range(5):
        mine, a, b = cols_ref[f], even_halo_ref[f], odd_halo_ref[f]
        right = jnp.where(stream_odd, b, a)
        left = jnp.where(stream_odd, a, b)
        own.append(mine)
        near.append(jnp.where(odd, pltpu.roll(left, 1, 1), pltpu.roll(right, LANES - 1, 1)))
        wrapped.append(jnp.where(odd, pltpu.roll(mine, 1, 1), pltpu.roll(mine, LANES - 1, 1)))
    for q, v in enumerate(halo_terms(own, near, wrapped)):
        side_ref[q] = v

    last = pl.multiple_of(jnp.where(where_ref[0] == 0, rows - 1, 0) * planes, planes)
    for part in range(planes // SUB):
        at = pl.ds(last + SUB * part, SUB)
        tip_ref[20 + 5 * part] = phi_ref[at, :]
        for k in range(3):
            tip_ref[21 + 5 * part + k] = conc_ref[k, at, :]
        tip_ref[24 + 5 * part] = eps_ref[at, :]

    eliminate_kernel(
        rows, planes, 0, where_ref, conc_ref, acc_ref, fe_ref, fu_ref, side_ref, rim_ref,
        t_ref, s_ref, tip_ref,
    )


def eliminate_kernel(
    rows, planes, part, where_ref, conc_ref, acc_ref, fe_ref, fu_ref, side_ref, rim_ref,
    t_ref, s_ref, tip_ref,
):
    wall = where_ref[0]
    lane = lax.broadcasted_iota(jnp.int32, (SUB, LANES), 1)
    edge = (lane == 0) | (lane == LANES - 1)
    plane = lax.broadcasted_iota(jnp.int32, (SUB, LANES), 0) + SUB * part
    rims = [side for side, p in enumerate((0, planes - 1)) if p // SUB == part]
    on_rim = {side: plane == (planes - 1) * side for side in rims}

    def place(i):
        return jnp.where(wall == 0, i, rows - 1 - i)

    def tile(r):
        return pl.ds(pl.multiple_of(r * planes + SUB * part, SUB), SUB)

    def own_block(i):
        r = place(i)
        at = tile(r)
        q_all = []
        for q in range(NQ):
            moved = pltpu.roll(side_ref[q], LANES - 1 - 2 * ((planes // SUB) * r + part), 1)
            total = acc_ref[q, at, :] + jnp.where(edge, moved, 0.0)
            for side in rims:
                rim = jnp.broadcast_to(rim_ref[q, side, pl.ds(r, 1), :], (SUB, LANES))
                total = total + jnp.where(on_rim[side], rim, 0.0)
            q_all.append(total)
        a, d, b = q_all[0], q_all[2:5], q_all[8:11]
        one = jnp.ones_like(a)
        zero = jnp.zeros_like(a)
        D = [
            [a, -one, one, -2.0 * one],
            [b[0], d[0], zero, zero],
            [b[1], zero, d[1], zero],
            [b[2], zero, zero, d[2]],
        ]
        return at, D, [q_all[1], *q_all[5:8]]

    def next_face(i):
        r = place(i)
        r_next = place(i + 1)
        at, at_next, at_face = tile(r), tile(r_next), tile(jnp.minimum(r, r_next))
        m = [HALF_ZD[k] * (conc_ref[k, at, :] + conc_ref[k, at_next, :]) for k in range(3)]
        up = [fu_ref[0, k, at_face, :] for k in range(3)]
        low = [fu_ref[1, k, at_face, :] for k in range(3)]
        return fe_ref[at_face, :], m, up, low

    def reduce_row(i, carry):
        at, D, r = own_block(i)
        if carry is not None:
            T, s, e, m, low = carry
            D, r = couple(D, r, e, m, low, T, s)
        return at, D, r

    def step(i, carry):
        at, D, r = reduce_row(i, carry)
        e, m, up, low = next_face(i)
        T, s = solve_block(D, r, e, m, up)
        keep = pl.ds(pl.multiple_of(place(i) * SUB, SUB), SUB)
        for a in range(4):
            for b in range(4):
                t_ref[4 * a + b, keep, :] = T[a][b]
            s_ref[a, keep, :] = s[a]
        return T, s, e, m, low

    carry = step(0, None)
    carry = unrolled(1, rows - 1, step, carry, ELIMINATE_GROUP)
    at, D, r = reduce_row(rows - 1, carry)
    for a in range(4):
        for b in range(4):
            tip_ref[4 * a + b] = D[a][b]
        tip_ref[16 + a] = r[a]


def tip_block(ref, fields_ref, part):
    D = [[ref[4 * a + b] for b in range(4)] for a in range(4)]
    r = [ref[16 + a] for a in range(4)]
    f = [fields_ref[20 + 5 * part + q] for q in range(5)]
    return D, r, f[0], f[1:4], f[4]


def with_face(D, r, e, g, m, out, flux):
    D = [list(row) for row in D]
    r = list(r)
    D[0][0] = D[0][0] + e
    r[0] = r[0] + g
    for k in range(3):
        D[k + 1][k + 1] = D[k + 1][k + 1] + out[k]
        D[k + 1][0] = D[k + 1][0] + m[k]
        r[k + 1] = r[k + 1] - flux[k]
    return D, r


def substitute_kernel(
    rows, part, where_ref, own_ref, near_ref, own_first_ref, near_first_ref, t_ref, s_ref, out_ref,
    after=None,
):
    wall = where_ref[0]
    D, r, phi, conc, eps = tip_block(own_ref, own_first_ref, part)
    Dm, rm, phi_m, conc_m, eps_m = tip_block(near_ref, near_first_ref, part)
    e, g, out, into, flux = face(phi, eps, conc, phi_m, eps_m, conc_m, None)
    m = [HALF_ZD[k] * (conc[k] + conc_m[k]) for k in range(3)]
    Dm, rm = with_face(Dm, rm, e, -g, m, into, [-v for v in flux])
    T, s = solve_block(Dm, rm, e, m, out)
    D, r = with_face(D, r, e, g, m, out, flux)
    D, r = couple(D, r, e, m, into, T, s)
    x = mat_vec(inverse4(D), r)

    def tile(i):
        return pl.ds(pl.multiple_of(jnp.where(wall == 0, i, rows - 1 - i) * SUB, SUB), SUB)

    def put(i, x):
        at = tile(i)
        for a in range(4):
            out_ref[a, at, :] = x[a]

    put(rows - 1, x)

    def step(j, x):
        i = rows - 2 - j
        at = tile(i)
        T = [[t_ref[4 * a + b, at, :] for b in range(4)] for a in range(4)]
        x = [v + s_ref[a, at, :] for a, v in enumerate(mat_vec(T, x))]
        put(i, x)
        if after is not None and i % OUT_ROWS == 0:
            after(i)
        return x

    unrolled(0, rows - 1, step, x, rows - 1 if after is not None else SUBSTITUTE_GROUP)


def last_substitute_kernel(
    rows, planes, where_ref, own_ref, near_ref, own_first_ref, near_first_ref, t_ref, s_ref, *refs
):
    *done_refs, out_hbm, mine_ref, sems = refs
    parts = planes // SUB
    wall = where_ref[0]

    def to_hbm(ref, part, chunk, n):
        at = pl.ds(chunk, n)
        return pltpu.make_async_copy(
            ref.at[:, at], out_hbm.at[:, at, pl.ds(SUB * part, SUB), :], sems.at[len(copies)]
        )

    copies = []
    for part, ref in enumerate(done_refs):
        copies.append(to_hbm(ref, part, 0, rows))
        copies[-1].start()
    mine = mine_ref.reshape(4, rows, SUB, LANES)

    def after(i):
        first = jnp.where(wall == 0, i, rows - OUT_ROWS - i)
        copies.append(to_hbm(mine, parts - 1, first, OUT_ROWS))
        copies[-1].start()

    substitute_kernel(
        rows, parts - 1, where_ref, own_ref, near_ref, own_first_ref, near_first_ref, t_ref, s_ref,
        mine_ref, after,
    )
    for copy in copies:
        copy.wait()


def swap_pairs(count, first):
    pairs = []
    for i in range(first, count + first, 2):
        a, b = i % count, (i + 1) % count
        pairs += [(a, b), (b, a)]
    return pairs


def on_device_pair(potential, concentration, permittivity, fixed_charge):
    rows, planes, cols = potential.shape
    cells = rows * planes
    phi = potential.reshape(cells, cols)
    conc = concentration.reshape(3, cells, cols)
    eps = permittivity.reshape(cells, cols)
    charge = fixed_charge.reshape(cells, cols)
    n_span, n_stream = lax.axis_size("span"), lax.axis_size("stream")
    where = jnp.stack(
        [lax.axis_index("wall"), lax.axis_index("span") % 2, lax.axis_index("stream") % 2]
    ).astype(jnp.int32)

    phi, conc, eps, charge, near, far, edge_cols = pl.pallas_call(
        functools.partial(pack_kernel, rows, planes),
        name="pack",
        out_shape=(
            sds(cells, cols), sds(3, cells, cols), sds(cells, cols), sds(cells, cols),
            sds(5, rows, cols), sds(5, rows, cols), sds(5, SUB, LANES),
        ),
        in_specs=[SMEM] + [pl.BlockSpec(memory_space=pltpu.HBM)] * 4,
        out_specs=(VMEM,) * 7,
        scratch_shapes=[pltpu.SemaphoreType.DMA((6,))],
        compiler_params=params(),
    )(where, *(pltpu.with_memory_space_constraint(v, pltpu.HBM) for v in (phi, conc, eps, charge)))

    far_halo = lax.ppermute(far, "span", swap_pairs(n_span, 1))
    near_halo = lax.ppermute(near, "span", swap_pairs(n_span, 0))
    odd_halo = lax.ppermute(edge_cols, "stream", swap_pairs(n_stream, 1))
    even_halo = lax.ppermute(edge_cols, "stream", swap_pairs(n_stream, 0))

    acc, fe, fu = pl.pallas_call(
        functools.partial(assemble_kernel, rows, planes),
        name="assemble",
        out_shape=(sds(NQ, cells, cols), sds(cells, cols), sds(2, 3, cells, cols)),
        in_specs=[SMEM] + [VMEM] * 4,
        out_specs=(VMEM,) * 3,
        scratch_shapes=[pltpu.VMEM((NQ, cells + planes, cols), jnp.float32)],
        compiler_params=params(),
        cost_estimate=pl.CostEstimate(flops=12_000_000, bytes_accessed=6_000_000, transcendentals=0),
    )(where, phi, conc, eps, charge)

    parts = planes // SUB
    across = [(0, 1), (1, 0)]
    kept = (sds(16, rows * SUB, cols), sds(4, rows * SUB, cols))
    terms = (sds(NQ, SUB, LANES), sds(NQ, 2, rows, LANES))
    T, s, tip, side, rim = pl.pallas_call(
        functools.partial(first_eliminate_kernel, rows, planes),
        name="eliminate",
        out_shape=(*kept, sds(20 + 5 * parts, SUB, cols), *terms),
        in_specs=[SMEM] + [VMEM] * 13,
        out_specs=(VMEM,) * 5,
        compiler_params=params(),
    )(
        where, phi, conc, eps, acc, fe, fu, near, far, near_halo, far_halo, edge_cols,
        even_halo, odd_halo,
    )
    solved = [(tip, lax.ppermute(tip, "wall", across), T, s)]
    for part in range(1, parts):
        T, s, tip = pl.pallas_call(
            functools.partial(eliminate_kernel, rows, planes, part),
            name="eliminate",
            out_shape=(*kept, sds(20, SUB, cols)),
            in_specs=[SMEM] + [VMEM] * 6,
            out_specs=(VMEM,) * 3,
            compiler_params=params(),
        )(where, conc, acc, fe, fu, side, rim)
        solved.append((tip, lax.ppermute(tip, "wall", across), T, s))

    fields = solved[0][:2]
    done = [
        pl.pallas_call(
            functools.partial(substitute_kernel, rows, part),
            name="substitute",
            out_shape=sds(4, rows * SUB, cols),
            in_specs=[SMEM] + [VMEM] * 6,
            out_specs=VMEM,
            compiler_params=params(),
        )(where, tip, tip_m, *fields, T, s)
        for part, (tip, tip_m, T, s) in enumerate(solved[:-1])
    ]
    tip, tip_m, T, s = solved[-1]
    return pl.pallas_call(
        functools.partial(last_substitute_kernel, rows, planes),
        name="substitute",
        out_shape=sds(4, rows, planes, cols),
        in_specs=[SMEM] + [VMEM] * (6 + len(done)),
        out_specs=pl.BlockSpec(memory_space=pltpu.HBM),
        scratch_shapes=[
            pltpu.VMEM((4, rows * SUB, cols), jnp.float32),
            pltpu.SemaphoreType.DMA((parts - 1 + rows // OUT_ROWS,)),
        ],
        compiler_params=params(),
    )(where, tip, tip_m, *fields, T, s, *(v.reshape(4, rows, SUB, cols) for v in done))


def with_halo(block, sides, width, periodic):
    for axis, dim in sides:
        count = lax.axis_size(axis)
        forward = [(i, i + 1) for i in range(count - 1)]
        if periodic:
            forward.append((count - 1, 0))
        backward = [(target, source) for source, target in forward]
        low = lax.ppermute(
            lax.slice_in_dim(block, block.shape[dim] - width, None, axis=dim), axis, forward
        )
        high = lax.ppermute(lax.slice_in_dim(block, 0, width, axis=dim), axis, backward)
        block = jnp.concatenate([low, block, high], axis=dim)
    return block


def bernoulli(values):
    near_zero = jnp.abs(values) < 0.001
    safe_values = jnp.where(near_zero, 1.0, values)
    series = 1.0 - 0.5 * values + values * values / 12.0
    return jnp.where(near_zero, series, safe_values / jnp.expm1(safe_values))


def block_mul(left_block, right_block):
    return jnp.sum(left_block[:, :, None] * right_block[None, :, :], axis=1)


def invert_small(matrix):
    order_size = matrix.shape[0]
    left_rows = [[matrix[i, j] for j in range(order_size)] for i in range(order_size)]
    blank_entry = jnp.zeros_like(matrix[0, 0])
    right_rows = [
        [blank_entry + (1.0 if i == j else 0.0) for j in range(order_size)]
        for i in range(order_size)
    ]
    for k in range(order_size):
        pivot_inv = 1.0 / left_rows[k][k]
        left_rows[k] = [v * pivot_inv for v in left_rows[k]]
        right_rows[k] = [v * pivot_inv for v in right_rows[k]]
        for i in range(order_size):
            if i != k:
                factor = left_rows[i][k]
                left_rows[i] = [a - factor * b for a, b in zip(left_rows[i], left_rows[k])]
                right_rows[i] = [a - factor * b for a, b in zip(right_rows[i], right_rows[k])]
    return jnp.stack([jnp.stack(r, 0) for r in right_rows], 0)


def block_thomas(lower, diagonal, upper, right_side):

    def forward(carried, row_blocks):
        coupled_prev, solved_prev = carried
        lower_row, diag_row, upper_row, side_row = row_blocks
        reduced = diag_row - block_mul(lower_row, coupled_prev)
        inverse = invert_small(reduced)
        coupled = block_mul(inverse, upper_row)
        solved = block_mul(inverse, side_row - block_mul(lower_row, solved_prev))
        return ((coupled, solved), (coupled, solved))

    initial = (jnp.zeros_like(diagonal[0]), jnp.zeros_like(right_side[0]))
    ignored_end, (coupled_all, solved_all) = lax.scan(
        forward, initial, (lower, diagonal, upper, right_side)
    )

    def backward(following, row_blocks):
        coupled, solved = row_blocks
        current = solved - block_mul(coupled, following)
        return (current, current)

    ignored_start, result = lax.scan(
        backward, jnp.zeros_like(right_side[0]), (coupled_all, solved_all), reverse=True
    )
    return result


def stack_blocks(entries):
    stacked = jnp.stack([jnp.stack([e for e in r], 0) for r in entries], 0)
    return jnp.moveaxis(stacked, 2, 0)


def assemble(center, neighbours, fixed_charge):
    potential, concentration, permittivity = center
    blank_entry = jnp.zeros_like(potential)
    charge = fixed_charge
    for k in range(3):
        charge = charge + VALENCE[k] * concentration[k]
    residual = [-charge, blank_entry, blank_entry, blank_entry]
    jacobian = [[blank_entry] * 4 for i in range(4)]
    lower = [[blank_entry] * 4 for i in range(4)]
    upper = [[blank_entry] * 4 for i in range(4)]
    for k in range(3):
        jacobian[0][k + 1] = blank_entry - VALENCE[k]
    for nearby, inside, weight, position in neighbours:
        near_potential, near_conc, near_perm = nearby
        harmonic = 2.0 * permittivity * near_perm / (permittivity + near_perm)
        face_perm = weight * (inside * harmonic + (1.0 - inside) * permittivity)
        residual[0] = residual[0] + face_perm * (potential - near_potential)
        jacobian[0][0] = jacobian[0][0] + face_perm
        offdiag = lower if position == "lower" else upper if position == "upper" else None
        if offdiag is not None:
            offdiag[0][0] = -inside * face_perm
        for k in range(3):
            drift = VALENCE[k] * (near_potential - potential)
            face_coef = inside * weight * MOBILITY[k]
            weight_out = bernoulli(drift)
            weight_in = bernoulli(-drift)
            mean_conc = 0.5 * (concentration[k] + near_conc[k])
            residual[k + 1] = residual[k + 1] + face_coef * (
                weight_out * concentration[k] - weight_in * near_conc[k]
            )
            jacobian[k + 1][k + 1] = jacobian[k + 1][k + 1] + face_coef * weight_out
            jacobian[k + 1][0] = jacobian[k + 1][0] + face_coef * VALENCE[k] * mean_conc
            if offdiag is not None:
                offdiag[k + 1][k + 1] = -face_coef * weight_in
                offdiag[k + 1][0] = -face_coef * VALENCE[k] * mean_conc
    residual_all = jnp.moveaxis(jnp.stack([e for e in residual], 0), 1, 0)
    return (residual_all, stack_blocks(jacobian), stack_blocks(lower), stack_blocks(upper))


def split_fields(block):
    return (block[0], block[1:4], block[4])


def partition_forward(previous_vec, previous_map, first_tip, last_tip):
    identity = jnp.eye(4, dtype=first_tip.dtype).reshape((4, 4) + (1,) * (first_tip.ndim - 2))
    start_vec = first_tip[:, 0:1]
    start_left = first_tip[:, 1:5]
    start_right = first_tip[:, 5:9]
    end_vec = last_tip[:, 0:1]
    end_left = last_tip[:, 1:5]
    end_right = last_tip[:, 5:9]
    schur_block = identity - block_mul(start_left, previous_map)
    inverse = invert_small(schur_block)
    offset = block_mul(inverse, start_vec + block_mul(start_left, previous_vec))
    reach_map = block_mul(inverse, start_right)
    next_vec = end_vec + block_mul(end_left, previous_vec + block_mul(previous_map, offset))
    next_map = block_mul(end_left, block_mul(previous_map, reach_map)) + end_right
    return (next_vec, next_map, offset, reach_map)


def reduced_sweep(every_tip, zero_vec, zero_map):

    def sweep_forward(carried, tip_pair):
        previous_vec, previous_map = carried
        next_vec, next_map, offset, reach_map = partition_forward(
            previous_vec, previous_map, tip_pair[0], tip_pair[1]
        )
        return ((next_vec, next_map), (previous_vec, previous_map, offset, reach_map))

    ignored_e, (vec_all, map_all, offset_all, reach_all) = lax.scan(
        sweep_forward, (zero_vec, zero_map), every_tip
    )

    def sweep_backward(right_value, pieces):
        offset, reach_map = pieces
        return (offset + block_mul(reach_map, right_value), right_value)

    ignored_f, right_all = lax.scan(sweep_backward, zero_vec, (offset_all, reach_all), reverse=True)
    return (vec_all, map_all, offset_all, reach_all, right_all)


def on_device(potential, concentration, permittivity, fixed_charge):
    cells_wall = potential.shape[0]
    stacked = jnp.concatenate([potential[None], concentration, permittivity[None]], 0)
    walled = with_halo(stacked, (("wall", 1),), 1, False)
    planed = with_halo(stacked, (("stream", 3), ("span", 2)), 1, True)
    center = split_fields(stacked)
    wall_index = lax.axis_index("wall")
    global_row = wall_index * cells_wall + jnp.arange(cells_wall, dtype=jnp.int32)
    line_length = lax.axis_size("wall") * cells_wall
    inside_lower = (global_row > 0).astype(jnp.float32)[:, None, None]
    inside_upper = (global_row < line_length - 1).astype(jnp.float32)[:, None, None]
    neighbours = [
        (split_fields(walled[:, :-2]), inside_lower, 1.0, "lower"),
        (split_fields(walled[:, 2:]), inside_upper, 1.0, "upper"),
        (split_fields(planed[:, :, :-2, 1:-1]), 1.0, PLANE_WEIGHT, "plane"),
        (split_fields(planed[:, :, 2:, 1:-1]), 1.0, PLANE_WEIGHT, "plane"),
        (split_fields(planed[:, :, 1:-1, :-2]), 1.0, PLANE_WEIGHT, "plane"),
        (split_fields(planed[:, :, 1:-1, 2:]), 1.0, PLANE_WEIGHT, "plane"),
    ]
    residual, diagonal, lower, upper = assemble(center, neighbours, fixed_charge)
    row_ids = jnp.arange(cells_wall, dtype=jnp.int32)
    first_mask = (row_ids == 0).astype(jnp.float32)[:, None, None, None, None]
    last_mask = (row_ids == cells_wall - 1).astype(jnp.float32)[:, None, None, None, None]
    right_side = jnp.concatenate(
        [-residual[:, :, None], -lower * first_mask, -upper * last_mask], 2
    )
    solved = block_thomas(lower, diagonal, upper, right_side)
    first_tip = solved[0]
    last_tip = solved[-1]
    lines_shape = first_tip.shape[2:]
    zero_vec = jnp.zeros((4, 1) + lines_shape, jnp.float32)
    zero_map = jnp.zeros((4, 4) + lines_shape, jnp.float32)
    line_tips = jnp.stack([first_tip, last_tip], 0)[None]
    every_tip = lax.all_gather(line_tips, "wall", axis=0, tiled=True)
    vec_all, map_all, offset_all, reach_all, right_all = reduced_sweep(
        every_tip, zero_vec, zero_map
    )

    def choose_own(stacked_all):
        return lax.dynamic_index_in_dim(stacked_all, wall_index, 0, False)

    previous_vec = choose_own(vec_all)
    previous_map = choose_own(map_all)
    offset = choose_own(offset_all)
    reach_map = choose_own(reach_all)
    right_value = choose_own(right_all)
    local_first = offset + block_mul(reach_map, right_value)
    left_value = previous_vec + block_mul(previous_map, local_first)
    update = solved[:, :, 0]
    update = update + jnp.sum(solved[:, :, 1:5] * left_value[None, None, :, 0], axis=2)
    update = update + jnp.sum(solved[:, :, 5:9] * right_value[None, None, :, 0], axis=2)
    return jnp.moveaxis(update, 1, 0)


def on_any(potential, concentration, permittivity, fixed_charge):
    rows, planes, cols = potential.shape
    pair = (
        lax.axis_size("wall") == 2
        and lax.axis_size("span") % 2 == 0
        and lax.axis_size("stream") % 2 == 0
        and cols == LANES
        and rows % SUB == 0
        and planes % SUB == 0
        and rows * planes // SUB * 2 <= LANES
    )
    chosen = on_device_pair if pair else on_device
    return chosen(potential, concentration, permittivity, fixed_charge)


def solution(mesh):
    return jax.shard_map(
        on_any,
        mesh=mesh,
        in_specs=(
            P("wall", "span", "stream"),
            P(None, "wall", "span", "stream"),
            P("wall", "span", "stream"),
            P("wall", "span", "stream"),
        ),
        out_specs=P(None, "wall", "span", "stream"),
        check_vma=False,
    )
```

```python
import functools

import jax
import jax.numpy as jnp
from jax import lax
from jax.experimental import pallas as pl
from jax.experimental.pallas import tpu as pltpu
from jax.sharding import PartitionSpec as P

VALENCE = (1.0, -1.0, 2.0)
MOBILITY = (1.0, 1.5, 0.7)
HALF_ZD = tuple(0.5 * z * d for z, d in zip(VALENCE, MOBILITY))
PLANE_WEIGHT = 0.01
LANES = 128
SUB = 8
NQ = 11
ASSEMBLE_GROUP = 8
ELIMINATE_GROUP = 30
SUBSTITUTE_GROUP = 31
OUT_ROWS = 8

VMEM = pl.BlockSpec(memory_space=pltpu.VMEM)
SMEM = pl.BlockSpec(memory_space=pltpu.SMEM)


def sds(*shape):
    return jax.ShapeDtypeStruct(shape, jnp.float32)


def params(mib=8):
    return pltpu.CompilerParams(vmem_limit_bytes=mib * 1024 * 1024)


def unrolled(start, stop, step, carry, group):
    full = (stop - start) // group if stop - start > group else 0

    def body(j, carry):
        for u in range(group):
            carry = step(start + group * j + u, carry)
        return carry

    if full:
        carry = lax.fori_loop(0, full, body, carry)
    for i in range(start + group * full, stop):
        carry = step(i, carry)
    return carry


def face(phi, eps, conc, phi_m, eps_m, conc_m, weight):
    x = phi_m - phi
    y = 0.5 * x
    y = jnp.where(y == 0.0, 1e-20, y)
    t = jnp.tanh(y)
    h = y * pl.reciprocal(t, approx=True)
    e = (eps * eps_m) * pl.reciprocal(eps + eps_m, approx=True)
    if weight is None:
        e = e + e
        h2 = h + y * t
        xw, yw, hw = x, y, h
    else:
        e = e * (weight + weight)
        hw = h * weight
        yw = y * weight
        xw = yw + yw
        h2 = hw + yw * t
    p1 = hw - yw
    m1 = hw + yw
    out = (p1, 1.5 * m1, 0.7 * (h2 - xw))
    into = (m1, 1.5 * p1, 0.7 * (h2 + xw))
    g = e * x
    flux = tuple(out[k] * conc[k] - into[k] * conc_m[k] for k in range(3))
    return e, g, out, into, flux


def inv2(a, b, c, d):
    r = pl.reciprocal(a * d - b * c, approx=True)
    return d * r, b * r, c * r, a * r


def inverse4(D):
    a0, a1, a2, a3 = inv2(D[0][0], D[0][1], D[1][0], D[1][1])
    A = ((a0, -a1), (-a2, a3))
    E = [[D[2 + i][0] * A[0][j] + D[2 + i][1] * A[1][j] for j in range(2)] for i in range(2)]
    S = [
        [D[2 + i][2 + j] - (E[i][0] * D[0][2 + j] + E[i][1] * D[1][2 + j]) for j in range(2)]
        for i in range(2)
    ]
    s0, s1, s2, s3 = inv2(S[0][0], S[0][1], S[1][0], S[1][1])
    I = ((s0, -s1), (-s2, s3))
    F = [[A[i][0] * D[0][2 + j] + A[i][1] * D[1][2 + j] for j in range(2)] for i in range(2)]
    X = [[I[i][0] * E[0][j] + I[i][1] * E[1][j] for j in range(2)] for i in range(2)]
    Y = [[F[i][0] * I[0][j] + F[i][1] * I[1][j] for j in range(2)] for i in range(2)]
    Z = [[A[i][j] + (F[i][0] * X[0][j] + F[i][1] * X[1][j]) for j in range(2)] for i in range(2)]
    return [
        [Z[0][0], Z[0][1], -Y[0][0], -Y[0][1]],
        [Z[1][0], Z[1][1], -Y[1][0], -Y[1][1]],
        [-X[0][0], -X[0][1], I[0][0], I[0][1]],
        [-X[1][0], -X[1][1], I[1][0], I[1][1]],
    ]


def mat_vec(G, v):
    return [(G[i][0] * v[0] + G[i][1] * v[1]) + (G[i][2] * v[2] + G[i][3] * v[3]) for i in range(4)]


def couple(D, r, e, m, f, T, s):
    Dn = [[D[0][j] - e * T[0][j] for j in range(4)]]
    rn = [r[0] + e * s[0]]
    for k in range(3):
        Dn.append([D[k + 1][j] - (m[k] * T[0][j] + f[k] * T[k + 1][j]) for j in range(4)])
        rn.append(r[k + 1] + (m[k] * s[0] + f[k] * s[k + 1]))
    return Dn, rn


def solve_block(D, r, e, m, f):
    G = inverse4(D)
    first = mat_vec(G, [e] + list(m))
    T = [[first[i]] + [G[i][k + 1] * f[k] for k in range(3)] for i in range(4)]
    return T, mat_vec(G, r)


def pack_kernel(
    rows, planes, where_ref, phi_hbm, conc_hbm, eps_hbm, charge_hbm,
    phi_ref, conc_ref, eps_ref, charge_ref, near_ref, far_ref, cols_ref, sems,
):
    fields = [
        (phi_hbm, phi_ref),
        *((conc_hbm.at[k], conc_ref.at[k]) for k in range(3)),
        (eps_hbm, eps_ref),
        (charge_hbm, charge_ref),
    ]
    copies = [pltpu.make_async_copy(*pair, sems.at[i]) for i, pair in enumerate(fields)]
    for copy in copies:
        copy.start()
    odd = where_ref[1] > 0
    pair_of_lane = lax.broadcasted_iota(jnp.int32, (SUB, LANES), 1) // 2
    for f in range(5):
        copies[f].wait()
        ref = fields[f][1]
        low = ref[pl.ds(0, rows, stride=planes), :]
        high = ref[pl.ds(planes - 1, rows, stride=planes), :]
        near_ref[f] = jnp.where(odd, high, low)
        far_ref[f] = jnp.where(odd, low, high)
        packed = jnp.zeros((SUB, LANES), jnp.float32)
        for j in range(rows * planes // SUB):
            moved = pltpu.roll(ref[SUB * j : SUB * (j + 1), :], 2 * j + 1, 1)
            packed = jnp.where(pair_of_lane == j, moved, packed)
        cols_ref[f] = packed
    copies[5].wait()


def assemble_kernel(
    rows, planes, where_ref, phi_ref, conc_ref, eps_ref, charge_ref,
    acc_ref, fe_ref, fu_ref, span_ref,
):
    wall = where_ref[0]
    first_wall = (wall == 0).astype(jnp.float32)
    last_wall = 1.0 - first_wall

    def cell(p, row0):
        at = pl.ds(row0 * planes + p, SUB, stride=planes)
        return phi_ref[at, :], eps_ref[at, :], [conc_ref[k, at, :] for k in range(3)]

    for row0 in range(0, rows, SUB):
        zero = jnp.zeros((SUB, LANES), jnp.float32)
        carry = [zero] * NQ
        phi, eps, conc = cell(0, row0)
        for p in range(planes):
            total = list(carry)
            if p + 1 < planes:
                phi_m, eps_m, conc_m = cell(p + 1, row0)
                e, g, out, into, flux = face(phi, eps, conc, phi_m, eps_m, conc_m, PLANE_WEIGHT)
                mine = [e, g, *out, *flux, *conc_m]
                total = [a + b for a, b in zip(total, mine)]
                carry = [e, -g, *into, *[-v for v in flux], *conc]
                phi, eps, conc = phi_m, eps_m, conc_m
            for q in range(NQ):
                span_ref[q, p * (rows + 1) + row0 : p * (rows + 1) + row0 + SUB, :] = total[q]

    def row_pass(part):
        lane = lax.broadcasted_iota(jnp.int32, (SUB, LANES), 1)
        weight = jnp.where(lane < LANES - 1, PLANE_WEIGHT, 0.0).astype(jnp.float32)

        def tile(r):
            return pl.ds(pl.multiple_of(r * planes + SUB * part, SUB), SUB)

        def load(r):
            at = tile(r)
            return phi_ref[at, :], eps_ref[at, :], [conc_ref[k, at, :] for k in range(3)]

        def finish(r, phi, eps, conc, lower, upper):
            at = tile(r)

            def fwd(v):
                return pltpu.roll(v, LANES - 1, 1)

            def back(v):
                return pltpu.roll(v, 1, 1)

            conc_m = [fwd(c) for c in conc]
            e, g, out, into, flux = face(phi, eps, conc, fwd(phi), fwd(eps), conc_m, weight)
            span = [span_ref[q, pl.ds(r + (rows + 1) * SUB * part, SUB, stride=rows + 1), :] for q in range(NQ)]
            total_e = (e + back(e)) + (lower[0] + upper[0]) + span[0]
            total_g = (g - back(g)) + (lower[1] + upper[1]) + span[1]
            charge = charge_ref[at, :] + conc[0] - conc[1] + 2.0 * conc[2]
            acc_ref[0, at, :] = total_e
            acc_ref[1, at, :] = total_g + charge
            for k in range(3):
                acc_ref[2 + k, at, :] = (out[k] + back(into[k])) + (lower[2][k] + upper[2][k]) + span[2 + k]
                acc_ref[5 + k, at, :] = -(
                    (flux[k] - back(flux[k])) + (lower[3][k] + upper[3][k]) + span[5 + k]
                )
                near = conc_m[k] + back(conc[k]) + span[8 + k] + 4.0 * conc[k]
                acc_ref[8 + k, at, :] = (HALF_ZD[k] * PLANE_WEIGHT) * near + HALF_ZD[k] * (
                    lower[4][k] + upper[4][k]
                )

        zero = jnp.zeros((SUB, LANES), jnp.float32)
        zeros = [zero] * 3

        phi, eps, conc = load(0)
        e = first_wall * eps
        lower = (e, -e * phi, zeros, zeros, zeros)

        def step(r, carry):
            phi, eps, conc, lower = carry
            phi_m, eps_m, conc_m = load(r + 1)
            e, g, out, into, flux = face(phi, eps, conc, phi_m, eps_m, conc_m, None)
            at = tile(r)
            fe_ref[at, :] = e
            for k in range(3):
                fu_ref[wall, k, at, :] = into[k]
                fu_ref[1 - wall, k, at, :] = out[k]
            both = [conc[k] + conc_m[k] for k in range(3)]
            upper = (e, g, out, flux, both)
            finish(r, phi, eps, conc, lower, upper)
            lower = (e, -g, list(into), [-v for v in flux], both)
            return phi_m, eps_m, conc_m, lower

        phi, eps, conc, lower = unrolled(0, rows - 1, step, (phi, eps, conc, lower), ASSEMBLE_GROUP)
        e = last_wall * eps
        upper = (e, -e * phi, zeros, zeros, zeros)
        finish(rows - 1, phi, eps, conc, lower, upper)

    for part in range(planes // SUB):
        row_pass(part)


def halo_terms(own, near, wrapped):
    e, g, out, _, flux = face(own[0], own[4], own[1:4], near[0], near[4], near[1:4], PLANE_WEIGHT)
    c = [near[1 + k] if wrapped is None else near[1 + k] - wrapped[1 + k] for k in range(3)]
    return [e, g, *out, *[-v for v in flux], *[(HALF_ZD[k] * PLANE_WEIGHT) * c[k] for k in range(3)]]


def first_eliminate_kernel(
    rows, planes, where_ref, phi_ref, conc_ref, eps_ref, acc_ref, fe_ref, fu_ref,
    near_ref, far_ref, near_halo_ref, far_halo_ref, cols_ref, even_halo_ref, odd_halo_ref,
    t_ref, s_ref, tip_ref, side_ref, rim_ref,
):
    span_odd = where_ref[1]
    stream_odd = where_ref[2] > 0

    for own_ref, halo_ref, side in (
        (near_ref, near_halo_ref, span_odd),
        (far_ref, far_halo_ref, 1 - span_odd),
    ):
        own = [own_ref[f] for f in range(5)]
        near = [halo_ref[f] for f in range(5)]
        for q, v in enumerate(halo_terms(own, near, None)):
            rim_ref[q, side] = v

    odd = lax.broadcasted_iota(jnp.int32, (SUB, LANES), 1) % 2 == 1
    own, near, wrapped = [], [], []
    for f in range(5):
        mine, a, b = cols_ref[f], even_halo_ref[f], odd_halo_ref[f]
        right = jnp.where(stream_odd, b, a)
        left = jnp.where(stream_odd, a, b)
        own.append(mine)
        near.append(jnp.where(odd, pltpu.roll(left, 1, 1), pltpu.roll(right, LANES - 1, 1)))
        wrapped.append(jnp.where(odd, pltpu.roll(mine, 1, 1), pltpu.roll(mine, LANES - 1, 1)))
    for q, v in enumerate(halo_terms(own, near, wrapped)):
        side_ref[q] = v

    last = pl.multiple_of(jnp.where(where_ref[0] == 0, rows - 1, 0) * planes, planes)
    for part in range(planes // SUB):
        at = pl.ds(last + SUB * part, SUB)
        tip_ref[20 + 5 * part] = phi_ref[at, :]
        for k in range(3):
            tip_ref[21 + 5 * part + k] = conc_ref[k, at, :]
        tip_ref[24 + 5 * part] = eps_ref[at, :]

    eliminate_kernel(
        rows, planes, 0, where_ref, conc_ref, acc_ref, fe_ref, fu_ref, side_ref, rim_ref,
        t_ref, s_ref, tip_ref,
    )


def eliminate_kernel(
    rows, planes, part, where_ref, conc_ref, acc_ref, fe_ref, fu_ref, side_ref, rim_ref,
    t_ref, s_ref, tip_ref,
):
    wall = where_ref[0]
    lane = lax.broadcasted_iota(jnp.int32, (SUB, LANES), 1)
    edge = (lane == 0) | (lane == LANES - 1)
    plane = lax.broadcasted_iota(jnp.int32, (SUB, LANES), 0) + SUB * part
    rims = [side for side, p in enumerate((0, planes - 1)) if p // SUB == part]
    on_rim = {side: plane == (planes - 1) * side for side in rims}

    def place(i):
        return jnp.where(wall == 0, i, rows - 1 - i)

    def tile(r):
        return pl.ds(pl.multiple_of(r * planes + SUB * part, SUB), SUB)

    def own_block(i):
        r = place(i)
        at = tile(r)
        q_all = []
        for q in range(NQ):
            moved = pltpu.roll(side_ref[q], LANES - 1 - 2 * ((planes // SUB) * r + part), 1)
            total = acc_ref[q, at, :] + jnp.where(edge, moved, 0.0)
            for side in rims:
                rim = jnp.broadcast_to(rim_ref[q, side, pl.ds(r, 1), :], (SUB, LANES))
                total = total + jnp.where(on_rim[side], rim, 0.0)
            q_all.append(total)
        a, d, b = q_all[0], q_all[2:5], q_all[8:11]
        one = jnp.ones_like(a)
        zero = jnp.zeros_like(a)
        D = [
            [a, -one, one, -2.0 * one],
            [b[0], d[0], zero, zero],
            [b[1], zero, d[1], zero],
            [b[2], zero, zero, d[2]],
        ]
        return at, D, [q_all[1], *q_all[5:8]]

    def next_face(i):
        r = place(i)
        r_next = place(i + 1)
        at, at_next, at_face = tile(r), tile(r_next), tile(jnp.minimum(r, r_next))
        m = [HALF_ZD[k] * (conc_ref[k, at, :] + conc_ref[k, at_next, :]) for k in range(3)]
        up = [fu_ref[0, k, at_face, :] for k in range(3)]
        low = [fu_ref[1, k, at_face, :] for k in range(3)]
        return fe_ref[at_face, :], m, up, low

    def reduce_row(i, carry):
        at, D, r = own_block(i)
        if carry is not None:
            T, s, e, m, low = carry
            D, r = couple(D, r, e, m, low, T, s)
        return at, D, r

    def step(i, carry):
        at, D, r = reduce_row(i, carry)
        e, m, up, low = next_face(i)
        T, s = solve_block(D, r, e, m, up)
        keep = pl.ds(pl.multiple_of(place(i) * SUB, SUB), SUB)
        for a in range(4):
            for b in range(4):
                t_ref[4 * a + b, keep, :] = T[a][b]
            s_ref[a, keep, :] = s[a]
        return T, s, e, m, low

    carry = step(0, None)
    carry = unrolled(1, rows - 1, step, carry, ELIMINATE_GROUP)
    at, D, r = reduce_row(rows - 1, carry)
    for a in range(4):
        for b in range(4):
            tip_ref[4 * a + b] = D[a][b]
        tip_ref[16 + a] = r[a]


def tip_block(ref, fields_ref, part):
    D = [[ref[4 * a + b] for b in range(4)] for a in range(4)]
    r = [ref[16 + a] for a in range(4)]
    f = [fields_ref[20 + 5 * part + q] for q in range(5)]
    return D, r, f[0], f[1:4], f[4]


def with_face(D, r, e, g, m, out, flux):
    D = [list(row) for row in D]
    r = list(r)
    D[0][0] = D[0][0] + e
    r[0] = r[0] + g
    for k in range(3):
        D[k + 1][k + 1] = D[k + 1][k + 1] + out[k]
        D[k + 1][0] = D[k + 1][0] + m[k]
        r[k + 1] = r[k + 1] - flux[k]
    return D, r


def substitute_kernel(
    rows, part, where_ref, own_ref, near_ref, own_first_ref, near_first_ref, t_ref, s_ref, out_ref,
    after=None,
):
    wall = where_ref[0]
    D, r, phi, conc, eps = tip_block(own_ref, own_first_ref, part)
    Dm, rm, phi_m, conc_m, eps_m = tip_block(near_ref, near_first_ref, part)
    e, g, out, into, flux = face(phi, eps, conc, phi_m, eps_m, conc_m, None)
    m = [HALF_ZD[k] * (conc[k] + conc_m[k]) for k in range(3)]
    Dm, rm = with_face(Dm, rm, e, -g, m, into, [-v for v in flux])
    T, s = solve_block(Dm, rm, e, m, out)
    D, r = with_face(D, r, e, g, m, out, flux)
    D, r = couple(D, r, e, m, into, T, s)
    x = mat_vec(inverse4(D), r)

    def tile(i):
        return pl.ds(pl.multiple_of(jnp.where(wall == 0, i, rows - 1 - i) * SUB, SUB), SUB)

    def put(i, x):
        at = tile(i)
        for a in range(4):
            out_ref[a, at, :] = x[a]

    put(rows - 1, x)

    def step(j, x):
        i = rows - 2 - j
        at = tile(i)
        T = [[t_ref[4 * a + b, at, :] for b in range(4)] for a in range(4)]
        x = [v + s_ref[a, at, :] for a, v in enumerate(mat_vec(T, x))]
        put(i, x)
        if after is not None and i % OUT_ROWS == 0:
            after(i)
        return x

    unrolled(0, rows - 1, step, x, rows - 1 if after is not None else SUBSTITUTE_GROUP)


def last_substitute_kernel(
    rows, planes, where_ref, own_ref, near_ref, own_first_ref, near_first_ref, t_ref, s_ref, *refs
):
    *done_refs, out_hbm, mine_ref, sems = refs
    parts = planes // SUB
    wall = where_ref[0]

    def to_hbm(ref, part, chunk, n):
        at = pl.ds(chunk, n)
        return pltpu.make_async_copy(
            ref.at[:, at], out_hbm.at[:, at, pl.ds(SUB * part, SUB), :], sems.at[len(copies)]
        )

    copies = []
    for part, ref in enumerate(done_refs):
        copies.append(to_hbm(ref, part, 0, rows))
        copies[-1].start()
    mine = mine_ref.reshape(4, rows, SUB, LANES)

    def after(i):
        first = jnp.where(wall == 0, i, rows - OUT_ROWS - i)
        copies.append(to_hbm(mine, parts - 1, first, OUT_ROWS))
        copies[-1].start()

    substitute_kernel(
        rows, parts - 1, where_ref, own_ref, near_ref, own_first_ref, near_first_ref, t_ref, s_ref,
        mine_ref, after,
    )
    for copy in copies:
        copy.wait()


def swap_pairs(count, first):
    pairs = []
    for i in range(first, count + first, 2):
        a, b = i % count, (i + 1) % count
        pairs += [(a, b), (b, a)]
    return pairs


def on_device_pair(potential, concentration, permittivity, fixed_charge):
    rows, planes, cols = potential.shape
    cells = rows * planes
    phi = potential.reshape(cells, cols)
    conc = concentration.reshape(3, cells, cols)
    eps = permittivity.reshape(cells, cols)
    charge = fixed_charge.reshape(cells, cols)
    n_span, n_stream = lax.axis_size("span"), lax.axis_size("stream")
    where = jnp.stack(
        [lax.axis_index("wall"), lax.axis_index("span") % 2, lax.axis_index("stream") % 2]
    ).astype(jnp.int32)

    phi, conc, eps, charge, near, far, edge_cols = pl.pallas_call(
        functools.partial(pack_kernel, rows, planes),
        name="pack",
        out_shape=(
            sds(cells, cols), sds(3, cells, cols), sds(cells, cols), sds(cells, cols),
            sds(5, rows, cols), sds(5, rows, cols), sds(5, SUB, LANES),
        ),
        in_specs=[SMEM] + [pl.BlockSpec(memory_space=pltpu.HBM)] * 4,
        out_specs=(VMEM,) * 7,
        scratch_shapes=[pltpu.SemaphoreType.DMA((6,))],
        compiler_params=params(),
    )(where, *(pltpu.with_memory_space_constraint(v, pltpu.HBM) for v in (phi, conc, eps, charge)))

    near_halo = lax.ppermute(near, "span", swap_pairs(n_span, 1))
    far_halo = lax.ppermute(far, "span", swap_pairs(n_span, 0))
    odd_halo = lax.ppermute(edge_cols, "stream", swap_pairs(n_stream, 1))
    even_halo = lax.ppermute(edge_cols, "stream", swap_pairs(n_stream, 0))

    acc, fe, fu = pl.pallas_call(
        functools.partial(assemble_kernel, rows, planes),
        name="assemble",
        out_shape=(sds(NQ, cells, cols), sds(cells, cols), sds(2, 3, cells, cols)),
        in_specs=[SMEM] + [VMEM] * 4,
        out_specs=(VMEM,) * 3,
        scratch_shapes=[pltpu.VMEM((NQ, cells + planes, cols), jnp.float32)],
        compiler_params=params(),
        cost_estimate=pl.CostEstimate(flops=12_000_000, bytes_accessed=6_000_000, transcendentals=0),
    )(where, phi, conc, eps, charge)

    parts = planes // SUB
    across = [(0, 1), (1, 0)]
    kept = (sds(16, rows * SUB, cols), sds(4, rows * SUB, cols))
    terms = (sds(NQ, SUB, LANES), sds(NQ, 2, rows, LANES))
    T, s, tip, side, rim = pl.pallas_call(
        functools.partial(first_eliminate_kernel, rows, planes),
        name="eliminate",
        out_shape=(*kept, sds(20 + 5 * parts, SUB, cols), *terms),
        in_specs=[SMEM] + [VMEM] * 13,
        out_specs=(VMEM,) * 5,
        compiler_params=params(),
    )(
        where, phi, conc, eps, acc, fe, fu, near, far, near_halo, far_halo, edge_cols,
        even_halo, odd_halo,
    )
    solved = [(tip, lax.ppermute(tip, "wall", across), T, s)]
    for part in range(1, parts):
        T, s, tip = pl.pallas_call(
            functools.partial(eliminate_kernel, rows, planes, part),
            name="eliminate",
            out_shape=(*kept, sds(20, SUB, cols)),
            in_specs=[SMEM] + [VMEM] * 6,
            out_specs=(VMEM,) * 3,
            compiler_params=params(),
        )(where, conc, acc, fe, fu, side, rim)
        solved.append((tip, lax.ppermute(tip, "wall", across), T, s))

    fields = solved[0][:2]
    done = [
        pl.pallas_call(
            functools.partial(substitute_kernel, rows, part),
            name="substitute",
            out_shape=sds(4, rows * SUB, cols),
            in_specs=[SMEM] + [VMEM] * 6,
            out_specs=VMEM,
            compiler_params=params(),
        )(where, tip, tip_m, *fields, T, s)
        for part, (tip, tip_m, T, s) in enumerate(solved[:-1])
    ]
    tip, tip_m, T, s = solved[-1]
    return pl.pallas_call(
        functools.partial(last_substitute_kernel, rows, planes),
        name="substitute",
        out_shape=sds(4, rows, planes, cols),
        in_specs=[SMEM] + [VMEM] * (6 + len(done)),
        out_specs=pl.BlockSpec(memory_space=pltpu.HBM),
        scratch_shapes=[
            pltpu.VMEM((4, rows * SUB, cols), jnp.float32),
            pltpu.SemaphoreType.DMA((parts - 1 + rows // OUT_ROWS,)),
        ],
        compiler_params=params(),
    )(where, tip, tip_m, *fields, T, s, *(v.reshape(4, rows, SUB, cols) for v in done))


def with_halo(block, sides, width, periodic):
    for axis, dim in sides:
        count = lax.axis_size(axis)
        forward = [(i, i + 1) for i in range(count - 1)]
        if periodic:
            forward.append((count - 1, 0))
        backward = [(target, source) for source, target in forward]
        low = lax.ppermute(
            lax.slice_in_dim(block, block.shape[dim] - width, None, axis=dim), axis, forward
        )
        high = lax.ppermute(lax.slice_in_dim(block, 0, width, axis=dim), axis, backward)
        block = jnp.concatenate([low, block, high], axis=dim)
    return block


def bernoulli(values):
    near_zero = jnp.abs(values) < 0.001
    safe_values = jnp.where(near_zero, 1.0, values)
    series = 1.0 - 0.5 * values + values * values / 12.0
    return jnp.where(near_zero, series, safe_values / jnp.expm1(safe_values))


def block_mul(left_block, right_block):
    return jnp.sum(left_block[:, :, None] * right_block[None, :, :], axis=1)


def invert_small(matrix):
    order_size = matrix.shape[0]
    left_rows = [[matrix[i, j] for j in range(order_size)] for i in range(order_size)]
    blank_entry = jnp.zeros_like(matrix[0, 0])
    right_rows = [
        [blank_entry + (1.0 if i == j else 0.0) for j in range(order_size)]
        for i in range(order_size)
    ]
    for k in range(order_size):
        pivot_inv = 1.0 / left_rows[k][k]
        left_rows[k] = [v * pivot_inv for v in left_rows[k]]
        right_rows[k] = [v * pivot_inv for v in right_rows[k]]
        for i in range(order_size):
            if i != k:
                factor = left_rows[i][k]
                left_rows[i] = [a - factor * b for a, b in zip(left_rows[i], left_rows[k])]
                right_rows[i] = [a - factor * b for a, b in zip(right_rows[i], right_rows[k])]
    return jnp.stack([jnp.stack(r, 0) for r in right_rows], 0)


def block_thomas(lower, diagonal, upper, right_side):

    def forward(carried, row_blocks):
        coupled_prev, solved_prev = carried
        lower_row, diag_row, upper_row, side_row = row_blocks
        reduced = diag_row - block_mul(lower_row, coupled_prev)
        inverse = invert_small(reduced)
        coupled = block_mul(inverse, upper_row)
        solved = block_mul(inverse, side_row - block_mul(lower_row, solved_prev))
        return ((coupled, solved), (coupled, solved))

    initial = (jnp.zeros_like(diagonal[0]), jnp.zeros_like(right_side[0]))
    ignored_end, (coupled_all, solved_all) = lax.scan(
        forward, initial, (lower, diagonal, upper, right_side)
    )

    def backward(following, row_blocks):
        coupled, solved = row_blocks
        current = solved - block_mul(coupled, following)
        return (current, current)

    ignored_start, result = lax.scan(
        backward, jnp.zeros_like(right_side[0]), (coupled_all, solved_all), reverse=True
    )
    return result


def stack_blocks(entries):
    stacked = jnp.stack([jnp.stack([e for e in r], 0) for r in entries], 0)
    return jnp.moveaxis(stacked, 2, 0)


def assemble(center, neighbours, fixed_charge):
    potential, concentration, permittivity = center
    blank_entry = jnp.zeros_like(potential)
    charge = fixed_charge
    for k in range(3):
        charge = charge + VALENCE[k] * concentration[k]
    residual = [-charge, blank_entry, blank_entry, blank_entry]
    jacobian = [[blank_entry] * 4 for i in range(4)]
    lower = [[blank_entry] * 4 for i in range(4)]
    upper = [[blank_entry] * 4 for i in range(4)]
    for k in range(3):
        jacobian[0][k + 1] = blank_entry - VALENCE[k]
    for nearby, inside, weight, position in neighbours:
        near_potential, near_conc, near_perm = nearby
        harmonic = 2.0 * permittivity * near_perm / (permittivity + near_perm)
        face_perm = weight * (inside * harmonic + (1.0 - inside) * permittivity)
        residual[0] = residual[0] + face_perm * (potential - near_potential)
        jacobian[0][0] = jacobian[0][0] + face_perm
        offdiag = lower if position == "lower" else upper if position == "upper" else None
        if offdiag is not None:
            offdiag[0][0] = -inside * face_perm
        for k in range(3):
            drift = VALENCE[k] * (near_potential - potential)
            face_coef = inside * weight * MOBILITY[k]
            weight_out = bernoulli(drift)
            weight_in = bernoulli(-drift)
            mean_conc = 0.5 * (concentration[k] + near_conc[k])
            residual[k + 1] = residual[k + 1] + face_coef * (
                weight_out * concentration[k] - weight_in * near_conc[k]
            )
            jacobian[k + 1][k + 1] = jacobian[k + 1][k + 1] + face_coef * weight_out
            jacobian[k + 1][0] = jacobian[k + 1][0] + face_coef * VALENCE[k] * mean_conc
            if offdiag is not None:
                offdiag[k + 1][k + 1] = -face_coef * weight_in
                offdiag[k + 1][0] = -face_coef * VALENCE[k] * mean_conc
    residual_all = jnp.moveaxis(jnp.stack([e for e in residual], 0), 1, 0)
    return (residual_all, stack_blocks(jacobian), stack_blocks(lower), stack_blocks(upper))


def split_fields(block):
    return (block[0], block[1:4], block[4])


def partition_forward(previous_vec, previous_map, first_tip, last_tip):
    identity = jnp.eye(4, dtype=first_tip.dtype).reshape((4, 4) + (1,) * (first_tip.ndim - 2))
    start_vec = first_tip[:, 0:1]
    start_left = first_tip[:, 1:5]
    start_right = first_tip[:, 5:9]
    end_vec = last_tip[:, 0:1]
    end_left = last_tip[:, 1:5]
    end_right = last_tip[:, 5:9]
    schur_block = identity - block_mul(start_left, previous_map)
    inverse = invert_small(schur_block)
    offset = block_mul(inverse, start_vec + block_mul(start_left, previous_vec))
    reach_map = block_mul(inverse, start_right)
    next_vec = end_vec + block_mul(end_left, previous_vec + block_mul(previous_map, offset))
    next_map = block_mul(end_left, block_mul(previous_map, reach_map)) + end_right
    return (next_vec, next_map, offset, reach_map)


def reduced_sweep(every_tip, zero_vec, zero_map):

    def sweep_forward(carried, tip_pair):
        previous_vec, previous_map = carried
        next_vec, next_map, offset, reach_map = partition_forward(
            previous_vec, previous_map, tip_pair[0], tip_pair[1]
        )
        return ((next_vec, next_map), (previous_vec, previous_map, offset, reach_map))

    ignored_e, (vec_all, map_all, offset_all, reach_all) = lax.scan(
        sweep_forward, (zero_vec, zero_map), every_tip
    )

    def sweep_backward(right_value, pieces):
        offset, reach_map = pieces
        return (offset + block_mul(reach_map, right_value), right_value)

    ignored_f, right_all = lax.scan(sweep_backward, zero_vec, (offset_all, reach_all), reverse=True)
    return (vec_all, map_all, offset_all, reach_all, right_all)


def on_device(potential, concentration, permittivity, fixed_charge):
    cells_wall = potential.shape[0]
    stacked = jnp.concatenate([potential[None], concentration, permittivity[None]], 0)
    walled = with_halo(stacked, (("wall", 1),), 1, False)
    planed = with_halo(stacked, (("stream", 3), ("span", 2)), 1, True)
    center = split_fields(stacked)
    wall_index = lax.axis_index("wall")
    global_row = wall_index * cells_wall + jnp.arange(cells_wall, dtype=jnp.int32)
    line_length = lax.axis_size("wall") * cells_wall
    inside_lower = (global_row > 0).astype(jnp.float32)[:, None, None]
    inside_upper = (global_row < line_length - 1).astype(jnp.float32)[:, None, None]
    neighbours = [
        (split_fields(walled[:, :-2]), inside_lower, 1.0, "lower"),
        (split_fields(walled[:, 2:]), inside_upper, 1.0, "upper"),
        (split_fields(planed[:, :, :-2, 1:-1]), 1.0, PLANE_WEIGHT, "plane"),
        (split_fields(planed[:, :, 2:, 1:-1]), 1.0, PLANE_WEIGHT, "plane"),
        (split_fields(planed[:, :, 1:-1, :-2]), 1.0, PLANE_WEIGHT, "plane"),
        (split_fields(planed[:, :, 1:-1, 2:]), 1.0, PLANE_WEIGHT, "plane"),
    ]
    residual, diagonal, lower, upper = assemble(center, neighbours, fixed_charge)
    row_ids = jnp.arange(cells_wall, dtype=jnp.int32)
    first_mask = (row_ids == 0).astype(jnp.float32)[:, None, None, None, None]
    last_mask = (row_ids == cells_wall - 1).astype(jnp.float32)[:, None, None, None, None]
    right_side = jnp.concatenate(
        [-residual[:, :, None], -lower * first_mask, -upper * last_mask], 2
    )
    solved = block_thomas(lower, diagonal, upper, right_side)
    first_tip = solved[0]
    last_tip = solved[-1]
    lines_shape = first_tip.shape[2:]
    zero_vec = jnp.zeros((4, 1) + lines_shape, jnp.float32)
    zero_map = jnp.zeros((4, 4) + lines_shape, jnp.float32)
    line_tips = jnp.stack([first_tip, last_tip], 0)[None]
    every_tip = lax.all_gather(line_tips, "wall", axis=0, tiled=True)
    vec_all, map_all, offset_all, reach_all, right_all = reduced_sweep(
        every_tip, zero_vec, zero_map
    )

    def choose_own(stacked_all):
        return lax.dynamic_index_in_dim(stacked_all, wall_index, 0, False)

    previous_vec = choose_own(vec_all)
    previous_map = choose_own(map_all)
    offset = choose_own(offset_all)
    reach_map = choose_own(reach_all)
    right_value = choose_own(right_all)
    local_first = offset + block_mul(reach_map, right_value)
    left_value = previous_vec + block_mul(previous_map, local_first)
    update = solved[:, :, 0]
    update = update + jnp.sum(solved[:, :, 1:5] * left_value[None, None, :, 0], axis=2)
    update = update + jnp.sum(solved[:, :, 5:9] * right_value[None, None, :, 0], axis=2)
    return jnp.moveaxis(update, 1, 0)


def on_any(potential, concentration, permittivity, fixed_charge):
    rows, planes, cols = potential.shape
    pair = (
        lax.axis_size("wall") == 2
        and lax.axis_size("span") % 2 == 0
        and lax.axis_size("stream") % 2 == 0
        and cols == LANES
        and rows % SUB == 0
        and planes % SUB == 0
        and rows * planes // SUB * 2 <= LANES
    )
    chosen = on_device_pair if pair else on_device
    return chosen(potential, concentration, permittivity, fixed_charge)


def solution(mesh):
    return jax.shard_map(
        on_any,
        mesh=mesh,
        in_specs=(
            P("wall", "span", "stream"),
            P(None, "wall", "span", "stream"),
            P("wall", "span", "stream"),
            P("wall", "span", "stream"),
        ),
        out_specs=P(None, "wall", "span", "stream"),
        check_vma=False,
    )
```

```python
import functools

import jax
import jax.numpy as jnp
from jax import lax
from jax.experimental import pallas as pl
from jax.experimental.pallas import tpu as pltpu
from jax.sharding import PartitionSpec as P

VALENCE = (1.0, -1.0, 2.0)
MOBILITY = (1.0, 1.5, 0.7)
HALF_ZD = tuple(0.5 * z * d for z, d in zip(VALENCE, MOBILITY))
PLANE_WEIGHT = 0.01
LANES = 128
SUB = 8
NQ = 11
ASSEMBLE_GROUP = 8
OUT_ROWS = 8
COMPOSE_LAST = False

VMEM = pl.BlockSpec(memory_space=pltpu.VMEM)


def sds(*shape):
    return jax.ShapeDtypeStruct(shape, jnp.float32)


def params(mib=8):
    return pltpu.CompilerParams(vmem_limit_bytes=mib * 1024 * 1024)


def unrolled(start, stop, step, carry, group):
    full = (stop - start) // group if stop - start > group else 0

    def body(j, carry):
        for u in range(group):
            carry = step(start + group * j + u, carry)
        return carry

    if full:
        carry = lax.fori_loop(0, full, body, carry)
    for i in range(start + group * full, stop):
        carry = step(i, carry)
    return carry


def face(phi, eps, conc, phi_m, eps_m, conc_m, weight):
    x = phi_m - phi
    y = 0.5 * x
    y = jnp.where(y == 0.0, 1e-20, y)
    t = jnp.tanh(y)
    h = y * pl.reciprocal(t, approx=True)
    e = (eps * eps_m) * pl.reciprocal(eps + eps_m, approx=True)
    if weight is None:
        e = e + e
        h2 = h + y * t
        xw, yw, hw = x, y, h
    else:
        e = e * (weight + weight)
        hw = h * weight
        yw = y * weight
        xw = yw + yw
        h2 = hw + yw * t
    p1 = hw - yw
    m1 = hw + yw
    out = (p1, 1.5 * m1, 0.7 * (h2 - xw))
    into = (m1, 1.5 * p1, 0.7 * (h2 + xw))
    g = e * x
    flux = tuple(out[k] * conc[k] - into[k] * conc_m[k] for k in range(3))
    return e, g, out, into, flux


class Signed:
    def __init__(self, value, sign=1):
        self.value, self.sign = value, sign

    def __neg__(self):
        return Signed(self.value, -self.sign)

    def __add__(self, other):
        if self.value is None:
            return other
        if other.value is None:
            return self
        if self.sign == other.sign:
            return Signed(self.value + other.value, self.sign)
        if self.sign > 0:
            return Signed(self.value - other.value)
        return Signed(other.value - self.value)

    def __sub__(self, other):
        return self + (-other)

    def __mul__(self, other):
        if self.value is None or other.value is None:
            return Signed(None)
        return Signed(self.value * other.value, self.sign * other.sign)

    def inverse(self):
        return Signed(pl.reciprocal(self.value, approx=True), self.sign)

    def array(self, like, sign=1):
        if self.value is None:
            return jnp.zeros_like(like)
        return self.value if self.sign == sign else -self.value


def signed(values):
    return [Signed(v) for v in values]


T_SIGN = ((1, 1, -1, -1), (1, 1, -1, -1), (1, -1, 1, -1), (1, -1, -1, 1))


def inv2(a, b, c, d):
    r = (a * d - b * c).inverse()
    return ((d * r, -(b * r)), (-(c * r), a * r))


def mul2(P, Q):
    return [[P[i][0] * Q[0][j] + P[i][1] * Q[1][j] for j in range(2)] for i in range(2)]


def inverse4(D):
    two = range(2)
    A = inv2(D[0][0], D[0][1], D[1][0], D[1][1])
    B = [[D[i][2 + j] for j in two] for i in two]
    E = mul2([[D[2 + i][j] for j in two] for i in two], A)
    EB = mul2(E, B)
    S = [[D[2 + i][2 + j] - EB[i][j] for j in two] for i in two]
    I = inv2(S[0][0], S[0][1], S[1][0], S[1][1])
    F = mul2(A, B)
    X = mul2(I, E)
    Y = mul2(F, I)
    FX = mul2(F, X)
    Z = [[A[i][j] + FX[i][j] for j in two] for i in two]
    return [[*Z[i], *(-y for y in Y[i])] for i in two] + [[*(-x for x in X[i]), *I[i]] for i in two]


def mat_vec(G, v):
    return [(G[i][0] * v[0] + G[i][1] * v[1]) + (G[i][2] * v[2] + G[i][3] * v[3]) for i in range(4)]


def couple(D, r, e, m, f, T, s):
    Dn = [[D[0][j] - e * T[0][j] for j in range(4)]]
    rn = [r[0] + e * s[0]]
    for k in range(3):
        Dn.append([D[k + 1][j] - (m[k] * T[0][j] + f[k] * T[k + 1][j]) for j in range(4)])
        rn.append(r[k + 1] + (m[k] * s[0] + f[k] * s[k + 1]))
    return Dn, rn


def solve_block(D, r, e, m, f):
    G = inverse4(D)
    first = mat_vec(G, [e] + list(m))
    T = [[first[i]] + [G[i][k + 1] * f[k] for k in range(3)] for i in range(4)]
    return T, mat_vec(G, r)


def pack_kernel(
    rows, planes, phi_hbm, conc_hbm, eps_hbm, charge_hbm,
    phi_ref, conc_ref, eps_ref, charge_ref, near_ref, far_ref, cols_ref, sems,
):
    fields = [
        (phi_hbm, phi_ref),
        *((conc_hbm.at[k], conc_ref.at[k]) for k in range(3)),
        (eps_hbm, eps_ref),
        (charge_hbm, charge_ref),
    ]
    copies = [pltpu.make_async_copy(*pair, sems.at[i]) for i, pair in enumerate(fields)]
    for copy in copies:
        copy.start()
    odd = lax.axis_index("span") % 2 > 0
    pair_of_lane = lax.broadcasted_iota(jnp.int32, (SUB, LANES), 1) // 2
    for f in range(5):
        copies[f].wait()
        ref = fields[f][1]
        low = ref[pl.ds(0, rows, stride=planes), :]
        high = ref[pl.ds(planes - 1, rows, stride=planes), :]
        near_ref[f] = jnp.where(odd, high, low)
        far_ref[f] = jnp.where(odd, low, high)
        packed = jnp.zeros((SUB, LANES), jnp.float32)
        for j in range(rows * planes // SUB):
            moved = pltpu.roll(ref[SUB * j : SUB * (j + 1), :], 2 * j + 1, 1)
            packed = jnp.where(pair_of_lane == j, moved, packed)
        cols_ref[f] = packed
    copies[5].wait()


def assemble_kernel(
    rows, planes, phi_ref, conc_ref, eps_ref, charge_ref,
    acc_ref, fe_ref, fu_ref, span_ref,
):
    wall = lax.axis_index("wall")
    first_wall = (wall == 0).astype(jnp.float32)
    last_wall = 1.0 - first_wall

    def cell(p, row0):
        at = pl.ds(row0 * planes + p, SUB, stride=planes)
        return phi_ref[at, :], eps_ref[at, :], [conc_ref[k, at, :] for k in range(3)]

    for row0 in range(0, rows, SUB):
        zero = jnp.zeros((SUB, LANES), jnp.float32)
        carry = [zero] * NQ
        phi, eps, conc = cell(0, row0)
        for p in range(planes):
            total = list(carry)
            if p + 1 < planes:
                phi_m, eps_m, conc_m = cell(p + 1, row0)
                e, g, out, into, flux = face(phi, eps, conc, phi_m, eps_m, conc_m, PLANE_WEIGHT)
                mine = [e, g, *out, *flux, *conc_m]
                total = [a + b for a, b in zip(total, mine)]
                carry = [e, -g, *into, *[-v for v in flux], *conc]
                phi, eps, conc = phi_m, eps_m, conc_m
            for q in range(NQ):
                span_ref[q, p * (rows + 1) + row0 : p * (rows + 1) + row0 + SUB, :] = total[q]

    def row_pass(part):
        lane = lax.broadcasted_iota(jnp.int32, (SUB, LANES), 1)
        weight = jnp.where(lane < LANES - 1, PLANE_WEIGHT, 0.0).astype(jnp.float32)

        def tile(r):
            return pl.ds(pl.multiple_of(r * planes + SUB * part, SUB), SUB)

        def load(r):
            at = tile(r)
            return phi_ref[at, :], eps_ref[at, :], [conc_ref[k, at, :] for k in range(3)]

        def finish(r, phi, eps, conc, lower, upper):
            at = tile(r)

            def fwd(v):
                return pltpu.roll(v, LANES - 1, 1)

            def back(v):
                return pltpu.roll(v, 1, 1)

            conc_m = [fwd(c) for c in conc]
            e, g, out, into, flux = face(phi, eps, conc, fwd(phi), fwd(eps), conc_m, weight)
            span = [span_ref[q, pl.ds(r + (rows + 1) * SUB * part, SUB, stride=rows + 1), :] for q in range(NQ)]
            total_e = (e + back(e)) + (lower[0] + upper[0]) + span[0]
            total_g = (g - back(g)) + (lower[1] + upper[1]) + span[1]
            charge = charge_ref[at, :] + conc[0] - conc[1] + 2.0 * conc[2]
            acc_ref[0, at, :] = total_e
            acc_ref[1, at, :] = total_g + charge
            for k in range(3):
                acc_ref[2 + k, at, :] = (out[k] + back(into[k])) + (lower[2][k] + upper[2][k]) + span[2 + k]
                acc_ref[5 + k, at, :] = -(
                    (flux[k] - back(flux[k])) + (lower[3][k] + upper[3][k]) + span[5 + k]
                )
                near = conc_m[k] + back(conc[k]) + span[8 + k] + 4.0 * conc[k]
                acc_ref[8 + k, at, :] = (HALF_ZD[k] * PLANE_WEIGHT) * near + HALF_ZD[k] * (
                    lower[4][k] + upper[4][k]
                )

        zero = jnp.zeros((SUB, LANES), jnp.float32)
        zeros = [zero] * 3

        phi, eps, conc = load(0)
        e = first_wall * eps
        lower = (e, -e * phi, zeros, zeros, zeros)

        def step(r, carry):
            phi, eps, conc, lower = carry
            phi_m, eps_m, conc_m = load(r + 1)
            e, g, out, into, flux = face(phi, eps, conc, phi_m, eps_m, conc_m, None)
            at = tile(r)
            fe_ref[at, :] = e
            for k in range(3):
                fu_ref[wall, k, at, :] = into[k]
                fu_ref[1 - wall, k, at, :] = out[k]
            both = [conc[k] + conc_m[k] for k in range(3)]
            upper = (e, g, out, flux, both)
            finish(r, phi, eps, conc, lower, upper)
            lower = (e, -g, list(into), [-v for v in flux], both)
            return phi_m, eps_m, conc_m, lower

        phi, eps, conc, lower = unrolled(0, rows - 1, step, (phi, eps, conc, lower), ASSEMBLE_GROUP)
        e = last_wall * eps
        upper = (e, -e * phi, zeros, zeros, zeros)
        finish(rows - 1, phi, eps, conc, lower, upper)

    for part in range(planes // SUB):
        row_pass(part)


def halo_terms(own, near, wrapped):
    e, g, out, _, flux = face(own[0], own[4], own[1:4], near[0], near[4], near[1:4], PLANE_WEIGHT)
    c = [near[1 + k] if wrapped is None else near[1 + k] - wrapped[1 + k] for k in range(3)]
    return [e, g, *out, *[-v for v in flux], *[(HALF_ZD[k] * PLANE_WEIGHT) * c[k] for k in range(3)]]


def first_eliminate_kernel(
    rows, planes, phi_ref, conc_ref, eps_ref, acc_ref, fe_ref, fu_ref,
    near_ref, far_ref, near_halo_ref, far_halo_ref, cols_ref, even_halo_ref, odd_halo_ref,
    t_ref, s_ref, tip_ref, side_ref, rim_ref,
):
    span_odd = lax.axis_index("span") % 2
    stream_odd = lax.axis_index("stream") % 2 > 0

    for own_ref, halo_ref, side in (
        (near_ref, near_halo_ref, span_odd),
        (far_ref, far_halo_ref, 1 - span_odd),
    ):
        own = [own_ref[f] for f in range(5)]
        near = [halo_ref[f] for f in range(5)]
        for q, v in enumerate(halo_terms(own, near, None)):
            rim_ref[q, side] = v

    odd = lax.broadcasted_iota(jnp.int32, (SUB, LANES), 1) % 2 == 1
    own, near, wrapped = [], [], []
    for f in range(5):
        mine, a, b = cols_ref[f], even_halo_ref[f], odd_halo_ref[f]
        right = jnp.where(stream_odd, b, a)
        left = jnp.where(stream_odd, a, b)
        own.append(mine)
        near.append(jnp.where(odd, pltpu.roll(left, 1, 1), pltpu.roll(right, LANES - 1, 1)))
        wrapped.append(jnp.where(odd, pltpu.roll(mine, 1, 1), pltpu.roll(mine, LANES - 1, 1)))
    for q, v in enumerate(halo_terms(own, near, wrapped)):
        side_ref[q] = v

    last = pl.multiple_of(jnp.where(lax.axis_index("wall") == 0, rows - 1, 0) * planes, planes)
    for part in range(planes // SUB):
        at = pl.ds(last + SUB * part, SUB)
        tip_ref[20 + 5 * part] = phi_ref[at, :]
        for k in range(3):
            tip_ref[21 + 5 * part + k] = conc_ref[k, at, :]
        tip_ref[24 + 5 * part] = eps_ref[at, :]

    eliminate_kernel(
        rows, planes, 0, conc_ref, acc_ref, fe_ref, fu_ref, side_ref, rim_ref,
        t_ref, s_ref, tip_ref,
    )


def eliminate_kernel(
    rows, planes, part, conc_ref, acc_ref, fe_ref, fu_ref, side_ref, rim_ref,
    t_ref, s_ref, tip_ref,
):
    wall = lax.axis_index("wall")
    lane = lax.broadcasted_iota(jnp.int32, (SUB, LANES), 1)
    edge = (lane == 0) | (lane == LANES - 1)
    plane = lax.broadcasted_iota(jnp.int32, (SUB, LANES), 0) + SUB * part
    rims = [side for side, p in enumerate((0, planes - 1)) if p // SUB == part]
    on_rim = {side: plane == (planes - 1) * side for side in rims}

    def place(i):
        return jnp.where(wall == 0, i, rows - 1 - i)

    def tile(r):
        return pl.ds(pl.multiple_of(r * planes + SUB * part, SUB), SUB)

    def own_block(i):
        r = place(i)
        at = tile(r)
        q_all = []
        for q in range(NQ):
            moved = pltpu.roll(side_ref[q], LANES - 1 - 2 * ((planes // SUB) * r + part), 1)
            total = acc_ref[q, at, :] + jnp.where(edge, moved, 0.0)
            for side in rims:
                rim = jnp.broadcast_to(rim_ref[q, side, pl.ds(r, 1), :], (SUB, LANES))
                total = total + jnp.where(on_rim[side], rim, 0.0)
            q_all.append(total)
        a, d, b = q_all[0], q_all[2:5], q_all[8:11]
        one = jnp.ones_like(a)
        zero = Signed(None)
        b, d = signed(b), signed(d)
        D = [
            [Signed(a), Signed(one, -1), Signed(one), Signed(2.0 * one, -1)],
            [b[0], d[0], zero, zero],
            [b[1], zero, d[1], zero],
            [b[2], zero, zero, d[2]],
        ]
        return at, D, signed([q_all[1], *q_all[5:8]])

    def next_face(i):
        r = place(i)
        r_next = place(i + 1)
        at, at_next, at_face = tile(r), tile(r_next), tile(jnp.minimum(r, r_next))
        m = [HALF_ZD[k] * (conc_ref[k, at, :] + conc_ref[k, at_next, :]) for k in range(3)]
        up = [fu_ref[0, k, at_face, :] for k in range(3)]
        low = [fu_ref[1, k, at_face, :] for k in range(3)]
        return Signed(fe_ref[at_face, :]), signed(m), signed(up), signed(low)

    def reduce_row(i, carry):
        at, D, r = own_block(i)
        if carry is not None:
            T, s, e, m, low = carry
            D, r = couple(D, r, e, m, low, T, s)
        return at, D, r

    def step(i, carry):
        at, D, r = reduce_row(i, carry)
        e, m, up, low = next_face(i)
        T, s = solve_block(D, r, e, m, up)
        like = e.value
        keep = pl.ds(pl.multiple_of(place(i) * SUB, SUB), SUB)
        for a in range(4):
            for b in range(4):
                t_ref[4 * a + b, keep, :] = T[a][b].array(like, T_SIGN[a][b])
            s_ref[a, keep, :] = s[a].array(like)
        return T, s, e, m, low

    carry = step(0, None)
    for i in range(1, rows - 1):
        carry = step(i, carry)
    at, D, r = reduce_row(rows - 1, carry)
    for a in range(4):
        for b in range(4):
            tip_ref[4 * a + b] = D[a][b].array(fe_ref[at, :])
        tip_ref[16 + a] = r[a].array(fe_ref[at, :])


def tip_block(ref, fields_ref, part):
    D = [signed(ref[4 * a + b] for b in range(4)) for a in range(4)]
    r = signed(ref[16 + a] for a in range(4))
    f = [fields_ref[20 + 5 * part + q] for q in range(5)]
    return D, r, f[0], f[1:4], f[4]


def with_face(D, r, e, g, m, out, flux):
    D = [list(row) for row in D]
    r = list(r)
    D[0][0] = D[0][0] + e
    r[0] = r[0] + g
    for k in range(3):
        D[k + 1][k + 1] = D[k + 1][k + 1] + out[k]
        D[k + 1][0] = D[k + 1][0] + m[k]
        r[k + 1] = r[k + 1] - flux[k]
    return D, r


def substitute_kernel(
    rows, part, own_ref, near_ref, own_first_ref, near_first_ref, t_ref, s_ref, out_ref,
    after=None, composed=False,
):
    wall = lax.axis_index("wall")
    D, r, phi, conc, eps = tip_block(own_ref, own_first_ref, part)
    Dm, rm, phi_m, conc_m, eps_m = tip_block(near_ref, near_first_ref, part)
    e, g, out, into, flux = face(phi, eps, conc, phi_m, eps_m, conc_m, None)
    e, g = Signed(e), Signed(g)
    out, into, flux = signed(out), signed(into), signed(flux)
    m = [Signed(HALF_ZD[k] * (conc[k] + conc_m[k])) for k in range(3)]
    Dm, rm = with_face(Dm, rm, e, -g, m, into, [-v for v in flux])
    T, s = solve_block(Dm, rm, e, m, out)
    D, r = with_face(D, r, e, g, m, out, flux)
    D, r = couple(D, r, e, m, into, T, s)
    x = mat_vec(inverse4(D), r)

    def put(i, x):
        at = kept_tile(rows, wall, i)
        for a in range(4):
            out_ref[a, at, :] = x[a].array(phi)

    put(rows - 1, x)
    if composed:
        for i in range(rows - 2, -1, -1):
            T, s = kept_block(t_ref, s_ref, kept_tile(rows, wall, i))
            put(i, [v + w for v, w in zip(mat_vec(T, x), s)])
            if after is not None and i % OUT_ROWS == 0:
                after(i)
        return

    for i in range(rows - 2, -1, -1):
        T, s = kept_block(t_ref, s_ref, kept_tile(rows, wall, i))
        x = [v + w for v, w in zip(mat_vec(T, x), s)]
        put(i, x)
        if after is not None and i % OUT_ROWS == 0:
            after(i)


def kept_tile(rows, wall, i):
    return pl.ds(pl.multiple_of(jnp.where(wall == 0, i, rows - 1 - i) * SUB, SUB), SUB)


def kept_block(t_ref, s_ref, at):
    T = [[Signed(t_ref[4 * a + b, at, :], T_SIGN[a][b]) for b in range(4)] for a in range(4)]
    return T, signed(s_ref[a, at, :] for a in range(4))


def compose_kernel(rows, t_ref, s_ref, t_out_ref, s_out_ref):
    wall = lax.axis_index("wall")
    T, s = None, None
    for i in range(rows - 2, -1, -1):
        at = kept_tile(rows, wall, i)
        T_row, s_row = kept_block(t_ref, s_ref, at)
        if T is None:
            T, s = T_row, s_row
        else:
            s = [v + w for v, w in zip(mat_vec(T_row, s), s_row)]
            columns = [mat_vec(T_row, [T[a][b] for a in range(4)]) for b in range(4)]
            T = [[columns[b][a] for b in range(4)] for a in range(4)]
        for a in range(4):
            like = t_ref[0, at, :]
            for b in range(4):
                t_out_ref[4 * a + b, at, :] = T[a][b].array(like, T_SIGN[a][b])
            s_out_ref[a, at, :] = s[a].array(like)


def last_substitute_kernel(
    rows, planes, own_ref, near_ref, own_first_ref, near_first_ref, t_ref, s_ref, *refs
):
    *done_refs, out_hbm, mine_ref, sems = refs
    parts = planes // SUB
    wall = lax.axis_index("wall")

    def to_hbm(ref, part, chunk, n):
        at = pl.ds(chunk, n)
        return pltpu.make_async_copy(
            ref.at[:, at], out_hbm.at[:, at, pl.ds(SUB * part, SUB), :], sems.at[len(copies)]
        )

    copies = []
    for part, ref in enumerate(done_refs):
        copies.append(to_hbm(ref, part, 0, rows))
        copies[-1].start()
    mine = mine_ref.reshape(4, rows, SUB, LANES)

    def after(i):
        first = jnp.where(wall == 0, i, rows - OUT_ROWS - i)
        copies.append(to_hbm(mine, parts - 1, first, OUT_ROWS))
        copies[-1].start()

    substitute_kernel(
        rows, parts - 1, own_ref, near_ref, own_first_ref, near_first_ref, t_ref, s_ref,
        mine_ref, after, COMPOSE_LAST,
    )
    for copy in copies:
        copy.wait()


def swap_pairs(count, first):
    pairs = []
    for i in range(first, count + first, 2):
        a, b = i % count, (i + 1) % count
        pairs += [(a, b), (b, a)]
    return pairs


def on_device_pair(potential, concentration, permittivity, fixed_charge):
    rows, planes, cols = potential.shape
    cells = rows * planes
    phi = potential.reshape(cells, cols)
    conc = concentration.reshape(3, cells, cols)
    eps = permittivity.reshape(cells, cols)
    charge = fixed_charge.reshape(cells, cols)
    n_span, n_stream = lax.axis_size("span"), lax.axis_size("stream")

    phi, conc, eps, charge, near, far, edge_cols = pl.pallas_call(
        functools.partial(pack_kernel, rows, planes),
        name="pack",
        out_shape=(
            sds(cells, cols), sds(3, cells, cols), sds(cells, cols), sds(cells, cols),
            sds(5, rows, cols), sds(5, rows, cols), sds(5, SUB, LANES),
        ),
        in_specs=[pl.BlockSpec(memory_space=pltpu.HBM)] * 4,
        out_specs=(VMEM,) * 7,
        scratch_shapes=[pltpu.SemaphoreType.DMA((6,))],
        compiler_params=params(),
    )(*(pltpu.with_memory_space_constraint(v, pltpu.HBM) for v in (phi, conc, eps, charge)))

    near_halo = lax.ppermute(near, "span", swap_pairs(n_span, 1))
    far_halo = lax.ppermute(far, "span", swap_pairs(n_span, 0))
    odd_halo = lax.ppermute(edge_cols, "stream", swap_pairs(n_stream, 1))
    even_halo = lax.ppermute(edge_cols, "stream", swap_pairs(n_stream, 0))

    acc, fe, fu = pl.pallas_call(
        functools.partial(assemble_kernel, rows, planes),
        name="assemble",
        out_shape=(sds(NQ, cells, cols), sds(cells, cols), sds(2, 3, cells, cols)),
        in_specs=[VMEM] * 4,
        out_specs=(VMEM,) * 3,
        scratch_shapes=[pltpu.VMEM((NQ, cells + planes, cols), jnp.float32)],
        compiler_params=params(),
        cost_estimate=pl.CostEstimate(flops=12_000_000, bytes_accessed=6_000_000, transcendentals=0),
    )(phi, conc, eps, charge)

    parts = planes // SUB
    across = [(0, 1), (1, 0)]
    kept = (sds(16, rows * SUB, cols), sds(4, rows * SUB, cols))
    terms = (sds(NQ, SUB, LANES), sds(NQ, 2, rows, LANES))
    T, s, tip, side, rim = pl.pallas_call(
        functools.partial(first_eliminate_kernel, rows, planes),
        name="eliminate",
        out_shape=(*kept, sds(20 + 5 * parts, SUB, cols), *terms),
        in_specs=[VMEM] * 13,
        out_specs=(VMEM,) * 5,
        compiler_params=params(),
    )(
        phi, conc, eps, acc, fe, fu, near, far, near_halo, far_halo, edge_cols,
        even_halo, odd_halo,
    )
    solved = [(tip, lax.ppermute(tip, "wall", across), T, s)]
    for part in range(1, parts):
        T, s, tip = pl.pallas_call(
            functools.partial(eliminate_kernel, rows, planes, part),
            name="eliminate",
            out_shape=(*kept, sds(20, SUB, cols)),
            in_specs=[VMEM] * 6,
            out_specs=(VMEM,) * 3,
            compiler_params=params(),
        )(conc, acc, fe, fu, side, rim)
        solved.append((tip, lax.ppermute(tip, "wall", across), T, s))

    fields = solved[0][:2]
    done = [
        pl.pallas_call(
            functools.partial(substitute_kernel, rows, part),
            name="substitute",
            out_shape=sds(4, rows * SUB, cols),
            in_specs=[VMEM] * 6,
            out_specs=VMEM,
            compiler_params=params(),
        )(tip, tip_m, *fields, T, s)
        for part, (tip, tip_m, T, s) in enumerate(solved[:-1])
    ]
    tip, tip_m, T, s = solved[-1]
    if COMPOSE_LAST:
        T, s = pl.pallas_call(
            functools.partial(compose_kernel, rows),
            name="compose",
            out_shape=kept,
            in_specs=[VMEM] * 2,
            out_specs=(VMEM,) * 2,
            compiler_params=params(),
        )(T, s)
    return pl.pallas_call(
        functools.partial(last_substitute_kernel, rows, planes),
        name="substitute",
        out_shape=sds(4, rows, planes, cols),
        in_specs=[VMEM] * (6 + len(done)),
        out_specs=pl.BlockSpec(memory_space=pltpu.HBM),
        scratch_shapes=[
            pltpu.VMEM((4, rows * SUB, cols), jnp.float32),
            pltpu.SemaphoreType.DMA((parts - 1 + rows // OUT_ROWS,)),
        ],
        compiler_params=params(),
    )(tip, tip_m, *fields, T, s, *(v.reshape(4, rows, SUB, cols) for v in done))


def with_halo(block, sides, width, periodic):
    for axis, dim in sides:
        count = lax.axis_size(axis)
        forward = [(i, i + 1) for i in range(count - 1)]
        if periodic:
            forward.append((count - 1, 0))
        backward = [(target, source) for source, target in forward]
        low = lax.ppermute(
            lax.slice_in_dim(block, block.shape[dim] - width, None, axis=dim), axis, forward
        )
        high = lax.ppermute(lax.slice_in_dim(block, 0, width, axis=dim), axis, backward)
        block = jnp.concatenate([low, block, high], axis=dim)
    return block


def bernoulli(values):
    near_zero = jnp.abs(values) < 0.001
    safe_values = jnp.where(near_zero, 1.0, values)
    series = 1.0 - 0.5 * values + values * values / 12.0
    return jnp.where(near_zero, series, safe_values / jnp.expm1(safe_values))


def block_mul(left_block, right_block):
    return jnp.sum(left_block[:, :, None] * right_block[None, :, :], axis=1)


def invert_small(matrix):
    order_size = matrix.shape[0]
    left_rows = [[matrix[i, j] for j in range(order_size)] for i in range(order_size)]
    blank_entry = jnp.zeros_like(matrix[0, 0])
    right_rows = [
        [blank_entry + (1.0 if i == j else 0.0) for j in range(order_size)]
        for i in range(order_size)
    ]
    for k in range(order_size):
        pivot_inv = 1.0 / left_rows[k][k]
        left_rows[k] = [v * pivot_inv for v in left_rows[k]]
        right_rows[k] = [v * pivot_inv for v in right_rows[k]]
        for i in range(order_size):
            if i != k:
                factor = left_rows[i][k]
                left_rows[i] = [a - factor * b for a, b in zip(left_rows[i], left_rows[k])]
                right_rows[i] = [a - factor * b for a, b in zip(right_rows[i], right_rows[k])]
    return jnp.stack([jnp.stack(r, 0) for r in right_rows], 0)


def block_thomas(lower, diagonal, upper, right_side):

    def forward(carried, row_blocks):
        coupled_prev, solved_prev = carried
        lower_row, diag_row, upper_row, side_row = row_blocks
        reduced = diag_row - block_mul(lower_row, coupled_prev)
        inverse = invert_small(reduced)
        coupled = block_mul(inverse, upper_row)
        solved = block_mul(inverse, side_row - block_mul(lower_row, solved_prev))
        return ((coupled, solved), (coupled, solved))

    initial = (jnp.zeros_like(diagonal[0]), jnp.zeros_like(right_side[0]))
    ignored_end, (coupled_all, solved_all) = lax.scan(
        forward, initial, (lower, diagonal, upper, right_side)
    )

    def backward(following, row_blocks):
        coupled, solved = row_blocks
        current = solved - block_mul(coupled, following)
        return (current, current)

    ignored_start, result = lax.scan(
        backward, jnp.zeros_like(right_side[0]), (coupled_all, solved_all), reverse=True
    )
    return result


def stack_blocks(entries):
    stacked = jnp.stack([jnp.stack([e for e in r], 0) for r in entries], 0)
    return jnp.moveaxis(stacked, 2, 0)


def assemble(center, neighbours, fixed_charge):
    potential, concentration, permittivity = center
    blank_entry = jnp.zeros_like(potential)
    charge = fixed_charge
    for k in range(3):
        charge = charge + VALENCE[k] * concentration[k]
    residual = [-charge, blank_entry, blank_entry, blank_entry]
    jacobian = [[blank_entry] * 4 for i in range(4)]
    lower = [[blank_entry] * 4 for i in range(4)]
    upper = [[blank_entry] * 4 for i in range(4)]
    for k in range(3):
        jacobian[0][k + 1] = blank_entry - VALENCE[k]
    for nearby, inside, weight, position in neighbours:
        near_potential, near_conc, near_perm = nearby
        harmonic = 2.0 * permittivity * near_perm / (permittivity + near_perm)
        face_perm = weight * (inside * harmonic + (1.0 - inside) * permittivity)
        residual[0] = residual[0] + face_perm * (potential - near_potential)
        jacobian[0][0] = jacobian[0][0] + face_perm
        offdiag = lower if position == "lower" else upper if position == "upper" else None
        if offdiag is not None:
            offdiag[0][0] = -inside * face_perm
        for k in range(3):
            drift = VALENCE[k] * (near_potential - potential)
            face_coef = inside * weight * MOBILITY[k]
            weight_out = bernoulli(drift)
            weight_in = bernoulli(-drift)
            mean_conc = 0.5 * (concentration[k] + near_conc[k])
            residual[k + 1] = residual[k + 1] + face_coef * (
                weight_out * concentration[k] - weight_in * near_conc[k]
            )
            jacobian[k + 1][k + 1] = jacobian[k + 1][k + 1] + face_coef * weight_out
            jacobian[k + 1][0] = jacobian[k + 1][0] + face_coef * VALENCE[k] * mean_conc
            if offdiag is not None:
                offdiag[k + 1][k + 1] = -face_coef * weight_in
                offdiag[k + 1][0] = -face_coef * VALENCE[k] * mean_conc
    residual_all = jnp.moveaxis(jnp.stack([e for e in residual], 0), 1, 0)
    return (residual_all, stack_blocks(jacobian), stack_blocks(lower), stack_blocks(upper))


def split_fields(block):
    return (block[0], block[1:4], block[4])


def partition_forward(previous_vec, previous_map, first_tip, last_tip):
    identity = jnp.eye(4, dtype=first_tip.dtype).reshape((4, 4) + (1,) * (first_tip.ndim - 2))
    start_vec = first_tip[:, 0:1]
    start_left = first_tip[:, 1:5]
    start_right = first_tip[:, 5:9]
    end_vec = last_tip[:, 0:1]
    end_left = last_tip[:, 1:5]
    end_right = last_tip[:, 5:9]
    schur_block = identity - block_mul(start_left, previous_map)
    inverse = invert_small(schur_block)
    offset = block_mul(inverse, start_vec + block_mul(start_left, previous_vec))
    reach_map = block_mul(inverse, start_right)
    next_vec = end_vec + block_mul(end_left, previous_vec + block_mul(previous_map, offset))
    next_map = block_mul(end_left, block_mul(previous_map, reach_map)) + end_right
    return (next_vec, next_map, offset, reach_map)


def reduced_sweep(every_tip, zero_vec, zero_map):

    def sweep_forward(carried, tip_pair):
        previous_vec, previous_map = carried
        next_vec, next_map, offset, reach_map = partition_forward(
            previous_vec, previous_map, tip_pair[0], tip_pair[1]
        )
        return ((next_vec, next_map), (previous_vec, previous_map, offset, reach_map))

    ignored_e, (vec_all, map_all, offset_all, reach_all) = lax.scan(
        sweep_forward, (zero_vec, zero_map), every_tip
    )

    def sweep_backward(right_value, pieces):
        offset, reach_map = pieces
        return (offset + block_mul(reach_map, right_value), right_value)

    ignored_f, right_all = lax.scan(sweep_backward, zero_vec, (offset_all, reach_all), reverse=True)
    return (vec_all, map_all, offset_all, reach_all, right_all)


def on_device(potential, concentration, permittivity, fixed_charge):
    cells_wall = potential.shape[0]
    stacked = jnp.concatenate([potential[None], concentration, permittivity[None]], 0)
    walled = with_halo(stacked, (("wall", 1),), 1, False)
    planed = with_halo(stacked, (("stream", 3), ("span", 2)), 1, True)
    center = split_fields(stacked)
    wall_index = lax.axis_index("wall")
    global_row = wall_index * cells_wall + jnp.arange(cells_wall, dtype=jnp.int32)
    line_length = lax.axis_size("wall") * cells_wall
    inside_lower = (global_row > 0).astype(jnp.float32)[:, None, None]
    inside_upper = (global_row < line_length - 1).astype(jnp.float32)[:, None, None]
    neighbours = [
        (split_fields(walled[:, :-2]), inside_lower, 1.0, "lower"),
        (split_fields(walled[:, 2:]), inside_upper, 1.0, "upper"),
        (split_fields(planed[:, :, :-2, 1:-1]), 1.0, PLANE_WEIGHT, "plane"),
        (split_fields(planed[:, :, 2:, 1:-1]), 1.0, PLANE_WEIGHT, "plane"),
        (split_fields(planed[:, :, 1:-1, :-2]), 1.0, PLANE_WEIGHT, "plane"),
        (split_fields(planed[:, :, 1:-1, 2:]), 1.0, PLANE_WEIGHT, "plane"),
    ]
    residual, diagonal, lower, upper = assemble(center, neighbours, fixed_charge)
    row_ids = jnp.arange(cells_wall, dtype=jnp.int32)
    first_mask = (row_ids == 0).astype(jnp.float32)[:, None, None, None, None]
    last_mask = (row_ids == cells_wall - 1).astype(jnp.float32)[:, None, None, None, None]
    right_side = jnp.concatenate(
        [-residual[:, :, None], -lower * first_mask, -upper * last_mask], 2
    )
    solved = block_thomas(lower, diagonal, upper, right_side)
    first_tip = solved[0]
    last_tip = solved[-1]
    lines_shape = first_tip.shape[2:]
    zero_vec = jnp.zeros((4, 1) + lines_shape, jnp.float32)
    zero_map = jnp.zeros((4, 4) + lines_shape, jnp.float32)
    line_tips = jnp.stack([first_tip, last_tip], 0)[None]
    every_tip = lax.all_gather(line_tips, "wall", axis=0, tiled=True)
    vec_all, map_all, offset_all, reach_all, right_all = reduced_sweep(
        every_tip, zero_vec, zero_map
    )

    def choose_own(stacked_all):
        return lax.dynamic_index_in_dim(stacked_all, wall_index, 0, False)

    previous_vec = choose_own(vec_all)
    previous_map = choose_own(map_all)
    offset = choose_own(offset_all)
    reach_map = choose_own(reach_all)
    right_value = choose_own(right_all)
    local_first = offset + block_mul(reach_map, right_value)
    left_value = previous_vec + block_mul(previous_map, local_first)
    update = solved[:, :, 0]
    update = update + jnp.sum(solved[:, :, 1:5] * left_value[None, None, :, 0], axis=2)
    update = update + jnp.sum(solved[:, :, 5:9] * right_value[None, None, :, 0], axis=2)
    return jnp.moveaxis(update, 1, 0)


def on_any(potential, concentration, permittivity, fixed_charge):
    rows, planes, cols = potential.shape
    pair = (
        lax.axis_size("wall") == 2
        and lax.axis_size("span") % 2 == 0
        and lax.axis_size("stream") % 2 == 0
        and cols == LANES
        and rows % SUB == 0
        and planes % SUB == 0
        and rows * planes // SUB * 2 <= LANES
    )
    chosen = on_device_pair if pair else on_device
    return chosen(potential, concentration, permittivity, fixed_charge)


def solution(mesh):
    return jax.shard_map(
        on_any,
        mesh=mesh,
        in_specs=(
            P("wall", "span", "stream"),
            P(None, "wall", "span", "stream"),
            P("wall", "span", "stream"),
            P("wall", "span", "stream"),
        ),
        out_specs=P(None, "wall", "span", "stream"),
        check_vma=False,
    )
```

```python
import functools

import jax
import jax.numpy as jnp
from jax import lax
from jax.experimental import pallas as pl
from jax.experimental.pallas import tpu as pltpu
from jax.sharding import PartitionSpec as P

VALENCE = (1.0, -1.0, 2.0)
MOBILITY = (1.0, 1.5, 0.7)
HALF_ZD = tuple(0.5 * z * d for z, d in zip(VALENCE, MOBILITY))
PLANE_WEIGHT = 0.01
LANES = 128
SUB = 8
NQ = 11
ASSEMBLE_GROUP = 8
OUT_ROWS = 8

VMEM = pl.BlockSpec(memory_space=pltpu.VMEM)


def sds(*shape):
    return jax.ShapeDtypeStruct(shape, jnp.float32)


def params(mib=8):
    return pltpu.CompilerParams(vmem_limit_bytes=mib * 1024 * 1024)


def unrolled(start, stop, step, carry, group):
    full = (stop - start) // group if stop - start > group else 0

    def body(j, carry):
        for u in range(group):
            carry = step(start + group * j + u, carry)
        return carry

    if full:
        carry = lax.fori_loop(0, full, body, carry)
    for i in range(start + group * full, stop):
        carry = step(i, carry)
    return carry


def face(phi, eps, conc, phi_m, eps_m, conc_m, weight):
    x = phi_m - phi
    y = 0.5 * x
    y = jnp.where(y == 0.0, 1e-20, y)
    t = jnp.tanh(y)
    h = y * pl.reciprocal(t, approx=True)
    e = (eps * eps_m) * pl.reciprocal(eps + eps_m, approx=True)
    if weight is None:
        e = e + e
        h2 = h + y * t
        xw, yw, hw = x, y, h
    else:
        e = e * (weight + weight)
        hw = h * weight
        yw = y * weight
        xw = yw + yw
        h2 = hw + yw * t
    p1 = hw - yw
    m1 = hw + yw
    out = (p1, 1.5 * m1, 0.7 * (h2 - xw))
    into = (m1, 1.5 * p1, 0.7 * (h2 + xw))
    g = e * x
    flux = tuple(out[k] * conc[k] - into[k] * conc_m[k] for k in range(3))
    return e, g, out, into, flux


class Signed:
    def __init__(self, value, sign=1):
        self.value, self.sign = value, sign

    def __neg__(self):
        return Signed(self.value, -self.sign)

    def __add__(self, other):
        if self.value is None:
            return other
        if other.value is None:
            return self
        if self.sign == other.sign:
            return Signed(self.value + other.value, self.sign)
        if self.sign > 0:
            return Signed(self.value - other.value)
        return Signed(other.value - self.value)

    def __sub__(self, other):
        return self + (-other)

    def __mul__(self, other):
        if self.value is None or other.value is None:
            return Signed(None)
        return Signed(self.value * other.value, self.sign * other.sign)

    def inverse(self):
        return Signed(pl.reciprocal(self.value, approx=True), self.sign)

    def array(self, like, sign=1):
        if self.value is None:
            return jnp.zeros_like(like)
        return self.value if self.sign == sign else -self.value


def signed(values):
    return [Signed(v) for v in values]


T_SIGN = ((1, 1, -1, -1), (1, 1, -1, -1), (1, -1, 1, -1), (1, -1, -1, 1))


def inv2(a, b, c, d):
    r = (a * d - b * c).inverse()
    return ((d * r, -(b * r)), (-(c * r), a * r))


def mul2(P, Q):
    return [[P[i][0] * Q[0][j] + P[i][1] * Q[1][j] for j in range(2)] for i in range(2)]


def factor4(D):
    two = range(2)
    A = inv2(D[0][0], D[0][1], D[1][0], D[1][1])
    B = [[D[i][2 + j] for j in two] for i in two]
    E = mul2([[D[2 + i][j] for j in two] for i in two], A)
    EB = mul2(E, B)
    S = [[D[2 + i][2 + j] - EB[i][j] for j in two] for i in two]
    I = inv2(S[0][0], S[0][1], S[1][0], S[1][1])
    return A, E, I, mul2(A, B)


def apply4(factors, w):
    A, E, I, F = factors
    two = range(2)
    t = [w[2 + i] - (E[i][0] * w[0] + E[i][1] * w[1]) for i in two]
    low = [I[i][0] * t[0] + I[i][1] * t[1] for i in two]
    high = [
        (A[i][0] * w[0] + A[i][1] * w[1]) - (F[i][0] * low[0] + F[i][1] * low[1]) for i in two
    ]
    return high + low


def mat_vec(G, v):
    return [(G[i][0] * v[0] + G[i][1] * v[1]) + (G[i][2] * v[2] + G[i][3] * v[3]) for i in range(4)]


def couple(D, r, e, m, f, T, s):
    Dn = [[D[0][j] - e * T[0][j] for j in range(4)]]
    rn = [r[0] + e * s[0]]
    for k in range(3):
        Dn.append([D[k + 1][j] - (m[k] * T[0][j] + f[k] * T[k + 1][j]) for j in range(4)])
        rn.append(r[k + 1] + (m[k] * s[0] + f[k] * s[k + 1]))
    return Dn, rn


def solve_block(D, r, e, m, f):
    factors = factor4(D)
    columns = [apply4(factors, [e] + list(m))]
    for k in range(3):
        w = [Signed(None)] * 4
        w[k + 1] = f[k]
        columns.append(apply4(factors, w))
    return [[columns[b][a] for b in range(4)] for a in range(4)], apply4(factors, r)


def pack_kernel(
    rows, planes, phi_hbm, conc_hbm, eps_hbm, charge_hbm,
    phi_ref, conc_ref, eps_ref, charge_ref, near_ref, far_ref, sems,
):
    fields = [
        (phi_hbm, phi_ref),
        *((conc_hbm.at[k], conc_ref.at[k]) for k in range(3)),
        (eps_hbm, eps_ref),
        (charge_hbm, charge_ref),
    ]
    copies = [pltpu.make_async_copy(*pair, sems.at[i]) for i, pair in enumerate(fields)]
    for copy in copies:
        copy.start()
    odd = lax.axis_index("span") % 2 > 0
    for f in range(5):
        copies[f].wait()
        ref = fields[f][1]
        low = ref[pl.ds(0, rows, stride=planes), :]
        high = ref[pl.ds(planes - 1, rows, stride=planes), :]
        near_ref[f] = jnp.where(odd, high, low)
        far_ref[f] = jnp.where(odd, low, high)
    copies[5].wait()


def columns_kernel(rows, planes, phi_ref, conc_ref, eps_ref, cols_ref):
    pair_of_lane = lax.broadcasted_iota(jnp.int32, (SUB, LANES), 1) // 2
    for f, ref in enumerate([phi_ref, *(conc_ref.at[k] for k in range(3)), eps_ref]):
        packed = jnp.zeros((SUB, LANES), jnp.float32)
        for j in range(rows * planes // SUB):
            moved = pltpu.roll(ref[SUB * j : SUB * (j + 1), :], 2 * j + 1, 1)
            packed = jnp.where(pair_of_lane == j, moved, packed)
        cols_ref[f] = packed


def assemble_kernel(
    rows, planes, phi_ref, conc_ref, eps_ref, charge_ref,
    acc_ref, fe_ref, fu_ref, span_ref,
):
    wall = lax.axis_index("wall")
    first_wall = (wall == 0).astype(jnp.float32)
    last_wall = 1.0 - first_wall

    def cell(p, row0):
        at = pl.ds(row0 * planes + p, SUB, stride=planes)
        return phi_ref[at, :], eps_ref[at, :], [conc_ref[k, at, :] for k in range(3)]

    for row0 in range(0, rows, SUB):
        zero = jnp.zeros((SUB, LANES), jnp.float32)
        carry = [zero] * NQ
        phi, eps, conc = cell(0, row0)
        for p in range(planes):
            total = list(carry)
            if p + 1 < planes:
                phi_m, eps_m, conc_m = cell(p + 1, row0)
                e, g, out, into, flux = face(phi, eps, conc, phi_m, eps_m, conc_m, PLANE_WEIGHT)
                mine = [e, g, *out, *flux, *conc_m]
                total = [a + b for a, b in zip(total, mine)]
                carry = [e, -g, *into, *[-v for v in flux], *conc]
                phi, eps, conc = phi_m, eps_m, conc_m
            for q in range(NQ):
                span_ref[q, p * (rows + 1) + row0 : p * (rows + 1) + row0 + SUB, :] = total[q]

    def row_pass(part):
        lane = lax.broadcasted_iota(jnp.int32, (SUB, LANES), 1)
        weight = jnp.where(lane < LANES - 1, PLANE_WEIGHT, 0.0).astype(jnp.float32)

        def tile(r):
            return pl.ds(pl.multiple_of(r * planes + SUB * part, SUB), SUB)

        def load(r):
            at = tile(r)
            return phi_ref[at, :], eps_ref[at, :], [conc_ref[k, at, :] for k in range(3)]

        def finish(r, phi, eps, conc, lower, upper):
            at = tile(r)

            def fwd(v):
                return pltpu.roll(v, LANES - 1, 1)

            def back(v):
                return pltpu.roll(v, 1, 1)

            conc_m = [fwd(c) for c in conc]
            e, g, out, into, flux = face(phi, eps, conc, fwd(phi), fwd(eps), conc_m, weight)
            span = [span_ref[q, pl.ds(r + (rows + 1) * SUB * part, SUB, stride=rows + 1), :] for q in range(NQ)]
            total_e = (e + back(e)) + (lower[0] + upper[0]) + span[0]
            total_g = (g - back(g)) + (lower[1] + upper[1]) + span[1]
            charge = charge_ref[at, :] + conc[0] - conc[1] + 2.0 * conc[2]
            acc_ref[0, at, :] = total_e
            acc_ref[1, at, :] = total_g + charge
            for k in range(3):
                acc_ref[2 + k, at, :] = (out[k] + back(into[k])) + (lower[2][k] + upper[2][k]) + span[2 + k]
                acc_ref[5 + k, at, :] = -(
                    (flux[k] - back(flux[k])) + (lower[3][k] + upper[3][k]) + span[5 + k]
                )
                near = conc_m[k] + back(conc[k]) + span[8 + k] + 4.0 * conc[k]
                acc_ref[8 + k, at, :] = (HALF_ZD[k] * PLANE_WEIGHT) * near + HALF_ZD[k] * (
                    lower[4][k] + upper[4][k]
                )

        zero = jnp.zeros((SUB, LANES), jnp.float32)
        zeros = [zero] * 3

        phi, eps, conc = load(0)
        e = first_wall * eps
        lower = (e, -e * phi, zeros, zeros, zeros)

        def step(r, carry):
            phi, eps, conc, lower = carry
            phi_m, eps_m, conc_m = load(r + 1)
            e, g, out, into, flux = face(phi, eps, conc, phi_m, eps_m, conc_m, None)
            at = tile(r)
            fe_ref[at, :] = e
            for k in range(3):
                fu_ref[wall, k, at, :] = into[k]
                fu_ref[1 - wall, k, at, :] = out[k]
            both = [conc[k] + conc_m[k] for k in range(3)]
            upper = (e, g, out, flux, both)
            finish(r, phi, eps, conc, lower, upper)
            lower = (e, -g, list(into), [-v for v in flux], both)
            return phi_m, eps_m, conc_m, lower

        phi, eps, conc, lower = unrolled(0, rows - 1, step, (phi, eps, conc, lower), ASSEMBLE_GROUP)
        e = last_wall * eps
        upper = (e, -e * phi, zeros, zeros, zeros)
        finish(rows - 1, phi, eps, conc, lower, upper)

    for part in range(planes // SUB):
        row_pass(part)


def halo_terms(own, near, wrapped):
    e, g, out, _, flux = face(own[0], own[4], own[1:4], near[0], near[4], near[1:4], PLANE_WEIGHT)
    c = [near[1 + k] if wrapped is None else near[1 + k] - wrapped[1 + k] for k in range(3)]
    return [e, g, *out, *[-v for v in flux], *[(HALF_ZD[k] * PLANE_WEIGHT) * c[k] for k in range(3)]]


def first_eliminate_kernel(
    rows, planes, phi_ref, conc_ref, eps_ref, acc_ref, fe_ref, fu_ref,
    near_ref, far_ref, near_halo_ref, far_halo_ref, cols_ref, even_halo_ref, odd_halo_ref,
    t_ref, s_ref, tip_ref, side_ref, rim_ref,
):
    span_odd = lax.axis_index("span") % 2
    stream_odd = lax.axis_index("stream") % 2 > 0

    for own_ref, halo_ref, side in (
        (near_ref, near_halo_ref, span_odd),
        (far_ref, far_halo_ref, 1 - span_odd),
    ):
        own = [own_ref[f] for f in range(5)]
        near = [halo_ref[f] for f in range(5)]
        for q, v in enumerate(halo_terms(own, near, None)):
            rim_ref[q, side] = v

    odd = lax.broadcasted_iota(jnp.int32, (SUB, LANES), 1) % 2 == 1
    own, near, wrapped = [], [], []
    for f in range(5):
        mine, a, b = cols_ref[f], even_halo_ref[f], odd_halo_ref[f]
        right = jnp.where(stream_odd, b, a)
        left = jnp.where(stream_odd, a, b)
        own.append(mine)
        near.append(jnp.where(odd, pltpu.roll(left, 1, 1), pltpu.roll(right, LANES - 1, 1)))
        wrapped.append(jnp.where(odd, pltpu.roll(mine, 1, 1), pltpu.roll(mine, LANES - 1, 1)))
    for q, v in enumerate(halo_terms(own, near, wrapped)):
        side_ref[q] = v

    last = pl.multiple_of(jnp.where(lax.axis_index("wall") == 0, rows - 1, 0) * planes, planes)
    for part in range(planes // SUB):
        at = pl.ds(last + SUB * part, SUB)
        tip_ref[20 + 5 * part] = phi_ref[at, :]
        for k in range(3):
            tip_ref[21 + 5 * part + k] = conc_ref[k, at, :]
        tip_ref[24 + 5 * part] = eps_ref[at, :]

    eliminate_kernel(
        rows, planes, 0, conc_ref, acc_ref, fe_ref, fu_ref, side_ref, rim_ref,
        t_ref, s_ref, tip_ref,
    )


def eliminate_kernel(
    rows, planes, part, conc_ref, acc_ref, fe_ref, fu_ref, side_ref, rim_ref,
    t_ref, s_ref, tip_ref,
):
    wall = lax.axis_index("wall")
    lane = lax.broadcasted_iota(jnp.int32, (SUB, LANES), 1)
    edge = (lane == 0) | (lane == LANES - 1)
    plane = lax.broadcasted_iota(jnp.int32, (SUB, LANES), 0) + SUB * part
    rims = [side for side, p in enumerate((0, planes - 1)) if p // SUB == part]
    on_rim = {side: plane == (planes - 1) * side for side in rims}

    def place(i):
        return jnp.where(wall == 0, i, rows - 1 - i)

    def tile(r):
        return pl.ds(pl.multiple_of(r * planes + SUB * part, SUB), SUB)

    def own_block(i):
        r = place(i)
        at = tile(r)
        q_all = []
        for q in range(NQ):
            moved = pltpu.roll(side_ref[q], LANES - 1 - 2 * ((planes // SUB) * r + part), 1)
            total = acc_ref[q, at, :] + jnp.where(edge, moved, 0.0)
            for side in rims:
                rim = jnp.broadcast_to(rim_ref[q, side, pl.ds(r, 1), :], (SUB, LANES))
                total = total + jnp.where(on_rim[side], rim, 0.0)
            q_all.append(total)
        a, d, b = q_all[0], q_all[2:5], q_all[8:11]
        one = jnp.ones_like(a)
        zero = Signed(None)
        b, d = signed(b), signed(d)
        D = [
            [Signed(a), Signed(one, -1), Signed(one), Signed(2.0 * one, -1)],
            [b[0], d[0], zero, zero],
            [b[1], zero, d[1], zero],
            [b[2], zero, zero, d[2]],
        ]
        return at, D, signed([q_all[1], *q_all[5:8]])

    def next_face(i):
        r = place(i)
        r_next = place(i + 1)
        at, at_next, at_face = tile(r), tile(r_next), tile(jnp.minimum(r, r_next))
        m = [HALF_ZD[k] * (conc_ref[k, at, :] + conc_ref[k, at_next, :]) for k in range(3)]
        up = [fu_ref[0, k, at_face, :] for k in range(3)]
        low = [fu_ref[1, k, at_face, :] for k in range(3)]
        return Signed(fe_ref[at_face, :]), signed(m), signed(up), signed(low)

    def reduce_row(i, carry):
        at, D, r = own_block(i)
        if carry is not None:
            T, s, e, m, low = carry
            D, r = couple(D, r, e, m, low, T, s)
        return at, D, r

    def step(i, carry):
        at, D, r = reduce_row(i, carry)
        e, m, up, low = next_face(i)
        T, s = solve_block(D, r, e, m, up)
        like = e.value
        keep = pl.ds(pl.multiple_of(place(i) * SUB, SUB), SUB)
        for a in range(4):
            for b in range(4):
                t_ref[4 * a + b, keep, :] = T[a][b].array(like, T_SIGN[a][b])
            s_ref[a, keep, :] = s[a].array(like)
        return T, s, e, m, low

    carry = step(0, None)
    for i in range(1, rows - 1):
        carry = step(i, carry)
    at, D, r = reduce_row(rows - 1, carry)
    for a in range(4):
        for b in range(4):
            tip_ref[4 * a + b] = D[a][b].array(fe_ref[at, :])
        tip_ref[16 + a] = r[a].array(fe_ref[at, :])


def tip_block(ref, fields_ref, part):
    D = [signed(ref[4 * a + b] for b in range(4)) for a in range(4)]
    r = signed(ref[16 + a] for a in range(4))
    f = [fields_ref[20 + 5 * part + q] for q in range(5)]
    return D, r, f[0], f[1:4], f[4]


def with_face(D, r, e, g, m, out, flux):
    D = [list(row) for row in D]
    r = list(r)
    D[0][0] = D[0][0] + e
    r[0] = r[0] + g
    for k in range(3):
        D[k + 1][k + 1] = D[k + 1][k + 1] + out[k]
        D[k + 1][0] = D[k + 1][0] + m[k]
        r[k + 1] = r[k + 1] - flux[k]
    return D, r


def substitute_kernel(
    rows, part, own_ref, near_ref, own_first_ref, near_first_ref, t_ref, s_ref, out_ref,
    after=None,
):
    wall = lax.axis_index("wall")
    D, r, phi, conc, eps = tip_block(own_ref, own_first_ref, part)
    Dm, rm, phi_m, conc_m, eps_m = tip_block(near_ref, near_first_ref, part)
    e, g, out, into, flux = face(phi, eps, conc, phi_m, eps_m, conc_m, None)
    e, g = Signed(e), Signed(g)
    out, into, flux = signed(out), signed(into), signed(flux)
    m = [Signed(HALF_ZD[k] * (conc[k] + conc_m[k])) for k in range(3)]
    Dm, rm = with_face(Dm, rm, e, -g, m, into, [-v for v in flux])
    T, s = solve_block(Dm, rm, e, m, out)
    D, r = with_face(D, r, e, g, m, out, flux)
    D, r = couple(D, r, e, m, into, T, s)
    x = apply4(factor4(D), r)

    def put(i, x):
        at = kept_tile(rows, wall, i)
        for a in range(4):
            out_ref[a, at, :] = x[a].array(phi)

    put(rows - 1, x)
    for i in range(rows - 2, -1, -1):
        T, s = kept_block(t_ref, s_ref, kept_tile(rows, wall, i))
        x = [v + w for v, w in zip(mat_vec(T, x), s)]
        put(i, x)
        if after is not None and i % OUT_ROWS == 0:
            after(i)


def kept_tile(rows, wall, i):
    return pl.ds(pl.multiple_of(jnp.where(wall == 0, i, rows - 1 - i) * SUB, SUB), SUB)


def kept_block(t_ref, s_ref, at):
    T = [[Signed(t_ref[4 * a + b, at, :], T_SIGN[a][b]) for b in range(4)] for a in range(4)]
    return T, signed(s_ref[a, at, :] for a in range(4))


def last_substitute_kernel(
    rows, planes, own_ref, near_ref, own_first_ref, near_first_ref, t_ref, s_ref, *refs
):
    *done_refs, out_hbm, mine_ref, sems = refs
    parts = planes // SUB
    wall = lax.axis_index("wall")

    def to_hbm(ref, part, chunk, n):
        at = pl.ds(chunk, n)
        return pltpu.make_async_copy(
            ref.at[:, at], out_hbm.at[:, at, pl.ds(SUB * part, SUB), :], sems.at[len(copies)]
        )

    copies = []
    for part, ref in enumerate(done_refs):
        copies.append(to_hbm(ref, part, 0, rows))
        copies[-1].start()
    mine = mine_ref.reshape(4, rows, SUB, LANES)

    def after(i):
        first = jnp.where(wall == 0, i, rows - OUT_ROWS - i)
        copies.append(to_hbm(mine, parts - 1, first, OUT_ROWS))
        copies[-1].start()

    substitute_kernel(
        rows, parts - 1, own_ref, near_ref, own_first_ref, near_first_ref, t_ref, s_ref,
        mine_ref, after,
    )
    for copy in copies:
        copy.wait()


def swap_pairs(count, first):
    pairs = []
    for i in range(first, count + first, 2):
        a, b = i % count, (i + 1) % count
        pairs += [(a, b), (b, a)]
    return pairs


def on_device_pair(potential, concentration, permittivity, fixed_charge):
    rows, planes, cols = potential.shape
    cells = rows * planes
    phi = potential.reshape(cells, cols)
    conc = concentration.reshape(3, cells, cols)
    eps = permittivity.reshape(cells, cols)
    charge = fixed_charge.reshape(cells, cols)
    n_span, n_stream = lax.axis_size("span"), lax.axis_size("stream")

    phi, conc, eps, charge, near, far = pl.pallas_call(
        functools.partial(pack_kernel, rows, planes),
        name="pack",
        out_shape=(
            sds(cells, cols), sds(3, cells, cols), sds(cells, cols), sds(cells, cols),
            sds(5, rows, cols), sds(5, rows, cols),
        ),
        in_specs=[pl.BlockSpec(memory_space=pltpu.HBM)] * 4,
        out_specs=(VMEM,) * 6,
        scratch_shapes=[pltpu.SemaphoreType.DMA((6,))],
        compiler_params=params(),
    )(*(pltpu.with_memory_space_constraint(v, pltpu.HBM) for v in (phi, conc, eps, charge)))

    near_halo = lax.ppermute(near, "span", swap_pairs(n_span, 1))
    far_halo = lax.ppermute(far, "span", swap_pairs(n_span, 0))
    edge_cols = pl.pallas_call(
        functools.partial(columns_kernel, rows, planes),
        name="columns",
        out_shape=sds(5, SUB, LANES),
        in_specs=[VMEM] * 3,
        out_specs=VMEM,
        compiler_params=params(),
    )(phi, conc, eps)
    odd_halo = lax.ppermute(edge_cols, "stream", swap_pairs(n_stream, 1))
    even_halo = lax.ppermute(edge_cols, "stream", swap_pairs(n_stream, 0))

    acc, fe, fu = pl.pallas_call(
        functools.partial(assemble_kernel, rows, planes),
        name="assemble",
        out_shape=(sds(NQ, cells, cols), sds(cells, cols), sds(2, 3, cells, cols)),
        in_specs=[VMEM] * 4,
        out_specs=(VMEM,) * 3,
        scratch_shapes=[pltpu.VMEM((NQ, cells + planes, cols), jnp.float32)],
        compiler_params=params(),
        cost_estimate=pl.CostEstimate(flops=12_000_000, bytes_accessed=6_000_000, transcendentals=0),
    )(phi, conc, eps, charge)

    parts = planes // SUB
    across = [(0, 1), (1, 0)]
    kept = (sds(16, rows * SUB, cols), sds(4, rows * SUB, cols))
    terms = (sds(NQ, SUB, LANES), sds(NQ, 2, rows, LANES))
    T, s, tip, side, rim = pl.pallas_call(
        functools.partial(first_eliminate_kernel, rows, planes),
        name="eliminate",
        out_shape=(*kept, sds(20 + 5 * parts, SUB, cols), *terms),
        in_specs=[VMEM] * 13,
        out_specs=(VMEM,) * 5,
        compiler_params=params(),
    )(
        phi, conc, eps, acc, fe, fu, near, far, near_halo, far_halo, edge_cols,
        even_halo, odd_halo,
    )
    solved = [(tip, lax.ppermute(tip, "wall", across), T, s)]
    for part in range(1, parts):
        T, s, tip = pl.pallas_call(
            functools.partial(eliminate_kernel, rows, planes, part),
            name="eliminate",
            out_shape=(*kept, sds(20, SUB, cols)),
            in_specs=[VMEM] * 6,
            out_specs=(VMEM,) * 3,
            compiler_params=params(),
        )(conc, acc, fe, fu, side, rim)
        solved.append((tip, lax.ppermute(tip, "wall", across), T, s))

    fields = solved[0][:2]
    done = [
        pl.pallas_call(
            functools.partial(substitute_kernel, rows, part),
            name="substitute",
            out_shape=sds(4, rows * SUB, cols),
            in_specs=[VMEM] * 6,
            out_specs=VMEM,
            compiler_params=params(),
        )(tip, tip_m, *fields, T, s)
        for part, (tip, tip_m, T, s) in enumerate(solved[:-1])
    ]
    tip, tip_m, T, s = solved[-1]
    return pl.pallas_call(
        functools.partial(last_substitute_kernel, rows, planes),
        name="substitute",
        out_shape=sds(4, rows, planes, cols),
        in_specs=[VMEM] * (6 + len(done)),
        out_specs=pl.BlockSpec(memory_space=pltpu.HBM),
        scratch_shapes=[
            pltpu.VMEM((4, rows * SUB, cols), jnp.float32),
            pltpu.SemaphoreType.DMA((parts - 1 + rows // OUT_ROWS,)),
        ],
        compiler_params=params(),
    )(tip, tip_m, *fields, T, s, *(v.reshape(4, rows, SUB, cols) for v in done))


def with_halo(block, sides, width, periodic):
    for axis, dim in sides:
        count = lax.axis_size(axis)
        forward = [(i, i + 1) for i in range(count - 1)]
        if periodic:
            forward.append((count - 1, 0))
        backward = [(target, source) for source, target in forward]
        low = lax.ppermute(
            lax.slice_in_dim(block, block.shape[dim] - width, None, axis=dim), axis, forward
        )
        high = lax.ppermute(lax.slice_in_dim(block, 0, width, axis=dim), axis, backward)
        block = jnp.concatenate([low, block, high], axis=dim)
    return block


def bernoulli(values):
    near_zero = jnp.abs(values) < 0.001
    safe_values = jnp.where(near_zero, 1.0, values)
    series = 1.0 - 0.5 * values + values * values / 12.0
    return jnp.where(near_zero, series, safe_values / jnp.expm1(safe_values))


def block_mul(left_block, right_block):
    return jnp.sum(left_block[:, :, None] * right_block[None, :, :], axis=1)


def invert_small(matrix):
    order_size = matrix.shape[0]
    left_rows = [[matrix[i, j] for j in range(order_size)] for i in range(order_size)]
    blank_entry = jnp.zeros_like(matrix[0, 0])
    right_rows = [
        [blank_entry + (1.0 if i == j else 0.0) for j in range(order_size)]
        for i in range(order_size)
    ]
    for k in range(order_size):
        pivot_inv = 1.0 / left_rows[k][k]
        left_rows[k] = [v * pivot_inv for v in left_rows[k]]
        right_rows[k] = [v * pivot_inv for v in right_rows[k]]
        for i in range(order_size):
            if i != k:
                factor = left_rows[i][k]
                left_rows[i] = [a - factor * b for a, b in zip(left_rows[i], left_rows[k])]
                right_rows[i] = [a - factor * b for a, b in zip(right_rows[i], right_rows[k])]
    return jnp.stack([jnp.stack(r, 0) for r in right_rows], 0)


def block_thomas(lower, diagonal, upper, right_side):

    def forward(carried, row_blocks):
        coupled_prev, solved_prev = carried
        lower_row, diag_row, upper_row, side_row = row_blocks
        reduced = diag_row - block_mul(lower_row, coupled_prev)
        inverse = invert_small(reduced)
        coupled = block_mul(inverse, upper_row)
        solved = block_mul(inverse, side_row - block_mul(lower_row, solved_prev))
        return ((coupled, solved), (coupled, solved))

    initial = (jnp.zeros_like(diagonal[0]), jnp.zeros_like(right_side[0]))
    ignored_end, (coupled_all, solved_all) = lax.scan(
        forward, initial, (lower, diagonal, upper, right_side)
    )

    def backward(following, row_blocks):
        coupled, solved = row_blocks
        current = solved - block_mul(coupled, following)
        return (current, current)

    ignored_start, result = lax.scan(
        backward, jnp.zeros_like(right_side[0]), (coupled_all, solved_all), reverse=True
    )
    return result


def stack_blocks(entries):
    stacked = jnp.stack([jnp.stack([e for e in r], 0) for r in entries], 0)
    return jnp.moveaxis(stacked, 2, 0)


def assemble(center, neighbours, fixed_charge):
    potential, concentration, permittivity = center
    blank_entry = jnp.zeros_like(potential)
    charge = fixed_charge
    for k in range(3):
        charge = charge + VALENCE[k] * concentration[k]
    residual = [-charge, blank_entry, blank_entry, blank_entry]
    jacobian = [[blank_entry] * 4 for i in range(4)]
    lower = [[blank_entry] * 4 for i in range(4)]
    upper = [[blank_entry] * 4 for i in range(4)]
    for k in range(3):
        jacobian[0][k + 1] = blank_entry - VALENCE[k]
    for nearby, inside, weight, position in neighbours:
        near_potential, near_conc, near_perm = nearby
        harmonic = 2.0 * permittivity * near_perm / (permittivity + near_perm)
        face_perm = weight * (inside * harmonic + (1.0 - inside) * permittivity)
        residual[0] = residual[0] + face_perm * (potential - near_potential)
        jacobian[0][0] = jacobian[0][0] + face_perm
        offdiag = lower if position == "lower" else upper if position == "upper" else None
        if offdiag is not None:
            offdiag[0][0] = -inside * face_perm
        for k in range(3):
            drift = VALENCE[k] * (near_potential - potential)
            face_coef = inside * weight * MOBILITY[k]
            weight_out = bernoulli(drift)
            weight_in = bernoulli(-drift)
            mean_conc = 0.5 * (concentration[k] + near_conc[k])
            residual[k + 1] = residual[k + 1] + face_coef * (
                weight_out * concentration[k] - weight_in * near_conc[k]
            )
            jacobian[k + 1][k + 1] = jacobian[k + 1][k + 1] + face_coef * weight_out
            jacobian[k + 1][0] = jacobian[k + 1][0] + face_coef * VALENCE[k] * mean_conc
            if offdiag is not None:
                offdiag[k + 1][k + 1] = -face_coef * weight_in
                offdiag[k + 1][0] = -face_coef * VALENCE[k] * mean_conc
    residual_all = jnp.moveaxis(jnp.stack([e for e in residual], 0), 1, 0)
    return (residual_all, stack_blocks(jacobian), stack_blocks(lower), stack_blocks(upper))


def split_fields(block):
    return (block[0], block[1:4], block[4])


def partition_forward(previous_vec, previous_map, first_tip, last_tip):
    identity = jnp.eye(4, dtype=first_tip.dtype).reshape((4, 4) + (1,) * (first_tip.ndim - 2))
    start_vec = first_tip[:, 0:1]
    start_left = first_tip[:, 1:5]
    start_right = first_tip[:, 5:9]
    end_vec = last_tip[:, 0:1]
    end_left = last_tip[:, 1:5]
    end_right = last_tip[:, 5:9]
    schur_block = identity - block_mul(start_left, previous_map)
    inverse = invert_small(schur_block)
    offset = block_mul(inverse, start_vec + block_mul(start_left, previous_vec))
    reach_map = block_mul(inverse, start_right)
    next_vec = end_vec + block_mul(end_left, previous_vec + block_mul(previous_map, offset))
    next_map = block_mul(end_left, block_mul(previous_map, reach_map)) + end_right
    return (next_vec, next_map, offset, reach_map)


def reduced_sweep(every_tip, zero_vec, zero_map):

    def sweep_forward(carried, tip_pair):
        previous_vec, previous_map = carried
        next_vec, next_map, offset, reach_map = partition_forward(
            previous_vec, previous_map, tip_pair[0], tip_pair[1]
        )
        return ((next_vec, next_map), (previous_vec, previous_map, offset, reach_map))

    ignored_e, (vec_all, map_all, offset_all, reach_all) = lax.scan(
        sweep_forward, (zero_vec, zero_map), every_tip
    )

    def sweep_backward(right_value, pieces):
        offset, reach_map = pieces
        return (offset + block_mul(reach_map, right_value), right_value)

    ignored_f, right_all = lax.scan(sweep_backward, zero_vec, (offset_all, reach_all), reverse=True)
    return (vec_all, map_all, offset_all, reach_all, right_all)


def on_device(potential, concentration, permittivity, fixed_charge):
    cells_wall = potential.shape[0]
    stacked = jnp.concatenate([potential[None], concentration, permittivity[None]], 0)
    walled = with_halo(stacked, (("wall", 1),), 1, False)
    planed = with_halo(stacked, (("stream", 3), ("span", 2)), 1, True)
    center = split_fields(stacked)
    wall_index = lax.axis_index("wall")
    global_row = wall_index * cells_wall + jnp.arange(cells_wall, dtype=jnp.int32)
    line_length = lax.axis_size("wall") * cells_wall
    inside_lower = (global_row > 0).astype(jnp.float32)[:, None, None]
    inside_upper = (global_row < line_length - 1).astype(jnp.float32)[:, None, None]
    neighbours = [
        (split_fields(walled[:, :-2]), inside_lower, 1.0, "lower"),
        (split_fields(walled[:, 2:]), inside_upper, 1.0, "upper"),
        (split_fields(planed[:, :, :-2, 1:-1]), 1.0, PLANE_WEIGHT, "plane"),
        (split_fields(planed[:, :, 2:, 1:-1]), 1.0, PLANE_WEIGHT, "plane"),
        (split_fields(planed[:, :, 1:-1, :-2]), 1.0, PLANE_WEIGHT, "plane"),
        (split_fields(planed[:, :, 1:-1, 2:]), 1.0, PLANE_WEIGHT, "plane"),
    ]
    residual, diagonal, lower, upper = assemble(center, neighbours, fixed_charge)
    row_ids = jnp.arange(cells_wall, dtype=jnp.int32)
    first_mask = (row_ids == 0).astype(jnp.float32)[:, None, None, None, None]
    last_mask = (row_ids == cells_wall - 1).astype(jnp.float32)[:, None, None, None, None]
    right_side = jnp.concatenate(
        [-residual[:, :, None], -lower * first_mask, -upper * last_mask], 2
    )
    solved = block_thomas(lower, diagonal, upper, right_side)
    first_tip = solved[0]
    last_tip = solved[-1]
    lines_shape = first_tip.shape[2:]
    zero_vec = jnp.zeros((4, 1) + lines_shape, jnp.float32)
    zero_map = jnp.zeros((4, 4) + lines_shape, jnp.float32)
    line_tips = jnp.stack([first_tip, last_tip], 0)[None]
    every_tip = lax.all_gather(line_tips, "wall", axis=0, tiled=True)
    vec_all, map_all, offset_all, reach_all, right_all = reduced_sweep(
        every_tip, zero_vec, zero_map
    )

    def choose_own(stacked_all):
        return lax.dynamic_index_in_dim(stacked_all, wall_index, 0, False)

    previous_vec = choose_own(vec_all)
    previous_map = choose_own(map_all)
    offset = choose_own(offset_all)
    reach_map = choose_own(reach_all)
    right_value = choose_own(right_all)
    local_first = offset + block_mul(reach_map, right_value)
    left_value = previous_vec + block_mul(previous_map, local_first)
    update = solved[:, :, 0]
    update = update + jnp.sum(solved[:, :, 1:5] * left_value[None, None, :, 0], axis=2)
    update = update + jnp.sum(solved[:, :, 5:9] * right_value[None, None, :, 0], axis=2)
    return jnp.moveaxis(update, 1, 0)


def on_any(potential, concentration, permittivity, fixed_charge):
    rows, planes, cols = potential.shape
    pair = (
        lax.axis_size("wall") == 2
        and lax.axis_size("span") % 2 == 0
        and lax.axis_size("stream") % 2 == 0
        and cols == LANES
        and rows % SUB == 0
        and planes % SUB == 0
        and rows * planes // SUB * 2 <= LANES
    )
    chosen = on_device_pair if pair else on_device
    return chosen(potential, concentration, permittivity, fixed_charge)


def solution(mesh):
    return jax.shard_map(
        on_any,
        mesh=mesh,
        in_specs=(
            P("wall", "span", "stream"),
            P(None, "wall", "span", "stream"),
            P("wall", "span", "stream"),
            P("wall", "span", "stream"),
        ),
        out_specs=P(None, "wall", "span", "stream"),
        check_vma=False,
    )
```

```python
import functools

import jax
import jax.numpy as jnp
from jax import lax
from jax.experimental import pallas as pl
from jax.experimental.pallas import tpu as pltpu
from jax.sharding import PartitionSpec as P

VALENCE = (1.0, -1.0, 2.0)
MOBILITY = (1.0, 1.5, 0.7)
HALF_ZD = tuple(0.5 * z * d for z, d in zip(VALENCE, MOBILITY))
PLANE_WEIGHT = 0.01
LANES = 128
SUB = 8
NQ = 11
ASSEMBLE_GROUP = 8
OUT_ROWS = 8

VMEM = pl.BlockSpec(memory_space=pltpu.VMEM)


def sds(*shape):
    return jax.ShapeDtypeStruct(shape, jnp.float32)


def params(mib=8):
    return pltpu.CompilerParams(vmem_limit_bytes=mib * 1024 * 1024)


def unrolled(start, stop, step, carry, group):
    full = (stop - start) // group if stop - start > group else 0

    def body(j, carry):
        for u in range(group):
            carry = step(start + group * j + u, carry)
        return carry

    if full:
        carry = lax.fori_loop(0, full, body, carry)
    for i in range(start + group * full, stop):
        carry = step(i, carry)
    return carry


def face(phi, eps, conc, phi_m, eps_m, conc_m, weight):
    x = phi_m - phi
    y = 0.5 * x
    y = jnp.where(y == 0.0, 1e-20, y)
    t = jnp.tanh(y)
    h = y * pl.reciprocal(t, approx=True)
    e = (eps * eps_m) * pl.reciprocal(eps + eps_m, approx=True)
    if weight is None:
        e = e + e
        h2 = h + y * t
        xw, yw, hw = x, y, h
    else:
        e = e * (weight + weight)
        hw = h * weight
        yw = y * weight
        xw = yw + yw
        h2 = hw + yw * t
    p1 = hw - yw
    m1 = hw + yw
    out = (p1, 1.5 * m1, 0.7 * (h2 - xw))
    into = (m1, 1.5 * p1, 0.7 * (h2 + xw))
    g = e * x
    flux = tuple(out[k] * conc[k] - into[k] * conc_m[k] for k in range(3))
    return e, g, out, into, flux


class Signed:
    def __init__(self, value, sign=1):
        self.value, self.sign = value, sign

    def __neg__(self):
        return Signed(self.value, -self.sign)

    def __add__(self, other):
        if self.value is None:
            return other
        if other.value is None:
            return self
        if self.sign == other.sign:
            return Signed(self.value + other.value, self.sign)
        if self.sign > 0:
            return Signed(self.value - other.value)
        return Signed(other.value - self.value)

    def __sub__(self, other):
        return self + (-other)

    def __mul__(self, other):
        if self.value is None or other.value is None:
            return Signed(None)
        return Signed(self.value * other.value, self.sign * other.sign)

    def inverse(self):
        return Signed(pl.reciprocal(self.value, approx=True), self.sign)

    def array(self, like, sign=1):
        if self.value is None:
            return jnp.zeros_like(like)
        return self.value if self.sign == sign else -self.value


def signed(values):
    return [Signed(v) for v in values]


T_SIGN = ((1, 1, -1, -1), (1, 1, -1, -1), (1, -1, 1, -1), (1, -1, -1, 1))


def inv2(a, b, c, d):
    r = (a * d - b * c).inverse()
    return ((d * r, -(b * r)), (-(c * r), a * r))


def mul2(P, Q):
    return [[P[i][0] * Q[0][j] + P[i][1] * Q[1][j] for j in range(2)] for i in range(2)]


def factor4(D):
    two = range(2)
    A = inv2(D[0][0], D[0][1], D[1][0], D[1][1])
    B = [[D[i][2 + j] for j in two] for i in two]
    E = mul2([[D[2 + i][j] for j in two] for i in two], A)
    EB = mul2(E, B)
    S = [[D[2 + i][2 + j] - EB[i][j] for j in two] for i in two]
    I = inv2(S[0][0], S[0][1], S[1][0], S[1][1])
    return A, E, I, mul2(A, B)


def apply4(factors, w):
    A, E, I, F = factors
    two = range(2)
    t = [w[2 + i] - (E[i][0] * w[0] + E[i][1] * w[1]) for i in two]
    low = [I[i][0] * t[0] + I[i][1] * t[1] for i in two]
    high = [
        (A[i][0] * w[0] + A[i][1] * w[1]) - (F[i][0] * low[0] + F[i][1] * low[1]) for i in two
    ]
    return high + low


def mat_vec(G, v):
    return [(G[i][0] * v[0] + G[i][1] * v[1]) + (G[i][2] * v[2] + G[i][3] * v[3]) for i in range(4)]


def couple(D, r, e, m, f, T, s):
    Dn = [[D[0][j] - e * T[0][j] for j in range(4)]]
    rn = [r[0] + e * s[0]]
    for k in range(3):
        Dn.append([D[k + 1][j] - (m[k] * T[0][j] + f[k] * T[k + 1][j]) for j in range(4)])
        rn.append(r[k + 1] + (m[k] * s[0] + f[k] * s[k + 1]))
    return Dn, rn


def solve_block(D, r, e, m, f):
    factors = factor4(D)
    columns = [apply4(factors, [e] + list(m))]
    for k in range(3):
        w = [Signed(None)] * 4
        w[k + 1] = f[k]
        columns.append(apply4(factors, w))
    return [[columns[b][a] for b in range(4)] for a in range(4)], apply4(factors, r)


def pack_kernel(
    rows, planes, phi_hbm, conc_hbm, eps_hbm, charge_hbm,
    phi_ref, conc_ref, eps_ref, charge_ref, near_ref, far_ref, sems,
):
    fields = [
        (phi_hbm, phi_ref),
        *((conc_hbm.at[k], conc_ref.at[k]) for k in range(3)),
        (eps_hbm, eps_ref),
        (charge_hbm, charge_ref),
    ]
    copies = [pltpu.make_async_copy(*pair, sems.at[i]) for i, pair in enumerate(fields)]
    for copy in copies:
        copy.start()
    odd = lax.axis_index("span") % 2 > 0
    for f in range(5):
        copies[f].wait()
        ref = fields[f][1]
        low = ref[pl.ds(0, rows, stride=planes), :]
        high = ref[pl.ds(planes - 1, rows, stride=planes), :]
        near_ref[f] = jnp.where(odd, high, low)
        far_ref[f] = jnp.where(odd, low, high)
    copies[5].wait()


def columns_kernel(rows, planes, phi_ref, conc_ref, eps_ref, cols_ref, wide_ref):
    parts = planes // SUB
    pair_of_lane = lax.broadcasted_iota(jnp.int32, (SUB, LANES), 1) // 2
    for f, ref in enumerate([phi_ref, *(conc_ref.at[k] for k in range(3)), eps_ref]):
        packed = jnp.zeros((SUB, LANES), jnp.float32)
        for j in range(rows * planes // SUB):
            tile = ref[SUB * j : SUB * (j + 1), :]
            wide_ref[f, pl.ds(j // parts * (planes + 1) + SUB * (j % parts), SUB), :] = tile
            moved = pltpu.roll(tile, 2 * j + 1, 1)
            packed = jnp.where(pair_of_lane == j, moved, packed)
        cols_ref[f] = packed


def assemble_kernel(
    rows, planes, phi_ref, conc_ref, eps_ref, charge_ref, wide_ref,
    acc_ref, fe_ref, fu_ref, span_ref,
):
    wall = lax.axis_index("wall")
    first_wall = (wall == 0).astype(jnp.float32)
    last_wall = 1.0 - first_wall

    def cell(p, row0):
        at = pl.ds(row0 * (planes + 1) + p, SUB, stride=planes + 1)
        return wide_ref[0, at, :], wide_ref[4, at, :], [wide_ref[1 + k, at, :] for k in range(3)]

    for row0 in range(0, rows, SUB):
        zero = jnp.zeros((SUB, LANES), jnp.float32)
        carry = [zero] * NQ
        phi, eps, conc = cell(0, row0)
        for p in range(planes):
            total = list(carry)
            if p + 1 < planes:
                phi_m, eps_m, conc_m = cell(p + 1, row0)
                e, g, out, into, flux = face(phi, eps, conc, phi_m, eps_m, conc_m, PLANE_WEIGHT)
                mine = [e, g, *out, *flux, *conc_m]
                total = [a + b for a, b in zip(total, mine)]
                carry = [e, -g, *into, *[-v for v in flux], *conc]
                phi, eps, conc = phi_m, eps_m, conc_m
            for q in range(NQ):
                span_ref[q, p * (rows + 1) + row0 : p * (rows + 1) + row0 + SUB, :] = total[q]

    def row_pass(part):
        lane = lax.broadcasted_iota(jnp.int32, (SUB, LANES), 1)
        weight = jnp.where(lane < LANES - 1, PLANE_WEIGHT, 0.0).astype(jnp.float32)

        def tile(r):
            return pl.ds(pl.multiple_of(r * planes + SUB * part, SUB), SUB)

        def load(r):
            at = tile(r)
            return phi_ref[at, :], eps_ref[at, :], [conc_ref[k, at, :] for k in range(3)]

        def finish(r, phi, eps, conc, lower, upper):
            at = tile(r)

            def fwd(v):
                return pltpu.roll(v, LANES - 1, 1)

            def back(v):
                return pltpu.roll(v, 1, 1)

            conc_m = [fwd(c) for c in conc]
            e, g, out, into, flux = face(phi, eps, conc, fwd(phi), fwd(eps), conc_m, weight)
            span = [span_ref[q, pl.ds(r + (rows + 1) * SUB * part, SUB, stride=rows + 1), :] for q in range(NQ)]
            total_e = (e + back(e)) + (lower[0] + upper[0]) + span[0]
            total_g = (g - back(g)) + (lower[1] + upper[1]) + span[1]
            charge = charge_ref[at, :] + conc[0] - conc[1] + 2.0 * conc[2]
            acc_ref[0, at, :] = total_e
            acc_ref[1, at, :] = total_g + charge
            for k in range(3):
                acc_ref[2 + k, at, :] = (out[k] + back(into[k])) + (lower[2][k] + upper[2][k]) + span[2 + k]
                acc_ref[5 + k, at, :] = -(
                    (flux[k] - back(flux[k])) + (lower[3][k] + upper[3][k]) + span[5 + k]
                )
                near = conc_m[k] + back(conc[k]) + span[8 + k] + 4.0 * conc[k]
                acc_ref[8 + k, at, :] = (HALF_ZD[k] * PLANE_WEIGHT) * near + HALF_ZD[k] * (
                    lower[4][k] + upper[4][k]
                )

        zero = jnp.zeros((SUB, LANES), jnp.float32)
        zeros = [zero] * 3

        phi, eps, conc = load(0)
        e = first_wall * eps
        lower = (e, -e * phi, zeros, zeros, zeros)

        def step(r, carry):
            phi, eps, conc, lower = carry
            phi_m, eps_m, conc_m = load(r + 1)
            e, g, out, into, flux = face(phi, eps, conc, phi_m, eps_m, conc_m, None)
            at = tile(r)
            fe_ref[at, :] = e
            for k in range(3):
                fu_ref[wall, k, at, :] = into[k]
                fu_ref[1 - wall, k, at, :] = out[k]
            both = [conc[k] + conc_m[k] for k in range(3)]
            upper = (e, g, out, flux, both)
            finish(r, phi, eps, conc, lower, upper)
            lower = (e, -g, list(into), [-v for v in flux], both)
            return phi_m, eps_m, conc_m, lower

        phi, eps, conc, lower = unrolled(0, rows - 1, step, (phi, eps, conc, lower), ASSEMBLE_GROUP)
        e = last_wall * eps
        upper = (e, -e * phi, zeros, zeros, zeros)
        finish(rows - 1, phi, eps, conc, lower, upper)

    for part in range(planes // SUB):
        row_pass(part)


def halo_terms(own, near, wrapped):
    e, g, out, _, flux = face(own[0], own[4], own[1:4], near[0], near[4], near[1:4], PLANE_WEIGHT)
    c = [near[1 + k] if wrapped is None else near[1 + k] - wrapped[1 + k] for k in range(3)]
    return [e, g, *out, *[-v for v in flux], *[(HALF_ZD[k] * PLANE_WEIGHT) * c[k] for k in range(3)]]


def first_eliminate_kernel(
    rows, planes, phi_ref, conc_ref, eps_ref, acc_ref, fe_ref, fu_ref,
    near_ref, far_ref, near_halo_ref, far_halo_ref, cols_ref, even_halo_ref, odd_halo_ref,
    t_ref, s_ref, tip_ref, side_ref, rim_ref,
):
    span_odd = lax.axis_index("span") % 2
    stream_odd = lax.axis_index("stream") % 2 > 0

    for own_ref, halo_ref, side in (
        (near_ref, near_halo_ref, span_odd),
        (far_ref, far_halo_ref, 1 - span_odd),
    ):
        own = [own_ref[f] for f in range(5)]
        near = [halo_ref[f] for f in range(5)]
        for q, v in enumerate(halo_terms(own, near, None)):
            rim_ref[q, side] = v

    odd = lax.broadcasted_iota(jnp.int32, (SUB, LANES), 1) % 2 == 1
    own, near, wrapped = [], [], []
    for f in range(5):
        mine, a, b = cols_ref[f], even_halo_ref[f], odd_halo_ref[f]
        right = jnp.where(stream_odd, b, a)
        left = jnp.where(stream_odd, a, b)
        own.append(mine)
        near.append(jnp.where(odd, pltpu.roll(left, 1, 1), pltpu.roll(right, LANES - 1, 1)))
        wrapped.append(jnp.where(odd, pltpu.roll(mine, 1, 1), pltpu.roll(mine, LANES - 1, 1)))
    for q, v in enumerate(halo_terms(own, near, wrapped)):
        side_ref[q] = v

    last = pl.multiple_of(jnp.where(lax.axis_index("wall") == 0, rows - 1, 0) * planes, planes)
    for part in range(planes // SUB):
        at = pl.ds(last + SUB * part, SUB)
        tip_ref[20 + 5 * part] = phi_ref[at, :]
        for k in range(3):
            tip_ref[21 + 5 * part + k] = conc_ref[k, at, :]
        tip_ref[24 + 5 * part] = eps_ref[at, :]

    eliminate_kernel(
        rows, planes, 0, conc_ref, acc_ref, fe_ref, fu_ref, side_ref, rim_ref,
        t_ref, s_ref, tip_ref,
    )


def eliminate_kernel(
    rows, planes, part, conc_ref, acc_ref, fe_ref, fu_ref, side_ref, rim_ref,
    t_ref, s_ref, tip_ref,
):
    wall = lax.axis_index("wall")
    lane = lax.broadcasted_iota(jnp.int32, (SUB, LANES), 1)
    edge = (lane == 0) | (lane == LANES - 1)
    plane = lax.broadcasted_iota(jnp.int32, (SUB, LANES), 0) + SUB * part
    rims = [side for side, p in enumerate((0, planes - 1)) if p // SUB == part]
    on_rim = {side: plane == (planes - 1) * side for side in rims}

    def place(i):
        return jnp.where(wall == 0, i, rows - 1 - i)

    def tile(r):
        return pl.ds(pl.multiple_of(r * planes + SUB * part, SUB), SUB)

    def own_block(i):
        r = place(i)
        at = tile(r)
        q_all = []
        for q in range(NQ):
            moved = pltpu.roll(side_ref[q], LANES - 1 - 2 * ((planes // SUB) * r + part), 1)
            total = acc_ref[q, at, :] + jnp.where(edge, moved, 0.0)
            for side in rims:
                rim = jnp.broadcast_to(rim_ref[q, side, pl.ds(r, 1), :], (SUB, LANES))
                total = total + jnp.where(on_rim[side], rim, 0.0)
            q_all.append(total)
        a, d, b = q_all[0], q_all[2:5], q_all[8:11]
        one = jnp.ones_like(a)
        zero = Signed(None)
        b, d = signed(b), signed(d)
        D = [
            [Signed(a), Signed(one, -1), Signed(one), Signed(2.0 * one, -1)],
            [b[0], d[0], zero, zero],
            [b[1], zero, d[1], zero],
            [b[2], zero, zero, d[2]],
        ]
        return at, D, signed([q_all[1], *q_all[5:8]])

    def next_face(i):
        r = place(i)
        r_next = place(i + 1)
        at, at_next, at_face = tile(r), tile(r_next), tile(jnp.minimum(r, r_next))
        m = [HALF_ZD[k] * (conc_ref[k, at, :] + conc_ref[k, at_next, :]) for k in range(3)]
        up = [fu_ref[0, k, at_face, :] for k in range(3)]
        low = [fu_ref[1, k, at_face, :] for k in range(3)]
        return Signed(fe_ref[at_face, :]), signed(m), signed(up), signed(low)

    def reduce_row(i, carry):
        at, D, r = own_block(i)
        if carry is not None:
            T, s, e, m, low = carry
            D, r = couple(D, r, e, m, low, T, s)
        return at, D, r

    def step(i, carry):
        at, D, r = reduce_row(i, carry)
        e, m, up, low = next_face(i)
        T, s = solve_block(D, r, e, m, up)
        like = e.value
        keep = pl.ds(pl.multiple_of(place(i) * SUB, SUB), SUB)
        for a in range(4):
            for b in range(4):
                t_ref[4 * a + b, keep, :] = T[a][b].array(like, T_SIGN[a][b])
            s_ref[a, keep, :] = s[a].array(like)
        return T, s, e, m, low

    carry = step(0, None)
    for i in range(1, rows - 1):
        carry = step(i, carry)
    at, D, r = reduce_row(rows - 1, carry)
    for a in range(4):
        for b in range(4):
            tip_ref[4 * a + b] = D[a][b].array(fe_ref[at, :])
        tip_ref[16 + a] = r[a].array(fe_ref[at, :])


def tip_block(ref, fields_ref, part):
    D = [signed(ref[4 * a + b] for b in range(4)) for a in range(4)]
    r = signed(ref[16 + a] for a in range(4))
    f = [fields_ref[20 + 5 * part + q] for q in range(5)]
    return D, r, f[0], f[1:4], f[4]


def with_face(D, r, e, g, m, out, flux):
    D = [list(row) for row in D]
    r = list(r)
    D[0][0] = D[0][0] + e
    r[0] = r[0] + g
    for k in range(3):
        D[k + 1][k + 1] = D[k + 1][k + 1] + out[k]
        D[k + 1][0] = D[k + 1][0] + m[k]
        r[k + 1] = r[k + 1] - flux[k]
    return D, r


def substitute_kernel(
    rows, part, own_ref, near_ref, own_first_ref, near_first_ref, t_ref, s_ref, out_ref,
    after=None,
):
    wall = lax.axis_index("wall")
    D, r, phi, conc, eps = tip_block(own_ref, own_first_ref, part)
    Dm, rm, phi_m, conc_m, eps_m = tip_block(near_ref, near_first_ref, part)
    e, g, out, into, flux = face(phi, eps, conc, phi_m, eps_m, conc_m, None)
    e, g = Signed(e), Signed(g)
    out, into, flux = signed(out), signed(into), signed(flux)
    m = [Signed(HALF_ZD[k] * (conc[k] + conc_m[k])) for k in range(3)]
    Dm, rm = with_face(Dm, rm, e, -g, m, into, [-v for v in flux])
    T, s = solve_block(Dm, rm, e, m, out)
    D, r = with_face(D, r, e, g, m, out, flux)
    D, r = couple(D, r, e, m, into, T, s)
    x = apply4(factor4(D), r)

    def put(i, x):
        at = kept_tile(rows, wall, i)
        for a in range(4):
            out_ref[a, at, :] = x[a].array(phi)

    put(rows - 1, x)
    for i in range(rows - 2, -1, -1):
        T, s = kept_block(t_ref, s_ref, kept_tile(rows, wall, i))
        x = [v + w for v, w in zip(mat_vec(T, x), s)]
        put(i, x)
        if after is not None and i % OUT_ROWS == 0:
            after(i)


def kept_tile(rows, wall, i):
    return pl.ds(pl.multiple_of(jnp.where(wall == 0, i, rows - 1 - i) * SUB, SUB), SUB)


def kept_block(t_ref, s_ref, at):
    T = [[Signed(t_ref[4 * a + b, at, :], T_SIGN[a][b]) for b in range(4)] for a in range(4)]
    return T, signed(s_ref[a, at, :] for a in range(4))


def write_kernel(
    rows, planes, part, own_ref, near_ref, own_first_ref, near_first_ref, t_ref, s_ref, *refs
):
    out_hbm, mine_ref, sems = refs[-3:]
    wall = lax.axis_index("wall")
    mine = mine_ref.reshape(4, rows, SUB, LANES)
    copies = []

    def after(i):
        first = jnp.where(wall == 0, i, rows - OUT_ROWS - i)
        at = pl.ds(first, OUT_ROWS)
        copies.append(
            pltpu.make_async_copy(
                mine.at[:, at], out_hbm.at[:, at, pl.ds(SUB * part, SUB), :], sems.at[len(copies)]
            )
        )
        copies[-1].start()

    substitute_kernel(
        rows, part, own_ref, near_ref, own_first_ref, near_first_ref, t_ref, s_ref, mine_ref, after
    )
    for copy in copies:
        copy.wait()


def swap_pairs(count, first):
    pairs = []
    for i in range(first, count + first, 2):
        a, b = i % count, (i + 1) % count
        pairs += [(a, b), (b, a)]
    return pairs


def on_device_pair(potential, concentration, permittivity, fixed_charge):
    rows, planes, cols = potential.shape
    cells = rows * planes
    phi = potential.reshape(cells, cols)
    conc = concentration.reshape(3, cells, cols)
    eps = permittivity.reshape(cells, cols)
    charge = fixed_charge.reshape(cells, cols)
    n_span, n_stream = lax.axis_size("span"), lax.axis_size("stream")

    phi, conc, eps, charge, near, far = pl.pallas_call(
        functools.partial(pack_kernel, rows, planes),
        name="pack",
        out_shape=(
            sds(cells, cols), sds(3, cells, cols), sds(cells, cols), sds(cells, cols),
            sds(5, rows, cols), sds(5, rows, cols),
        ),
        in_specs=[pl.BlockSpec(memory_space=pltpu.HBM)] * 4,
        out_specs=(VMEM,) * 6,
        scratch_shapes=[pltpu.SemaphoreType.DMA((6,))],
        compiler_params=params(),
    )(*(pltpu.with_memory_space_constraint(v, pltpu.HBM) for v in (phi, conc, eps, charge)))

    near_halo = lax.ppermute(near, "span", swap_pairs(n_span, 1))
    far_halo = lax.ppermute(far, "span", swap_pairs(n_span, 0))
    edge_cols, wide = pl.pallas_call(
        functools.partial(columns_kernel, rows, planes),
        name="columns",
        out_shape=(sds(5, SUB, LANES), sds(5, rows * (planes + 1), cols)),
        in_specs=[VMEM] * 3,
        out_specs=(VMEM,) * 2,
        compiler_params=params(),
    )(phi, conc, eps)
    odd_halo = lax.ppermute(edge_cols, "stream", swap_pairs(n_stream, 1))
    even_halo = lax.ppermute(edge_cols, "stream", swap_pairs(n_stream, 0))

    acc, fe, fu = pl.pallas_call(
        functools.partial(assemble_kernel, rows, planes),
        name="assemble",
        out_shape=(sds(NQ, cells, cols), sds(cells, cols), sds(2, 3, cells, cols)),
        in_specs=[VMEM] * 5,
        out_specs=(VMEM,) * 3,
        scratch_shapes=[pltpu.VMEM((NQ, cells + planes, cols), jnp.float32)],
        compiler_params=params(),
        cost_estimate=pl.CostEstimate(flops=12_000_000, bytes_accessed=6_000_000, transcendentals=0),
    )(phi, conc, eps, charge, wide)

    parts = planes // SUB
    across = [(0, 1), (1, 0)]
    kept = (sds(16, rows * SUB, cols), sds(4, rows * SUB, cols))
    terms = (sds(NQ, SUB, LANES), sds(NQ, 2, rows, LANES))
    T, s, tip, side, rim = pl.pallas_call(
        functools.partial(first_eliminate_kernel, rows, planes),
        name="eliminate",
        out_shape=(*kept, sds(20 + 5 * parts, SUB, cols), *terms),
        in_specs=[VMEM] * 13,
        out_specs=(VMEM,) * 5,
        compiler_params=params(),
    )(
        phi, conc, eps, acc, fe, fu, near, far, near_halo, far_halo, edge_cols,
        even_halo, odd_halo,
    )
    solved = [(tip, lax.ppermute(tip, "wall", across), T, s)]
    for part in range(1, parts):
        T, s, tip = pl.pallas_call(
            functools.partial(eliminate_kernel, rows, planes, part),
            name="eliminate",
            out_shape=(*kept, sds(20, SUB, cols)),
            in_specs=[VMEM] * 6,
            out_specs=(VMEM,) * 3,
            compiler_params=params(),
        )(conc, acc, fe, fu, side, rim)
        solved.append((tip, lax.ppermute(tip, "wall", across), T, s))

    fields = solved[0][:2]
    update = ()
    hbm = pl.BlockSpec(memory_space=pltpu.HBM)
    for part, (tip, tip_m, T, s) in enumerate(solved):
        update = pl.pallas_call(
            functools.partial(write_kernel, rows, planes, part),
            name="substitute",
            out_shape=(sds(4, rows, planes, cols),),
            in_specs=[VMEM] * 6 + [hbm] * len(update),
            out_specs=(hbm,),
            scratch_shapes=[
                pltpu.VMEM((4, rows * SUB, cols), jnp.float32),
                pltpu.SemaphoreType.DMA((rows // OUT_ROWS,)),
            ],
            input_output_aliases={6: 0} if update else {},
            compiler_params=params(),
        )(tip, tip_m, *fields, T, s, *update)
    return update[0]


def with_halo(block, sides, width, periodic):
    for axis, dim in sides:
        count = lax.axis_size(axis)
        forward = [(i, i + 1) for i in range(count - 1)]
        if periodic:
            forward.append((count - 1, 0))
        backward = [(target, source) for source, target in forward]
        low = lax.ppermute(
            lax.slice_in_dim(block, block.shape[dim] - width, None, axis=dim), axis, forward
        )
        high = lax.ppermute(lax.slice_in_dim(block, 0, width, axis=dim), axis, backward)
        block = jnp.concatenate([low, block, high], axis=dim)
    return block


def bernoulli(values):
    near_zero = jnp.abs(values) < 0.001
    safe_values = jnp.where(near_zero, 1.0, values)
    series = 1.0 - 0.5 * values + values * values / 12.0
    return jnp.where(near_zero, series, safe_values / jnp.expm1(safe_values))


def block_mul(left_block, right_block):
    return jnp.sum(left_block[:, :, None] * right_block[None, :, :], axis=1)


def invert_small(matrix):
    order_size = matrix.shape[0]
    left_rows = [[matrix[i, j] for j in range(order_size)] for i in range(order_size)]
    blank_entry = jnp.zeros_like(matrix[0, 0])
    right_rows = [
        [blank_entry + (1.0 if i == j else 0.0) for j in range(order_size)]
        for i in range(order_size)
    ]
    for k in range(order_size):
        pivot_inv = 1.0 / left_rows[k][k]
        left_rows[k] = [v * pivot_inv for v in left_rows[k]]
        right_rows[k] = [v * pivot_inv for v in right_rows[k]]
        for i in range(order_size):
            if i != k:
                factor = left_rows[i][k]
                left_rows[i] = [a - factor * b for a, b in zip(left_rows[i], left_rows[k])]
                right_rows[i] = [a - factor * b for a, b in zip(right_rows[i], right_rows[k])]
    return jnp.stack([jnp.stack(r, 0) for r in right_rows], 0)


def block_thomas(lower, diagonal, upper, right_side):

    def forward(carried, row_blocks):
        coupled_prev, solved_prev = carried
        lower_row, diag_row, upper_row, side_row = row_blocks
        reduced = diag_row - block_mul(lower_row, coupled_prev)
        inverse = invert_small(reduced)
        coupled = block_mul(inverse, upper_row)
        solved = block_mul(inverse, side_row - block_mul(lower_row, solved_prev))
        return ((coupled, solved), (coupled, solved))

    initial = (jnp.zeros_like(diagonal[0]), jnp.zeros_like(right_side[0]))
    ignored_end, (coupled_all, solved_all) = lax.scan(
        forward, initial, (lower, diagonal, upper, right_side)
    )

    def backward(following, row_blocks):
        coupled, solved = row_blocks
        current = solved - block_mul(coupled, following)
        return (current, current)

    ignored_start, result = lax.scan(
        backward, jnp.zeros_like(right_side[0]), (coupled_all, solved_all), reverse=True
    )
    return result


def stack_blocks(entries):
    stacked = jnp.stack([jnp.stack([e for e in r], 0) for r in entries], 0)
    return jnp.moveaxis(stacked, 2, 0)


def assemble(center, neighbours, fixed_charge):
    potential, concentration, permittivity = center
    blank_entry = jnp.zeros_like(potential)
    charge = fixed_charge
    for k in range(3):
        charge = charge + VALENCE[k] * concentration[k]
    residual = [-charge, blank_entry, blank_entry, blank_entry]
    jacobian = [[blank_entry] * 4 for i in range(4)]
    lower = [[blank_entry] * 4 for i in range(4)]
    upper = [[blank_entry] * 4 for i in range(4)]
    for k in range(3):
        jacobian[0][k + 1] = blank_entry - VALENCE[k]
    for nearby, inside, weight, position in neighbours:
        near_potential, near_conc, near_perm = nearby
        harmonic = 2.0 * permittivity * near_perm / (permittivity + near_perm)
        face_perm = weight * (inside * harmonic + (1.0 - inside) * permittivity)
        residual[0] = residual[0] + face_perm * (potential - near_potential)
        jacobian[0][0] = jacobian[0][0] + face_perm
        offdiag = lower if position == "lower" else upper if position == "upper" else None
        if offdiag is not None:
            offdiag[0][0] = -inside * face_perm
        for k in range(3):
            drift = VALENCE[k] * (near_potential - potential)
            face_coef = inside * weight * MOBILITY[k]
            weight_out = bernoulli(drift)
            weight_in = bernoulli(-drift)
            mean_conc = 0.5 * (concentration[k] + near_conc[k])
            residual[k + 1] = residual[k + 1] + face_coef * (
                weight_out * concentration[k] - weight_in * near_conc[k]
            )
            jacobian[k + 1][k + 1] = jacobian[k + 1][k + 1] + face_coef * weight_out
            jacobian[k + 1][0] = jacobian[k + 1][0] + face_coef * VALENCE[k] * mean_conc
            if offdiag is not None:
                offdiag[k + 1][k + 1] = -face_coef * weight_in
                offdiag[k + 1][0] = -face_coef * VALENCE[k] * mean_conc
    residual_all = jnp.moveaxis(jnp.stack([e for e in residual], 0), 1, 0)
    return (residual_all, stack_blocks(jacobian), stack_blocks(lower), stack_blocks(upper))


def split_fields(block):
    return (block[0], block[1:4], block[4])


def partition_forward(previous_vec, previous_map, first_tip, last_tip):
    identity = jnp.eye(4, dtype=first_tip.dtype).reshape((4, 4) + (1,) * (first_tip.ndim - 2))
    start_vec = first_tip[:, 0:1]
    start_left = first_tip[:, 1:5]
    start_right = first_tip[:, 5:9]
    end_vec = last_tip[:, 0:1]
    end_left = last_tip[:, 1:5]
    end_right = last_tip[:, 5:9]
    schur_block = identity - block_mul(start_left, previous_map)
    inverse = invert_small(schur_block)
    offset = block_mul(inverse, start_vec + block_mul(start_left, previous_vec))
    reach_map = block_mul(inverse, start_right)
    next_vec = end_vec + block_mul(end_left, previous_vec + block_mul(previous_map, offset))
    next_map = block_mul(end_left, block_mul(previous_map, reach_map)) + end_right
    return (next_vec, next_map, offset, reach_map)


def reduced_sweep(every_tip, zero_vec, zero_map):

    def sweep_forward(carried, tip_pair):
        previous_vec, previous_map = carried
        next_vec, next_map, offset, reach_map = partition_forward(
            previous_vec, previous_map, tip_pair[0], tip_pair[1]
        )
        return ((next_vec, next_map), (previous_vec, previous_map, offset, reach_map))

    ignored_e, (vec_all, map_all, offset_all, reach_all) = lax.scan(
        sweep_forward, (zero_vec, zero_map), every_tip
    )

    def sweep_backward(right_value, pieces):
        offset, reach_map = pieces
        return (offset + block_mul(reach_map, right_value), right_value)

    ignored_f, right_all = lax.scan(sweep_backward, zero_vec, (offset_all, reach_all), reverse=True)
    return (vec_all, map_all, offset_all, reach_all, right_all)


def on_device(potential, concentration, permittivity, fixed_charge):
    cells_wall = potential.shape[0]
    stacked = jnp.concatenate([potential[None], concentration, permittivity[None]], 0)
    walled = with_halo(stacked, (("wall", 1),), 1, False)
    planed = with_halo(stacked, (("stream", 3), ("span", 2)), 1, True)
    center = split_fields(stacked)
    wall_index = lax.axis_index("wall")
    global_row = wall_index * cells_wall + jnp.arange(cells_wall, dtype=jnp.int32)
    line_length = lax.axis_size("wall") * cells_wall
    inside_lower = (global_row > 0).astype(jnp.float32)[:, None, None]
    inside_upper = (global_row < line_length - 1).astype(jnp.float32)[:, None, None]
    neighbours = [
        (split_fields(walled[:, :-2]), inside_lower, 1.0, "lower"),
        (split_fields(walled[:, 2:]), inside_upper, 1.0, "upper"),
        (split_fields(planed[:, :, :-2, 1:-1]), 1.0, PLANE_WEIGHT, "plane"),
        (split_fields(planed[:, :, 2:, 1:-1]), 1.0, PLANE_WEIGHT, "plane"),
        (split_fields(planed[:, :, 1:-1, :-2]), 1.0, PLANE_WEIGHT, "plane"),
        (split_fields(planed[:, :, 1:-1, 2:]), 1.0, PLANE_WEIGHT, "plane"),
    ]
    residual, diagonal, lower, upper = assemble(center, neighbours, fixed_charge)
    row_ids = jnp.arange(cells_wall, dtype=jnp.int32)
    first_mask = (row_ids == 0).astype(jnp.float32)[:, None, None, None, None]
    last_mask = (row_ids == cells_wall - 1).astype(jnp.float32)[:, None, None, None, None]
    right_side = jnp.concatenate(
        [-residual[:, :, None], -lower * first_mask, -upper * last_mask], 2
    )
    solved = block_thomas(lower, diagonal, upper, right_side)
    first_tip = solved[0]
    last_tip = solved[-1]
    lines_shape = first_tip.shape[2:]
    zero_vec = jnp.zeros((4, 1) + lines_shape, jnp.float32)
    zero_map = jnp.zeros((4, 4) + lines_shape, jnp.float32)
    line_tips = jnp.stack([first_tip, last_tip], 0)[None]
    every_tip = lax.all_gather(line_tips, "wall", axis=0, tiled=True)
    vec_all, map_all, offset_all, reach_all, right_all = reduced_sweep(
        every_tip, zero_vec, zero_map
    )

    def choose_own(stacked_all):
        return lax.dynamic_index_in_dim(stacked_all, wall_index, 0, False)

    previous_vec = choose_own(vec_all)
    previous_map = choose_own(map_all)
    offset = choose_own(offset_all)
    reach_map = choose_own(reach_all)
    right_value = choose_own(right_all)
    local_first = offset + block_mul(reach_map, right_value)
    left_value = previous_vec + block_mul(previous_map, local_first)
    update = solved[:, :, 0]
    update = update + jnp.sum(solved[:, :, 1:5] * left_value[None, None, :, 0], axis=2)
    update = update + jnp.sum(solved[:, :, 5:9] * right_value[None, None, :, 0], axis=2)
    return jnp.moveaxis(update, 1, 0)


def on_any(potential, concentration, permittivity, fixed_charge):
    rows, planes, cols = potential.shape
    pair = (
        lax.axis_size("wall") == 2
        and lax.axis_size("span") % 2 == 0
        and lax.axis_size("stream") % 2 == 0
        and cols == LANES
        and rows % SUB == 0
        and planes % SUB == 0
        and rows * planes // SUB * 2 <= LANES
    )
    chosen = on_device_pair if pair else on_device
    return chosen(potential, concentration, permittivity, fixed_charge)


def solution(mesh):
    return jax.shard_map(
        on_any,
        mesh=mesh,
        in_specs=(
            P("wall", "span", "stream"),
            P(None, "wall", "span", "stream"),
            P("wall", "span", "stream"),
            P("wall", "span", "stream"),
        ),
        out_specs=P(None, "wall", "span", "stream"),
        check_vma=False,
    )
```

```python
import functools

import jax
import jax.numpy as jnp
from jax import lax
from jax.experimental import pallas as pl
from jax.experimental.pallas import tpu as pltpu
from jax.sharding import PartitionSpec as P

VALENCE = (1.0, -1.0, 2.0)
MOBILITY = (1.0, 1.5, 0.7)
HALF_ZD = tuple(0.5 * z * d for z, d in zip(VALENCE, MOBILITY))
PLANE_WEIGHT = 0.01
LANES = 128
SUB = 8
NQ = 11
ASSEMBLE_GROUP = 9
OUT_ROWS = 8

VMEM = pl.BlockSpec(memory_space=pltpu.VMEM)


def sds(*shape):
    return jax.ShapeDtypeStruct(shape, jnp.float32)


def params(mib=8):
    return pltpu.CompilerParams(vmem_limit_bytes=mib * 1024 * 1024)


def unrolled(start, stop, step, carry, group):
    full = (stop - start) // group if stop - start > group else 0

    def body(j, carry):
        for u in range(group):
            carry = step(start + group * j + u, carry)
        return carry

    if full:
        carry = lax.fori_loop(0, full, body, carry)
    for i in range(start + group * full, stop):
        carry = step(i, carry)
    return carry


def face(phi, eps, conc, phi_m, eps_m, conc_m, weight):
    x = phi_m - phi
    y = 0.5 * x
    y = jnp.where(y == 0.0, 1e-20, y)
    t = jnp.tanh(y)
    h = y * pl.reciprocal(t, approx=True)
    e = (eps * eps_m) * pl.reciprocal(eps + eps_m, approx=True)
    if weight is None:
        e = e + e
        h2 = h + y * t
        xw, yw, hw = x, y, h
    else:
        e = e * (weight + weight)
        hw = h * weight
        yw = y * weight
        xw = yw + yw
        h2 = hw + yw * t
    p1 = hw - yw
    m1 = hw + yw
    out = (p1, 1.5 * m1, 0.7 * (h2 - xw))
    into = (m1, 1.5 * p1, 0.7 * (h2 + xw))
    g = e * x
    flux = tuple(out[k] * conc[k] - into[k] * conc_m[k] for k in range(3))
    return e, g, out, into, flux


class Signed:
    def __init__(self, value, sign=1):
        self.value, self.sign = value, sign

    def __neg__(self):
        return Signed(self.value, -self.sign)

    def __add__(self, other):
        if self.value is None:
            return other
        if other.value is None:
            return self
        if self.sign == other.sign:
            return Signed(self.value + other.value, self.sign)
        if self.sign > 0:
            return Signed(self.value - other.value)
        return Signed(other.value - self.value)

    def __sub__(self, other):
        return self + (-other)

    def __mul__(self, other):
        if self.value is None or other.value is None:
            return Signed(None)
        return Signed(self.value * other.value, self.sign * other.sign)

    def inverse(self):
        return Signed(pl.reciprocal(self.value, approx=True), self.sign)

    def array(self, like, sign=1):
        if self.value is None:
            return jnp.zeros_like(like)
        return self.value if self.sign == sign else -self.value


def signed(values):
    return [Signed(v) for v in values]


T_SIGN = ((1, 1, -1, -1), (1, 1, -1, -1), (1, -1, 1, -1), (1, -1, -1, 1))


def inv2(a, b, c, d):
    r = (a * d - b * c).inverse()
    return ((d * r, -(b * r)), (-(c * r), a * r))


def mul2(P, Q):
    return [[P[i][0] * Q[0][j] + P[i][1] * Q[1][j] for j in range(2)] for i in range(2)]


def factor4(D):
    two = range(2)
    A = inv2(D[0][0], D[0][1], D[1][0], D[1][1])
    B = [[D[i][2 + j] for j in two] for i in two]
    E = mul2([[D[2 + i][j] for j in two] for i in two], A)
    EB = mul2(E, B)
    S = [[D[2 + i][2 + j] - EB[i][j] for j in two] for i in two]
    I = inv2(S[0][0], S[0][1], S[1][0], S[1][1])
    return A, E, I, mul2(A, B)


def apply4(factors, w):
    A, E, I, F = factors
    two = range(2)
    t = [w[2 + i] - (E[i][0] * w[0] + E[i][1] * w[1]) for i in two]
    low = [I[i][0] * t[0] + I[i][1] * t[1] for i in two]
    high = [
        (A[i][0] * w[0] + A[i][1] * w[1]) - (F[i][0] * low[0] + F[i][1] * low[1]) for i in two
    ]
    return high + low


def mat_vec(G, v):
    return [(G[i][0] * v[0] + G[i][1] * v[1]) + (G[i][2] * v[2] + G[i][3] * v[3]) for i in range(4)]


def couple(D, r, e, m, f, T, s):
    Dn = [[D[0][j] - e * T[0][j] for j in range(4)]]
    rn = [r[0] + e * s[0]]
    for k in range(3):
        Dn.append([D[k + 1][j] - (m[k] * T[0][j] + f[k] * T[k + 1][j]) for j in range(4)])
        rn.append(r[k + 1] + (m[k] * s[0] + f[k] * s[k + 1]))
    return Dn, rn


def solve_block(D, r, e, m, f):
    factors = factor4(D)
    columns = [apply4(factors, [e] + list(m))]
    for k in range(3):
        w = [Signed(None)] * 4
        w[k + 1] = f[k]
        columns.append(apply4(factors, w))
    return [[columns[b][a] for b in range(4)] for a in range(4)], apply4(factors, r)


def pack_kernel(
    rows, planes, phi_hbm, conc_hbm, eps_hbm, charge_hbm,
    phi_ref, conc_ref, eps_ref, charge_ref, near_ref, far_ref, sems,
):
    fields = [
        (phi_hbm, phi_ref),
        *((conc_hbm.at[k], conc_ref.at[k]) for k in range(3)),
        (eps_hbm, eps_ref),
        (charge_hbm, charge_ref),
    ]
    copies = [pltpu.make_async_copy(*pair, sems.at[i]) for i, pair in enumerate(fields)]
    for copy in copies:
        copy.start()
    odd = lax.axis_index("span") % 2 > 0
    for f in range(5):
        copies[f].wait()
        ref = fields[f][1]
        low = ref[pl.ds(0, rows, stride=planes), :]
        high = ref[pl.ds(planes - 1, rows, stride=planes), :]
        near_ref[f] = jnp.where(odd, high, low)
        far_ref[f] = jnp.where(odd, low, high)
    copies[5].wait()


def columns_kernel(rows, planes, phi_ref, conc_ref, eps_ref, cols_ref, wide_ref):
    parts = planes // SUB
    pair_of_lane = lax.broadcasted_iota(jnp.int32, (SUB, LANES), 1) // 2
    for f, ref in enumerate([phi_ref, *(conc_ref.at[k] for k in range(3)), eps_ref]):
        packed = jnp.zeros((SUB, LANES), jnp.float32)
        for j in range(rows * planes // SUB):
            tile = ref[SUB * j : SUB * (j + 1), :]
            wide_ref[f, pl.ds(j // parts * (planes + 1) + SUB * (j % parts), SUB), :] = tile
            moved = pltpu.roll(tile, 2 * j + 1, 1)
            packed = jnp.where(pair_of_lane == j, moved, packed)
        cols_ref[f] = packed


def assemble_kernel(
    rows, planes, phi_ref, conc_ref, eps_ref, charge_ref, wide_ref,
    acc_ref, fe_ref, fu_ref, span_ref,
):
    wall = lax.axis_index("wall")
    first_wall = (wall == 0).astype(jnp.float32)
    last_wall = 1.0 - first_wall

    def cell(p, row0):
        at = pl.ds(row0 * (planes + 1) + p, SUB, stride=planes + 1)
        return wide_ref[0, at, :], wide_ref[4, at, :], [wide_ref[1 + k, at, :] for k in range(3)]

    for row0 in range(0, rows, SUB):
        zero = jnp.zeros((SUB, LANES), jnp.float32)
        carry = [zero] * NQ
        phi, eps, conc = cell(0, row0)
        for p in range(planes):
            total = list(carry)
            if p + 1 < planes:
                phi_m, eps_m, conc_m = cell(p + 1, row0)
                e, g, out, into, flux = face(phi, eps, conc, phi_m, eps_m, conc_m, PLANE_WEIGHT)
                mine = [e, g, *out, *flux, *conc_m]
                total = [a + b for a, b in zip(total, mine)]
                carry = [e, -g, *into, *[-v for v in flux], *conc]
                phi, eps, conc = phi_m, eps_m, conc_m
            for q in range(NQ):
                span_ref[q, p * (rows + 1) + row0 : p * (rows + 1) + row0 + SUB, :] = total[q]

    def row_pass(part):
        lane = lax.broadcasted_iota(jnp.int32, (SUB, LANES), 1)
        weight = jnp.where(lane < LANES - 1, PLANE_WEIGHT, 0.0).astype(jnp.float32)

        def tile(r):
            return pl.ds(pl.multiple_of(r * planes + SUB * part, SUB), SUB)

        def load(r):
            at = tile(r)
            return phi_ref[at, :], eps_ref[at, :], [conc_ref[k, at, :] for k in range(3)]

        def finish(r, phi, eps, conc, lower, upper):
            at = tile(r)

            def fwd(v):
                return pltpu.roll(v, LANES - 1, 1)

            def back(v):
                return pltpu.roll(v, 1, 1)

            conc_m = [fwd(c) for c in conc]
            e, g, out, into, flux = face(phi, eps, conc, fwd(phi), fwd(eps), conc_m, weight)
            span = [span_ref[q, pl.ds(r + (rows + 1) * SUB * part, SUB, stride=rows + 1), :] for q in range(NQ)]
            total_e = (e + back(e)) + (lower[0] + upper[0]) + span[0]
            total_g = (g - back(g)) + (lower[1] + upper[1]) + span[1]
            charge = charge_ref[at, :] + conc[0] - conc[1] + 2.0 * conc[2]
            acc_ref[0, at, :] = total_e
            acc_ref[1, at, :] = total_g + charge
            for k in range(3):
                acc_ref[2 + k, at, :] = (out[k] + back(into[k])) + (lower[2][k] + upper[2][k]) + span[2 + k]
                acc_ref[5 + k, at, :] = -(
                    (flux[k] - back(flux[k])) + (lower[3][k] + upper[3][k]) + span[5 + k]
                )
                near = conc_m[k] + back(conc[k]) + span[8 + k] + 4.0 * conc[k]
                acc_ref[8 + k, at, :] = (HALF_ZD[k] * PLANE_WEIGHT) * near + HALF_ZD[k] * (
                    lower[4][k] + upper[4][k]
                )

        zero = jnp.zeros((SUB, LANES), jnp.float32)
        zeros = [zero] * 3

        phi, eps, conc = load(0)
        e = first_wall * eps
        lower = (e, -e * phi, zeros, zeros, zeros)

        def step(r, carry):
            phi, eps, conc, lower = carry
            phi_m, eps_m, conc_m = load(r + 1)
            e, g, out, into, flux = face(phi, eps, conc, phi_m, eps_m, conc_m, None)
            at = tile(r)
            fe_ref[at, :] = e
            for k in range(3):
                fu_ref[wall, k, at, :] = into[k]
                fu_ref[1 - wall, k, at, :] = out[k]
            both = [conc[k] + conc_m[k] for k in range(3)]
            upper = (e, g, out, flux, both)
            finish(r, phi, eps, conc, lower, upper)
            lower = (e, -g, list(into), [-v for v in flux], both)
            return phi_m, eps_m, conc_m, lower

        phi, eps, conc, lower = unrolled(0, rows - 1, step, (phi, eps, conc, lower), ASSEMBLE_GROUP)
        e = last_wall * eps
        upper = (e, -e * phi, zeros, zeros, zeros)
        finish(rows - 1, phi, eps, conc, lower, upper)

    for part in range(planes // SUB):
        row_pass(part)


def halo_terms(own, near, wrapped):
    e, g, out, _, flux = face(own[0], own[4], own[1:4], near[0], near[4], near[1:4], PLANE_WEIGHT)
    c = [near[1 + k] if wrapped is None else near[1 + k] - wrapped[1 + k] for k in range(3)]
    return [e, g, *out, *[-v for v in flux], *[(HALF_ZD[k] * PLANE_WEIGHT) * c[k] for k in range(3)]]


def first_eliminate_kernel(
    rows, planes, phi_ref, conc_ref, eps_ref, acc_ref, fe_ref, fu_ref,
    near_ref, far_ref, near_halo_ref, far_halo_ref, cols_ref, even_halo_ref, odd_halo_ref,
    t_ref, s_ref, tip_ref, side_ref, rim_ref,
):
    span_odd = lax.axis_index("span") % 2
    stream_odd = lax.axis_index("stream") % 2 > 0

    for own_ref, halo_ref, side in (
        (near_ref, near_halo_ref, span_odd),
        (far_ref, far_halo_ref, 1 - span_odd),
    ):
        own = [own_ref[f] for f in range(5)]
        near = [halo_ref[f] for f in range(5)]
        for q, v in enumerate(halo_terms(own, near, None)):
            rim_ref[q, side] = v

    odd = lax.broadcasted_iota(jnp.int32, (SUB, LANES), 1) % 2 == 1
    own, near, wrapped = [], [], []
    for f in range(5):
        mine, a, b = cols_ref[f], even_halo_ref[f], odd_halo_ref[f]
        right = jnp.where(stream_odd, b, a)
        left = jnp.where(stream_odd, a, b)
        own.append(mine)
        near.append(jnp.where(odd, pltpu.roll(left, 1, 1), pltpu.roll(right, LANES - 1, 1)))
        wrapped.append(jnp.where(odd, pltpu.roll(mine, 1, 1), pltpu.roll(mine, LANES - 1, 1)))
    for q, v in enumerate(halo_terms(own, near, wrapped)):
        side_ref[q] = v

    last = pl.multiple_of(jnp.where(lax.axis_index("wall") == 0, rows - 1, 0) * planes, planes)
    for part in range(planes // SUB):
        at = pl.ds(last + SUB * part, SUB)
        tip_ref[20 + 5 * part] = phi_ref[at, :]
        for k in range(3):
            tip_ref[21 + 5 * part + k] = conc_ref[k, at, :]
        tip_ref[24 + 5 * part] = eps_ref[at, :]

    eliminate_kernel(
        rows, planes, 0, conc_ref, acc_ref, fe_ref, fu_ref, side_ref, rim_ref,
        t_ref, s_ref, tip_ref,
    )


def eliminate_kernel(
    rows, planes, part, conc_ref, acc_ref, fe_ref, fu_ref, side_ref, rim_ref,
    t_ref, s_ref, tip_ref,
):
    wall = lax.axis_index("wall")
    lane = lax.broadcasted_iota(jnp.int32, (SUB, LANES), 1)
    edge = (lane == 0) | (lane == LANES - 1)
    plane = lax.broadcasted_iota(jnp.int32, (SUB, LANES), 0) + SUB * part
    rims = [side for side, p in enumerate((0, planes - 1)) if p // SUB == part]
    on_rim = {side: plane == (planes - 1) * side for side in rims}

    def place(i):
        return jnp.where(wall == 0, i, rows - 1 - i)

    def tile(r):
        return pl.ds(pl.multiple_of(r * planes + SUB * part, SUB), SUB)

    def own_block(i):
        r = place(i)
        at = tile(r)
        q_all = []
        for q in range(NQ):
            moved = pltpu.roll(side_ref[q], LANES - 1 - 2 * ((planes // SUB) * r + part), 1)
            total = acc_ref[q, at, :] + jnp.where(edge, moved, 0.0)
            for side in rims:
                rim = jnp.broadcast_to(rim_ref[q, side, pl.ds(r, 1), :], (SUB, LANES))
                total = total + jnp.where(on_rim[side], rim, 0.0)
            q_all.append(total)
        a, d, b = q_all[0], q_all[2:5], q_all[8:11]
        one = jnp.ones_like(a)
        zero = Signed(None)
        b, d = signed(b), signed(d)
        D = [
            [Signed(a), Signed(one, -1), Signed(one), Signed(2.0 * one, -1)],
            [b[0], d[0], zero, zero],
            [b[1], zero, d[1], zero],
            [b[2], zero, zero, d[2]],
        ]
        return at, D, signed([q_all[1], *q_all[5:8]])

    def next_face(i):
        r = place(i)
        r_next = place(i + 1)
        at, at_next, at_face = tile(r), tile(r_next), tile(jnp.minimum(r, r_next))
        m = [HALF_ZD[k] * (conc_ref[k, at, :] + conc_ref[k, at_next, :]) for k in range(3)]
        up = [fu_ref[0, k, at_face, :] for k in range(3)]
        low = [fu_ref[1, k, at_face, :] for k in range(3)]
        return Signed(fe_ref[at_face, :]), signed(m), signed(up), signed(low)

    def reduce_row(i, carry):
        at, D, r = own_block(i)
        if carry is not None:
            T, s, e, m, low = carry
            D, r = couple(D, r, e, m, low, T, s)
        return at, D, r

    def step(i, carry):
        at, D, r = reduce_row(i, carry)
        e, m, up, low = next_face(i)
        T, s = solve_block(D, r, e, m, up)
        like = e.value
        keep = pl.ds(pl.multiple_of(place(i) * SUB, SUB), SUB)
        for a in range(4):
            for b in range(4):
                t_ref[4 * a + b, keep, :] = T[a][b].array(like, T_SIGN[a][b])
            s_ref[a, keep, :] = s[a].array(like)
        return T, s, e, m, low

    carry = step(0, None)
    for i in range(1, rows - 1):
        carry = step(i, carry)
    at, D, r = reduce_row(rows - 1, carry)
    for a in range(4):
        for b in range(4):
            tip_ref[4 * a + b] = D[a][b].array(fe_ref[at, :])
        tip_ref[16 + a] = r[a].array(fe_ref[at, :])


def tip_block(ref, fields_ref, part):
    D = [signed(ref[4 * a + b] for b in range(4)) for a in range(4)]
    r = signed(ref[16 + a] for a in range(4))
    f = [fields_ref[20 + 5 * part + q] for q in range(5)]
    return D, r, f[0], f[1:4], f[4]


def with_face(D, r, e, g, m, out, flux):
    D = [list(row) for row in D]
    r = list(r)
    D[0][0] = D[0][0] + e
    r[0] = r[0] + g
    for k in range(3):
        D[k + 1][k + 1] = D[k + 1][k + 1] + out[k]
        D[k + 1][0] = D[k + 1][0] + m[k]
        r[k + 1] = r[k + 1] - flux[k]
    return D, r


def substitute_kernel(
    rows, part, own_ref, near_ref, own_first_ref, near_first_ref, t_ref, s_ref, out_ref,
    after=None,
):
    wall = lax.axis_index("wall")
    D, r, phi, conc, eps = tip_block(own_ref, own_first_ref, part)
    Dm, rm, phi_m, conc_m, eps_m = tip_block(near_ref, near_first_ref, part)
    e, g, out, into, flux = face(phi, eps, conc, phi_m, eps_m, conc_m, None)
    e, g = Signed(e), Signed(g)
    out, into, flux = signed(out), signed(into), signed(flux)
    m = [Signed(HALF_ZD[k] * (conc[k] + conc_m[k])) for k in range(3)]
    Dm, rm = with_face(Dm, rm, e, -g, m, into, [-v for v in flux])
    T, s = solve_block(Dm, rm, e, m, out)
    D, r = with_face(D, r, e, g, m, out, flux)
    D, r = couple(D, r, e, m, into, T, s)
    x = apply4(factor4(D), r)

    def put(i, x):
        at = kept_tile(rows, wall, i)
        for a in range(4):
            out_ref[a, at, :] = x[a].array(phi)

    put(rows - 1, x)
    for i in range(rows - 2, -1, -1):
        T, s = kept_block(t_ref, s_ref, kept_tile(rows, wall, i))
        x = [v + w for v, w in zip(mat_vec(T, x), s)]
        put(i, x)
        if after is not None and i % OUT_ROWS == 0:
            after(i)


def kept_tile(rows, wall, i):
    return pl.ds(pl.multiple_of(jnp.where(wall == 0, i, rows - 1 - i) * SUB, SUB), SUB)


def kept_block(t_ref, s_ref, at):
    T = [[Signed(t_ref[4 * a + b, at, :], T_SIGN[a][b]) for b in range(4)] for a in range(4)]
    return T, signed(s_ref[a, at, :] for a in range(4))


def write_kernel(
    rows, planes, part, own_ref, near_ref, own_first_ref, near_first_ref, t_ref, s_ref, *refs
):
    out_hbm, mine_ref, sems = refs[-3:]
    wall = lax.axis_index("wall")
    mine = mine_ref.reshape(4, rows, SUB, LANES)
    copies = []

    def after(i):
        first = jnp.where(wall == 0, i, rows - OUT_ROWS - i)
        at = pl.ds(first, OUT_ROWS)
        copies.append(
            pltpu.make_async_copy(
                mine.at[:, at], out_hbm.at[:, at, pl.ds(SUB * part, SUB), :], sems.at[len(copies)]
            )
        )
        copies[-1].start()

    substitute_kernel(
        rows, part, own_ref, near_ref, own_first_ref, near_first_ref, t_ref, s_ref, mine_ref, after
    )
    for copy in copies:
        copy.wait()


def swap_pairs(count, first):
    pairs = []
    for i in range(first, count + first, 2):
        a, b = i % count, (i + 1) % count
        pairs += [(a, b), (b, a)]
    return pairs


def on_device_pair(potential, concentration, permittivity, fixed_charge):
    rows, planes, cols = potential.shape
    cells = rows * planes
    phi = potential.reshape(cells, cols)
    conc = concentration.reshape(3, cells, cols)
    eps = permittivity.reshape(cells, cols)
    charge = fixed_charge.reshape(cells, cols)
    n_span, n_stream = lax.axis_size("span"), lax.axis_size("stream")

    phi, conc, eps, charge, near, far = pl.pallas_call(
        functools.partial(pack_kernel, rows, planes),
        name="pack",
        out_shape=(
            sds(cells, cols), sds(3, cells, cols), sds(cells, cols), sds(cells, cols),
            sds(5, rows, cols), sds(5, rows, cols),
        ),
        in_specs=[pl.BlockSpec(memory_space=pltpu.HBM)] * 4,
        out_specs=(VMEM,) * 6,
        scratch_shapes=[pltpu.SemaphoreType.DMA((6,))],
        compiler_params=params(),
    )(*(pltpu.with_memory_space_constraint(v, pltpu.HBM) for v in (phi, conc, eps, charge)))

    near_halo = lax.ppermute(near, "span", swap_pairs(n_span, 1))
    far_halo = lax.ppermute(far, "span", swap_pairs(n_span, 0))
    edge_cols, wide = pl.pallas_call(
        functools.partial(columns_kernel, rows, planes),
        name="columns",
        out_shape=(sds(5, SUB, LANES), sds(5, rows * (planes + 1), cols)),
        in_specs=[VMEM] * 3,
        out_specs=(VMEM,) * 2,
        compiler_params=params(),
    )(phi, conc, eps)
    odd_halo = lax.ppermute(edge_cols, "stream", swap_pairs(n_stream, 1))
    even_halo = lax.ppermute(edge_cols, "stream", swap_pairs(n_stream, 0))

    acc, fe, fu = pl.pallas_call(
        functools.partial(assemble_kernel, rows, planes),
        name="assemble",
        out_shape=(sds(NQ, cells, cols), sds(cells, cols), sds(2, 3, cells, cols)),
        in_specs=[VMEM] * 5,
        out_specs=(VMEM,) * 3,
        scratch_shapes=[pltpu.VMEM((NQ, cells + planes, cols), jnp.float32)],
        compiler_params=params(),
        cost_estimate=pl.CostEstimate(flops=12_000_000, bytes_accessed=6_000_000, transcendentals=0),
    )(phi, conc, eps, charge, wide)

    parts = planes // SUB
    across = [(0, 1), (1, 0)]
    kept = (sds(16, rows * SUB, cols), sds(4, rows * SUB, cols))
    terms = (sds(NQ, SUB, LANES), sds(NQ, 2, rows, LANES))
    T, s, tip, side, rim = pl.pallas_call(
        functools.partial(first_eliminate_kernel, rows, planes),
        name="eliminate",
        out_shape=(*kept, sds(20 + 5 * parts, SUB, cols), *terms),
        in_specs=[VMEM] * 13,
        out_specs=(VMEM,) * 5,
        compiler_params=params(),
    )(
        phi, conc, eps, acc, fe, fu, near, far, near_halo, far_halo, edge_cols,
        even_halo, odd_halo,
    )
    solved = [(tip, lax.ppermute(tip, "wall", across), T, s)]
    for part in range(1, parts):
        T, s, tip = pl.pallas_call(
            functools.partial(eliminate_kernel, rows, planes, part),
            name="eliminate",
            out_shape=(*kept, sds(20, SUB, cols)),
            in_specs=[VMEM] * 6,
            out_specs=(VMEM,) * 3,
            compiler_params=params(),
        )(conc, acc, fe, fu, side, rim)
        solved.append((tip, lax.ppermute(tip, "wall", across), T, s))

    fields = solved[0][:2]
    update = ()
    hbm = pl.BlockSpec(memory_space=pltpu.HBM)
    for part, (tip, tip_m, T, s) in enumerate(solved):
        update = pl.pallas_call(
            functools.partial(write_kernel, rows, planes, part),
            name="substitute",
            out_shape=(sds(4, rows, planes, cols),),
            in_specs=[VMEM] * 6 + [hbm] * len(update),
            out_specs=(hbm,),
            scratch_shapes=[
                pltpu.VMEM((4, rows * SUB, cols), jnp.float32),
                pltpu.SemaphoreType.DMA((rows // OUT_ROWS,)),
            ],
            input_output_aliases={6: 0} if update else {},
            compiler_params=params(),
        )(tip, tip_m, *fields, T, s, *update)
    return update[0]


def with_halo(block, sides, width, periodic):
    for axis, dim in sides:
        count = lax.axis_size(axis)
        forward = [(i, i + 1) for i in range(count - 1)]
        if periodic:
            forward.append((count - 1, 0))
        backward = [(target, source) for source, target in forward]
        low = lax.ppermute(
            lax.slice_in_dim(block, block.shape[dim] - width, None, axis=dim), axis, forward
        )
        high = lax.ppermute(lax.slice_in_dim(block, 0, width, axis=dim), axis, backward)
        block = jnp.concatenate([low, block, high], axis=dim)
    return block


def bernoulli(values):
    near_zero = jnp.abs(values) < 0.001
    safe_values = jnp.where(near_zero, 1.0, values)
    series = 1.0 - 0.5 * values + values * values / 12.0
    return jnp.where(near_zero, series, safe_values / jnp.expm1(safe_values))


def block_mul(left_block, right_block):
    return jnp.sum(left_block[:, :, None] * right_block[None, :, :], axis=1)


def invert_small(matrix):
    order_size = matrix.shape[0]
    left_rows = [[matrix[i, j] for j in range(order_size)] for i in range(order_size)]
    blank_entry = jnp.zeros_like(matrix[0, 0])
    right_rows = [
        [blank_entry + (1.0 if i == j else 0.0) for j in range(order_size)]
        for i in range(order_size)
    ]
    for k in range(order_size):
        pivot_inv = 1.0 / left_rows[k][k]
        left_rows[k] = [v * pivot_inv for v in left_rows[k]]
        right_rows[k] = [v * pivot_inv for v in right_rows[k]]
        for i in range(order_size):
            if i != k:
                factor = left_rows[i][k]
                left_rows[i] = [a - factor * b for a, b in zip(left_rows[i], left_rows[k])]
                right_rows[i] = [a - factor * b for a, b in zip(right_rows[i], right_rows[k])]
    return jnp.stack([jnp.stack(r, 0) for r in right_rows], 0)


def block_thomas(lower, diagonal, upper, right_side):

    def forward(carried, row_blocks):
        coupled_prev, solved_prev = carried
        lower_row, diag_row, upper_row, side_row = row_blocks
        reduced = diag_row - block_mul(lower_row, coupled_prev)
        inverse = invert_small(reduced)
        coupled = block_mul(inverse, upper_row)
        solved = block_mul(inverse, side_row - block_mul(lower_row, solved_prev))
        return ((coupled, solved), (coupled, solved))

    initial = (jnp.zeros_like(diagonal[0]), jnp.zeros_like(right_side[0]))
    ignored_end, (coupled_all, solved_all) = lax.scan(
        forward, initial, (lower, diagonal, upper, right_side)
    )

    def backward(following, row_blocks):
        coupled, solved = row_blocks
        current = solved - block_mul(coupled, following)
        return (current, current)

    ignored_start, result = lax.scan(
        backward, jnp.zeros_like(right_side[0]), (coupled_all, solved_all), reverse=True
    )
    return result


def stack_blocks(entries):
    stacked = jnp.stack([jnp.stack([e for e in r], 0) for r in entries], 0)
    return jnp.moveaxis(stacked, 2, 0)


def assemble(center, neighbours, fixed_charge):
    potential, concentration, permittivity = center
    blank_entry = jnp.zeros_like(potential)
    charge = fixed_charge
    for k in range(3):
        charge = charge + VALENCE[k] * concentration[k]
    residual = [-charge, blank_entry, blank_entry, blank_entry]
    jacobian = [[blank_entry] * 4 for i in range(4)]
    lower = [[blank_entry] * 4 for i in range(4)]
    upper = [[blank_entry] * 4 for i in range(4)]
    for k in range(3):
        jacobian[0][k + 1] = blank_entry - VALENCE[k]
    for nearby, inside, weight, position in neighbours:
        near_potential, near_conc, near_perm = nearby
        harmonic = 2.0 * permittivity * near_perm / (permittivity + near_perm)
        face_perm = weight * (inside * harmonic + (1.0 - inside) * permittivity)
        residual[0] = residual[0] + face_perm * (potential - near_potential)
        jacobian[0][0] = jacobian[0][0] + face_perm
        offdiag = lower if position == "lower" else upper if position == "upper" else None
        if offdiag is not None:
            offdiag[0][0] = -inside * face_perm
        for k in range(3):
            drift = VALENCE[k] * (near_potential - potential)
            face_coef = inside * weight * MOBILITY[k]
            weight_out = bernoulli(drift)
            weight_in = bernoulli(-drift)
            mean_conc = 0.5 * (concentration[k] + near_conc[k])
            residual[k + 1] = residual[k + 1] + face_coef * (
                weight_out * concentration[k] - weight_in * near_conc[k]
            )
            jacobian[k + 1][k + 1] = jacobian[k + 1][k + 1] + face_coef * weight_out
            jacobian[k + 1][0] = jacobian[k + 1][0] + face_coef * VALENCE[k] * mean_conc
            if offdiag is not None:
                offdiag[k + 1][k + 1] = -face_coef * weight_in
                offdiag[k + 1][0] = -face_coef * VALENCE[k] * mean_conc
    residual_all = jnp.moveaxis(jnp.stack([e for e in residual], 0), 1, 0)
    return (residual_all, stack_blocks(jacobian), stack_blocks(lower), stack_blocks(upper))


def split_fields(block):
    return (block[0], block[1:4], block[4])


def partition_forward(previous_vec, previous_map, first_tip, last_tip):
    identity = jnp.eye(4, dtype=first_tip.dtype).reshape((4, 4) + (1,) * (first_tip.ndim - 2))
    start_vec = first_tip[:, 0:1]
    start_left = first_tip[:, 1:5]
    start_right = first_tip[:, 5:9]
    end_vec = last_tip[:, 0:1]
    end_left = last_tip[:, 1:5]
    end_right = last_tip[:, 5:9]
    schur_block = identity - block_mul(start_left, previous_map)
    inverse = invert_small(schur_block)
    offset = block_mul(inverse, start_vec + block_mul(start_left, previous_vec))
    reach_map = block_mul(inverse, start_right)
    next_vec = end_vec + block_mul(end_left, previous_vec + block_mul(previous_map, offset))
    next_map = block_mul(end_left, block_mul(previous_map, reach_map)) + end_right
    return (next_vec, next_map, offset, reach_map)


def reduced_sweep(every_tip, zero_vec, zero_map):

    def sweep_forward(carried, tip_pair):
        previous_vec, previous_map = carried
        next_vec, next_map, offset, reach_map = partition_forward(
            previous_vec, previous_map, tip_pair[0], tip_pair[1]
        )
        return ((next_vec, next_map), (previous_vec, previous_map, offset, reach_map))

    ignored_e, (vec_all, map_all, offset_all, reach_all) = lax.scan(
        sweep_forward, (zero_vec, zero_map), every_tip
    )

    def sweep_backward(right_value, pieces):
        offset, reach_map = pieces
        return (offset + block_mul(reach_map, right_value), right_value)

    ignored_f, right_all = lax.scan(sweep_backward, zero_vec, (offset_all, reach_all), reverse=True)
    return (vec_all, map_all, offset_all, reach_all, right_all)


def on_device(potential, concentration, permittivity, fixed_charge):
    cells_wall = potential.shape[0]
    stacked = jnp.concatenate([potential[None], concentration, permittivity[None]], 0)
    walled = with_halo(stacked, (("wall", 1),), 1, False)
    planed = with_halo(stacked, (("stream", 3), ("span", 2)), 1, True)
    center = split_fields(stacked)
    wall_index = lax.axis_index("wall")
    global_row = wall_index * cells_wall + jnp.arange(cells_wall, dtype=jnp.int32)
    line_length = lax.axis_size("wall") * cells_wall
    inside_lower = (global_row > 0).astype(jnp.float32)[:, None, None]
    inside_upper = (global_row < line_length - 1).astype(jnp.float32)[:, None, None]
    neighbours = [
        (split_fields(walled[:, :-2]), inside_lower, 1.0, "lower"),
        (split_fields(walled[:, 2:]), inside_upper, 1.0, "upper"),
        (split_fields(planed[:, :, :-2, 1:-1]), 1.0, PLANE_WEIGHT, "plane"),
        (split_fields(planed[:, :, 2:, 1:-1]), 1.0, PLANE_WEIGHT, "plane"),
        (split_fields(planed[:, :, 1:-1, :-2]), 1.0, PLANE_WEIGHT, "plane"),
        (split_fields(planed[:, :, 1:-1, 2:]), 1.0, PLANE_WEIGHT, "plane"),
    ]
    residual, diagonal, lower, upper = assemble(center, neighbours, fixed_charge)
    row_ids = jnp.arange(cells_wall, dtype=jnp.int32)
    first_mask = (row_ids == 0).astype(jnp.float32)[:, None, None, None, None]
    last_mask = (row_ids == cells_wall - 1).astype(jnp.float32)[:, None, None, None, None]
    right_side = jnp.concatenate(
        [-residual[:, :, None], -lower * first_mask, -upper * last_mask], 2
    )
    solved = block_thomas(lower, diagonal, upper, right_side)
    first_tip = solved[0]
    last_tip = solved[-1]
    lines_shape = first_tip.shape[2:]
    zero_vec = jnp.zeros((4, 1) + lines_shape, jnp.float32)
    zero_map = jnp.zeros((4, 4) + lines_shape, jnp.float32)
    line_tips = jnp.stack([first_tip, last_tip], 0)[None]
    every_tip = lax.all_gather(line_tips, "wall", axis=0, tiled=True)
    vec_all, map_all, offset_all, reach_all, right_all = reduced_sweep(
        every_tip, zero_vec, zero_map
    )

    def choose_own(stacked_all):
        return lax.dynamic_index_in_dim(stacked_all, wall_index, 0, False)

    previous_vec = choose_own(vec_all)
    previous_map = choose_own(map_all)
    offset = choose_own(offset_all)
    reach_map = choose_own(reach_all)
    right_value = choose_own(right_all)
    local_first = offset + block_mul(reach_map, right_value)
    left_value = previous_vec + block_mul(previous_map, local_first)
    update = solved[:, :, 0]
    update = update + jnp.sum(solved[:, :, 1:5] * left_value[None, None, :, 0], axis=2)
    update = update + jnp.sum(solved[:, :, 5:9] * right_value[None, None, :, 0], axis=2)
    return jnp.moveaxis(update, 1, 0)


def on_any(potential, concentration, permittivity, fixed_charge):
    rows, planes, cols = potential.shape
    pair = (
        lax.axis_size("wall") == 2
        and lax.axis_size("span") % 2 == 0
        and lax.axis_size("stream") % 2 == 0
        and cols == LANES
        and rows % SUB == 0
        and planes % SUB == 0
        and rows * planes // SUB * 2 <= LANES
    )
    chosen = on_device_pair if pair else on_device
    return chosen(potential, concentration, permittivity, fixed_charge)


def solution(mesh):
    return jax.shard_map(
        on_any,
        mesh=mesh,
        in_specs=(
            P("wall", "span", "stream"),
            P(None, "wall", "span", "stream"),
            P("wall", "span", "stream"),
            P("wall", "span", "stream"),
        ),
        out_specs=P(None, "wall", "span", "stream"),
        check_vma=False,
    )
```

```python
import functools

import jax
import jax.numpy as jnp
from jax import lax
from jax.experimental import pallas as pl
from jax.experimental.pallas import tpu as pltpu
from jax.sharding import PartitionSpec as P

VALENCE = (1.0, -1.0, 2.0)
MOBILITY = (1.0, 1.5, 0.7)
HALF_ZD = tuple(0.5 * z * d for z, d in zip(VALENCE, MOBILITY))
PLANE_WEIGHT = 0.01
LANES = 128
SUB = 8
NQ = 11
ASSEMBLE_GROUP = 9
OUT_ROWS = 16

VMEM = pl.BlockSpec(memory_space=pltpu.VMEM)


def sds(*shape):
    return jax.ShapeDtypeStruct(shape, jnp.float32)


def params(mib=8):
    return pltpu.CompilerParams(vmem_limit_bytes=mib * 1024 * 1024)


def unrolled(start, stop, step, carry, group):
    full = (stop - start) // group if stop - start > group else 0

    def body(j, carry):
        for u in range(group):
            carry = step(start + group * j + u, carry)
        return carry

    if full:
        carry = lax.fori_loop(0, full, body, carry)
    for i in range(start + group * full, stop):
        carry = step(i, carry)
    return carry


def face(phi, eps, conc, phi_m, eps_m, conc_m, weight):
    x = phi_m - phi
    y = 0.5 * x
    y = jnp.where(y == 0.0, 1e-20, y)
    t = jnp.tanh(y)
    h = y * pl.reciprocal(t, approx=True)
    e = (eps * eps_m) * pl.reciprocal(eps + eps_m, approx=True)
    if weight is None:
        e = e + e
        h2 = h + y * t
        xw, yw, hw = x, y, h
    else:
        e = e * (weight + weight)
        hw = h * weight
        yw = y * weight
        xw = yw + yw
        h2 = hw + yw * t
    p1 = hw - yw
    m1 = hw + yw
    out = (p1, 1.5 * m1, 0.7 * (h2 - xw))
    into = (m1, 1.5 * p1, 0.7 * (h2 + xw))
    g = e * x
    flux = tuple(out[k] * conc[k] - into[k] * conc_m[k] for k in range(3))
    return e, g, out, into, flux


class Signed:
    def __init__(self, value, sign=1):
        self.value, self.sign = value, sign

    def __neg__(self):
        return Signed(self.value, -self.sign)

    def __add__(self, other):
        if self.value is None:
            return other
        if other.value is None:
            return self
        if self.sign == other.sign:
            return Signed(self.value + other.value, self.sign)
        if self.sign > 0:
            return Signed(self.value - other.value)
        return Signed(other.value - self.value)

    def __sub__(self, other):
        return self + (-other)

    def __mul__(self, other):
        if self.value is None or other.value is None:
            return Signed(None)
        return Signed(self.value * other.value, self.sign * other.sign)

    def inverse(self):
        return Signed(pl.reciprocal(self.value, approx=True), self.sign)

    def array(self, like, sign=1):
        if self.value is None:
            return jnp.zeros_like(like)
        return self.value if self.sign == sign else -self.value


def signed(values):
    return [Signed(v) for v in values]


T_SIGN = ((1, 1, -1, -1), (1, 1, -1, -1), (1, -1, 1, -1), (1, -1, -1, 1))


def inv2(a, b, c, d):
    r = (a * d - b * c).inverse()
    return ((d * r, -(b * r)), (-(c * r), a * r))


def mul2(P, Q):
    return [[P[i][0] * Q[0][j] + P[i][1] * Q[1][j] for j in range(2)] for i in range(2)]


def factor4(D):
    two = range(2)
    A = inv2(D[0][0], D[0][1], D[1][0], D[1][1])
    B = [[D[i][2 + j] for j in two] for i in two]
    E = mul2([[D[2 + i][j] for j in two] for i in two], A)
    EB = mul2(E, B)
    S = [[D[2 + i][2 + j] - EB[i][j] for j in two] for i in two]
    I = inv2(S[0][0], S[0][1], S[1][0], S[1][1])
    return A, E, I, mul2(A, B)


def apply4(factors, w):
    A, E, I, F = factors
    two = range(2)
    t = [w[2 + i] - (E[i][0] * w[0] + E[i][1] * w[1]) for i in two]
    low = [I[i][0] * t[0] + I[i][1] * t[1] for i in two]
    high = [
        (A[i][0] * w[0] + A[i][1] * w[1]) - (F[i][0] * low[0] + F[i][1] * low[1]) for i in two
    ]
    return high + low


def mat_vec(G, v):
    return [(G[i][0] * v[0] + G[i][1] * v[1]) + (G[i][2] * v[2] + G[i][3] * v[3]) for i in range(4)]


def couple(D, r, e, m, f, T, s):
    Dn = [[D[0][j] - e * T[0][j] for j in range(4)]]
    rn = [r[0] + e * s[0]]
    for k in range(3):
        Dn.append([D[k + 1][j] - (m[k] * T[0][j] + f[k] * T[k + 1][j]) for j in range(4)])
        rn.append(r[k + 1] + (m[k] * s[0] + f[k] * s[k + 1]))
    return Dn, rn


def solve_block(D, r, e, m, f):
    factors = factor4(D)
    columns = [apply4(factors, [e] + list(m))]
    for k in range(3):
        w = [Signed(None)] * 4
        w[k + 1] = f[k]
        columns.append(apply4(factors, w))
    return [[columns[b][a] for b in range(4)] for a in range(4)], apply4(factors, r)


def pack_kernel(
    rows, planes, phi_hbm, conc_hbm, eps_hbm, charge_hbm,
    phi_ref, conc_ref, eps_ref, charge_ref, near_ref, far_ref, sems,
):
    fields = [
        (phi_hbm, phi_ref),
        *((conc_hbm.at[k], conc_ref.at[k]) for k in range(3)),
        (eps_hbm, eps_ref),
        (charge_hbm, charge_ref),
    ]
    copies = [pltpu.make_async_copy(*pair, sems.at[i]) for i, pair in enumerate(fields)]
    for copy in copies:
        copy.start()
    odd = lax.axis_index("span") % 2 > 0
    for f in range(5):
        copies[f].wait()
        ref = fields[f][1]
        low = ref[pl.ds(0, rows, stride=planes), :]
        high = ref[pl.ds(planes - 1, rows, stride=planes), :]
        near_ref[f] = jnp.where(odd, high, low)
        far_ref[f] = jnp.where(odd, low, high)
    copies[5].wait()


def columns_kernel(rows, planes, phi_ref, conc_ref, eps_ref, cols_ref, wide_ref):
    parts = planes // SUB
    pair_of_lane = lax.broadcasted_iota(jnp.int32, (SUB, LANES), 1) // 2
    for f, ref in enumerate([phi_ref, *(conc_ref.at[k] for k in range(3)), eps_ref]):
        packed = jnp.zeros((SUB, LANES), jnp.float32)
        for j in range(rows * planes // SUB):
            tile = ref[SUB * j : SUB * (j + 1), :]
            wide_ref[f, pl.ds(j // parts * (planes + 1) + SUB * (j % parts), SUB), :] = tile
            moved = pltpu.roll(tile, 2 * j + 1, 1)
            packed = jnp.where(pair_of_lane == j, moved, packed)
        cols_ref[f] = packed


def assemble_kernel(
    rows, planes, phi_ref, conc_ref, eps_ref, charge_ref, wide_ref,
    acc_ref, fe_ref, fu_ref, span_ref,
):
    wall = lax.axis_index("wall")
    first_wall = (wall == 0).astype(jnp.float32)
    last_wall = 1.0 - first_wall

    def cell(p, row0):
        at = pl.ds(row0 * (planes + 1) + p, SUB, stride=planes + 1)
        return wide_ref[0, at, :], wide_ref[4, at, :], [wide_ref[1 + k, at, :] for k in range(3)]

    for row0 in range(0, rows, SUB):
        zero = jnp.zeros((SUB, LANES), jnp.float32)
        carry = [zero] * NQ
        phi, eps, conc = cell(0, row0)
        for p in range(planes):
            total = list(carry)
            if p + 1 < planes:
                phi_m, eps_m, conc_m = cell(p + 1, row0)
                e, g, out, into, flux = face(phi, eps, conc, phi_m, eps_m, conc_m, PLANE_WEIGHT)
                mine = [e, g, *out, *flux, *conc_m]
                total = [a + b for a, b in zip(total, mine)]
                carry = [e, -g, *into, *[-v for v in flux], *conc]
                phi, eps, conc = phi_m, eps_m, conc_m
            for q in range(NQ):
                span_ref[q, p * (rows + 1) + row0 : p * (rows + 1) + row0 + SUB, :] = total[q]

    def row_pass(part):
        lane = lax.broadcasted_iota(jnp.int32, (SUB, LANES), 1)
        weight = jnp.where(lane < LANES - 1, PLANE_WEIGHT, 0.0).astype(jnp.float32)

        def tile(r):
            return pl.ds(pl.multiple_of(r * planes + SUB * part, SUB), SUB)

        def load(r):
            at = tile(r)
            return phi_ref[at, :], eps_ref[at, :], [conc_ref[k, at, :] for k in range(3)]

        def finish(r, phi, eps, conc, lower, upper):
            at = tile(r)

            def fwd(v):
                return pltpu.roll(v, LANES - 1, 1)

            def back(v):
                return pltpu.roll(v, 1, 1)

            conc_m = [fwd(c) for c in conc]
            e, g, out, into, flux = face(phi, eps, conc, fwd(phi), fwd(eps), conc_m, weight)
            span = [span_ref[q, pl.ds(r + (rows + 1) * SUB * part, SUB, stride=rows + 1), :] for q in range(NQ)]
            total_e = (e + back(e)) + (lower[0] + upper[0]) + span[0]
            total_g = (g - back(g)) + (lower[1] + upper[1]) + span[1]
            charge = charge_ref[at, :] + conc[0] - conc[1] + 2.0 * conc[2]
            acc_ref[0, at, :] = total_e
            acc_ref[1, at, :] = total_g + charge
            for k in range(3):
                acc_ref[2 + k, at, :] = (out[k] + back(into[k])) + (lower[2][k] + upper[2][k]) + span[2 + k]
                acc_ref[5 + k, at, :] = -(
                    (flux[k] - back(flux[k])) + (lower[3][k] + upper[3][k]) + span[5 + k]
                )
                near = conc_m[k] + back(conc[k]) + span[8 + k] + 4.0 * conc[k]
                acc_ref[8 + k, at, :] = (HALF_ZD[k] * PLANE_WEIGHT) * near + HALF_ZD[k] * (
                    lower[4][k] + upper[4][k]
                )

        zero = jnp.zeros((SUB, LANES), jnp.float32)
        zeros = [zero] * 3

        phi, eps, conc = load(0)
        e = first_wall * eps
        lower = (e, -e * phi, zeros, zeros, zeros)

        def step(r, carry):
            phi, eps, conc, lower = carry
            phi_m, eps_m, conc_m = load(r + 1)
            e, g, out, into, flux = face(phi, eps, conc, phi_m, eps_m, conc_m, None)
            at = tile(r)
            fe_ref[at, :] = e
            for k in range(3):
                fu_ref[wall, k, at, :] = into[k]
                fu_ref[1 - wall, k, at, :] = out[k]
            both = [conc[k] + conc_m[k] for k in range(3)]
            upper = (e, g, out, flux, both)
            finish(r, phi, eps, conc, lower, upper)
            lower = (e, -g, list(into), [-v for v in flux], both)
            return phi_m, eps_m, conc_m, lower

        phi, eps, conc, lower = unrolled(0, rows - 1, step, (phi, eps, conc, lower), ASSEMBLE_GROUP)
        e = last_wall * eps
        upper = (e, -e * phi, zeros, zeros, zeros)
        finish(rows - 1, phi, eps, conc, lower, upper)

    for part in range(planes // SUB):
        row_pass(part)


def halo_terms(own, near, wrapped):
    e, g, out, _, flux = face(own[0], own[4], own[1:4], near[0], near[4], near[1:4], PLANE_WEIGHT)
    c = [near[1 + k] if wrapped is None else near[1 + k] - wrapped[1 + k] for k in range(3)]
    return [e, g, *out, *[-v for v in flux], *[(HALF_ZD[k] * PLANE_WEIGHT) * c[k] for k in range(3)]]


def first_eliminate_kernel(
    rows, planes, phi_ref, conc_ref, eps_ref, acc_ref, fe_ref, fu_ref,
    near_ref, far_ref, near_halo_ref, far_halo_ref, cols_ref, even_halo_ref, odd_halo_ref,
    t_ref, s_ref, tip_ref, side_ref, rim_ref,
):
    span_odd = lax.axis_index("span") % 2
    stream_odd = lax.axis_index("stream") % 2 > 0

    for own_ref, halo_ref, side in (
        (near_ref, near_halo_ref, span_odd),
        (far_ref, far_halo_ref, 1 - span_odd),
    ):
        own = [own_ref[f] for f in range(5)]
        near = [halo_ref[f] for f in range(5)]
        for q, v in enumerate(halo_terms(own, near, None)):
            rim_ref[q, side] = v

    odd = lax.broadcasted_iota(jnp.int32, (SUB, LANES), 1) % 2 == 1
    own, near, wrapped = [], [], []
    for f in range(5):
        mine, a, b = cols_ref[f], even_halo_ref[f], odd_halo_ref[f]
        right = jnp.where(stream_odd, b, a)
        left = jnp.where(stream_odd, a, b)
        own.append(mine)
        near.append(jnp.where(odd, pltpu.roll(left, 1, 1), pltpu.roll(right, LANES - 1, 1)))
        wrapped.append(jnp.where(odd, pltpu.roll(mine, 1, 1), pltpu.roll(mine, LANES - 1, 1)))
    for q, v in enumerate(halo_terms(own, near, wrapped)):
        side_ref[q] = v

    last = pl.multiple_of(jnp.where(lax.axis_index("wall") == 0, rows - 1, 0) * planes, planes)
    for part in range(planes // SUB):
        at = pl.ds(last + SUB * part, SUB)
        tip_ref[20 + 5 * part] = phi_ref[at, :]
        for k in range(3):
            tip_ref[21 + 5 * part + k] = conc_ref[k, at, :]
        tip_ref[24 + 5 * part] = eps_ref[at, :]

    eliminate_kernel(
        rows, planes, 0, conc_ref, acc_ref, fe_ref, fu_ref, side_ref, rim_ref,
        t_ref, s_ref, tip_ref,
    )


def eliminate_kernel(
    rows, planes, part, conc_ref, acc_ref, fe_ref, fu_ref, side_ref, rim_ref,
    t_ref, s_ref, tip_ref,
):
    wall = lax.axis_index("wall")
    lane = lax.broadcasted_iota(jnp.int32, (SUB, LANES), 1)
    edge = (lane == 0) | (lane == LANES - 1)
    plane = lax.broadcasted_iota(jnp.int32, (SUB, LANES), 0) + SUB * part
    rims = [side for side, p in enumerate((0, planes - 1)) if p // SUB == part]
    on_rim = {side: plane == (planes - 1) * side for side in rims}

    def place(i):
        return jnp.where(wall == 0, i, rows - 1 - i)

    def tile(r):
        return pl.ds(pl.multiple_of(r * planes + SUB * part, SUB), SUB)

    def own_block(i):
        r = place(i)
        at = tile(r)
        q_all = []
        for q in range(NQ):
            moved = pltpu.roll(side_ref[q], LANES - 1 - 2 * ((planes // SUB) * r + part), 1)
            total = acc_ref[q, at, :] + jnp.where(edge, moved, 0.0)
            for side in rims:
                rim = jnp.broadcast_to(rim_ref[q, side, pl.ds(r, 1), :], (SUB, LANES))
                total = total + jnp.where(on_rim[side], rim, 0.0)
            q_all.append(total)
        a, d, b = q_all[0], q_all[2:5], q_all[8:11]
        one = jnp.ones_like(a)
        zero = Signed(None)
        b, d = signed(b), signed(d)
        D = [
            [Signed(a), Signed(one, -1), Signed(one), Signed(2.0 * one, -1)],
            [b[0], d[0], zero, zero],
            [b[1], zero, d[1], zero],
            [b[2], zero, zero, d[2]],
        ]
        return at, D, signed([q_all[1], *q_all[5:8]])

    def next_face(i):
        r = place(i)
        r_next = place(i + 1)
        at, at_next, at_face = tile(r), tile(r_next), tile(jnp.minimum(r, r_next))
        m = [HALF_ZD[k] * (conc_ref[k, at, :] + conc_ref[k, at_next, :]) for k in range(3)]
        up = [fu_ref[0, k, at_face, :] for k in range(3)]
        low = [fu_ref[1, k, at_face, :] for k in range(3)]
        return Signed(fe_ref[at_face, :]), signed(m), signed(up), signed(low)

    def reduce_row(i, carry):
        at, D, r = own_block(i)
        if carry is not None:
            T, s, e, m, low = carry
            D, r = couple(D, r, e, m, low, T, s)
        return at, D, r

    def step(i, carry):
        at, D, r = reduce_row(i, carry)
        e, m, up, low = next_face(i)
        T, s = solve_block(D, r, e, m, up)
        like = e.value
        keep = pl.ds(pl.multiple_of(place(i) * SUB, SUB), SUB)
        for a in range(4):
            for b in range(4):
                t_ref[4 * a + b, keep, :] = T[a][b].array(like, T_SIGN[a][b])
            s_ref[a, keep, :] = s[a].array(like)
        return T, s, e, m, low

    carry = step(0, None)
    for i in range(1, rows - 1):
        carry = step(i, carry)
    at, D, r = reduce_row(rows - 1, carry)
    for a in range(4):
        for b in range(4):
            tip_ref[4 * a + b] = D[a][b].array(fe_ref[at, :])
        tip_ref[16 + a] = r[a].array(fe_ref[at, :])


def tip_block(ref, fields_ref, part):
    D = [signed(ref[4 * a + b] for b in range(4)) for a in range(4)]
    r = signed(ref[16 + a] for a in range(4))
    f = [fields_ref[20 + 5 * part + q] for q in range(5)]
    return D, r, f[0], f[1:4], f[4]


def with_face(D, r, e, g, m, out, flux):
    D = [list(row) for row in D]
    r = list(r)
    D[0][0] = D[0][0] + e
    r[0] = r[0] + g
    for k in range(3):
        D[k + 1][k + 1] = D[k + 1][k + 1] + out[k]
        D[k + 1][0] = D[k + 1][0] + m[k]
        r[k + 1] = r[k + 1] - flux[k]
    return D, r


def substitute_kernel(
    rows, part, own_ref, near_ref, own_first_ref, near_first_ref, t_ref, s_ref, out_ref,
    after=None,
):
    wall = lax.axis_index("wall")
    D, r, phi, conc, eps = tip_block(own_ref, own_first_ref, part)
    Dm, rm, phi_m, conc_m, eps_m = tip_block(near_ref, near_first_ref, part)
    e, g, out, into, flux = face(phi, eps, conc, phi_m, eps_m, conc_m, None)
    e, g = Signed(e), Signed(g)
    out, into, flux = signed(out), signed(into), signed(flux)
    m = [Signed(HALF_ZD[k] * (conc[k] + conc_m[k])) for k in range(3)]
    Dm, rm = with_face(Dm, rm, e, -g, m, into, [-v for v in flux])
    T, s = solve_block(Dm, rm, e, m, out)
    D, r = with_face(D, r, e, g, m, out, flux)
    D, r = couple(D, r, e, m, into, T, s)
    x = apply4(factor4(D), r)

    def put(i, x):
        at = kept_tile(rows, wall, i)
        for a in range(4):
            out_ref[a, at, :] = x[a].array(phi)

    put(rows - 1, x)
    for i in range(rows - 2, -1, -1):
        T, s = kept_block(t_ref, s_ref, kept_tile(rows, wall, i))
        x = [v + w for v, w in zip(mat_vec(T, x), s)]
        put(i, x)
        if after is not None and i % OUT_ROWS == 0:
            after(i)


def kept_tile(rows, wall, i):
    return pl.ds(pl.multiple_of(jnp.where(wall == 0, i, rows - 1 - i) * SUB, SUB), SUB)


def kept_block(t_ref, s_ref, at):
    T = [[Signed(t_ref[4 * a + b, at, :], T_SIGN[a][b]) for b in range(4)] for a in range(4)]
    return T, signed(s_ref[a, at, :] for a in range(4))


def write_kernel(
    rows, planes, part, own_ref, near_ref, own_first_ref, near_first_ref, t_ref, s_ref, *refs
):
    out_hbm, mine_ref, sems = refs[-3:]
    wall = lax.axis_index("wall")
    mine = mine_ref.reshape(4, rows, SUB, LANES)
    copies = []

    def after(i):
        first = jnp.where(wall == 0, i, rows - OUT_ROWS - i)
        at = pl.ds(first, OUT_ROWS)
        copies.append(
            pltpu.make_async_copy(
                mine.at[:, at], out_hbm.at[:, at, pl.ds(SUB * part, SUB), :], sems.at[len(copies)]
            )
        )
        copies[-1].start()

    substitute_kernel(
        rows, part, own_ref, near_ref, own_first_ref, near_first_ref, t_ref, s_ref, mine_ref, after
    )
    for copy in copies:
        copy.wait()


def swap_pairs(count, first):
    pairs = []
    for i in range(first, count + first, 2):
        a, b = i % count, (i + 1) % count
        pairs += [(a, b), (b, a)]
    return pairs


def on_device_pair(potential, concentration, permittivity, fixed_charge):
    rows, planes, cols = potential.shape
    cells = rows * planes
    phi = potential.reshape(cells, cols)
    conc = concentration.reshape(3, cells, cols)
    eps = permittivity.reshape(cells, cols)
    charge = fixed_charge.reshape(cells, cols)
    n_span, n_stream = lax.axis_size("span"), lax.axis_size("stream")

    phi, conc, eps, charge, near, far = pl.pallas_call(
        functools.partial(pack_kernel, rows, planes),
        name="pack",
        out_shape=(
            sds(cells, cols), sds(3, cells, cols), sds(cells, cols), sds(cells, cols),
            sds(5, rows, cols), sds(5, rows, cols),
        ),
        in_specs=[pl.BlockSpec(memory_space=pltpu.HBM)] * 4,
        out_specs=(VMEM,) * 6,
        scratch_shapes=[pltpu.SemaphoreType.DMA((6,))],
        compiler_params=params(),
    )(*(pltpu.with_memory_space_constraint(v, pltpu.HBM) for v in (phi, conc, eps, charge)))

    near_halo = lax.ppermute(near, "span", swap_pairs(n_span, 1))
    far_halo = lax.ppermute(far, "span", swap_pairs(n_span, 0))
    edge_cols, wide = pl.pallas_call(
        functools.partial(columns_kernel, rows, planes),
        name="columns",
        out_shape=(sds(5, SUB, LANES), sds(5, rows * (planes + 1), cols)),
        in_specs=[VMEM] * 3,
        out_specs=(VMEM,) * 2,
        compiler_params=params(),
    )(phi, conc, eps)
    odd_halo = lax.ppermute(edge_cols, "stream", swap_pairs(n_stream, 1))
    even_halo = lax.ppermute(edge_cols, "stream", swap_pairs(n_stream, 0))

    acc, fe, fu = pl.pallas_call(
        functools.partial(assemble_kernel, rows, planes),
        name="assemble",
        out_shape=(sds(NQ, cells, cols), sds(cells, cols), sds(2, 3, cells, cols)),
        in_specs=[VMEM] * 5,
        out_specs=(VMEM,) * 3,
        scratch_shapes=[pltpu.VMEM((NQ, cells + planes, cols), jnp.float32)],
        compiler_params=params(),
        cost_estimate=pl.CostEstimate(flops=12_000_000, bytes_accessed=6_000_000, transcendentals=0),
    )(phi, conc, eps, charge, wide)

    parts = planes // SUB
    across = [(0, 1), (1, 0)]
    kept = (sds(16, rows * SUB, cols), sds(4, rows * SUB, cols))
    terms = (sds(NQ, SUB, LANES), sds(NQ, 2, rows, LANES))
    T, s, tip, side, rim = pl.pallas_call(
        functools.partial(first_eliminate_kernel, rows, planes),
        name="eliminate",
        out_shape=(*kept, sds(20 + 5 * parts, SUB, cols), *terms),
        in_specs=[VMEM] * 13,
        out_specs=(VMEM,) * 5,
        compiler_params=params(),
    )(
        phi, conc, eps, acc, fe, fu, near, far, near_halo, far_halo, edge_cols,
        even_halo, odd_halo,
    )
    solved = [(tip, lax.ppermute(tip, "wall", across), T, s)]
    for part in range(1, parts):
        T, s, tip = pl.pallas_call(
            functools.partial(eliminate_kernel, rows, planes, part),
            name="eliminate",
            out_shape=(*kept, sds(20, SUB, cols)),
            in_specs=[VMEM] * 6,
            out_specs=(VMEM,) * 3,
            compiler_params=params(),
        )(conc, acc, fe, fu, side, rim)
        solved.append((tip, lax.ppermute(tip, "wall", across), T, s))

    fields = solved[0][:2]
    update = ()
    hbm = pl.BlockSpec(memory_space=pltpu.HBM)
    for part, (tip, tip_m, T, s) in enumerate(solved):
        update = pl.pallas_call(
            functools.partial(write_kernel, rows, planes, part),
            name="substitute",
            out_shape=(sds(4, rows, planes, cols),),
            in_specs=[VMEM] * 6 + [hbm] * len(update),
            out_specs=(hbm,),
            scratch_shapes=[
                pltpu.VMEM((4, rows * SUB, cols), jnp.float32),
                pltpu.SemaphoreType.DMA((rows // OUT_ROWS,)),
            ],
            input_output_aliases={6: 0} if update else {},
            compiler_params=params(),
        )(tip, tip_m, *fields, T, s, *update)
    return update[0]


def with_halo(block, sides, width, periodic):
    for axis, dim in sides:
        count = lax.axis_size(axis)
        forward = [(i, i + 1) for i in range(count - 1)]
        if periodic:
            forward.append((count - 1, 0))
        backward = [(target, source) for source, target in forward]
        low = lax.ppermute(
            lax.slice_in_dim(block, block.shape[dim] - width, None, axis=dim), axis, forward
        )
        high = lax.ppermute(lax.slice_in_dim(block, 0, width, axis=dim), axis, backward)
        block = jnp.concatenate([low, block, high], axis=dim)
    return block


def bernoulli(values):
    near_zero = jnp.abs(values) < 0.001
    safe_values = jnp.where(near_zero, 1.0, values)
    series = 1.0 - 0.5 * values + values * values / 12.0
    return jnp.where(near_zero, series, safe_values / jnp.expm1(safe_values))


def block_mul(left_block, right_block):
    return jnp.sum(left_block[:, :, None] * right_block[None, :, :], axis=1)


def invert_small(matrix):
    order_size = matrix.shape[0]
    left_rows = [[matrix[i, j] for j in range(order_size)] for i in range(order_size)]
    blank_entry = jnp.zeros_like(matrix[0, 0])
    right_rows = [
        [blank_entry + (1.0 if i == j else 0.0) for j in range(order_size)]
        for i in range(order_size)
    ]
    for k in range(order_size):
        pivot_inv = 1.0 / left_rows[k][k]
        left_rows[k] = [v * pivot_inv for v in left_rows[k]]
        right_rows[k] = [v * pivot_inv for v in right_rows[k]]
        for i in range(order_size):
            if i != k:
                factor = left_rows[i][k]
                left_rows[i] = [a - factor * b for a, b in zip(left_rows[i], left_rows[k])]
                right_rows[i] = [a - factor * b for a, b in zip(right_rows[i], right_rows[k])]
    return jnp.stack([jnp.stack(r, 0) for r in right_rows], 0)


def block_thomas(lower, diagonal, upper, right_side):

    def forward(carried, row_blocks):
        coupled_prev, solved_prev = carried
        lower_row, diag_row, upper_row, side_row = row_blocks
        reduced = diag_row - block_mul(lower_row, coupled_prev)
        inverse = invert_small(reduced)
        coupled = block_mul(inverse, upper_row)
        solved = block_mul(inverse, side_row - block_mul(lower_row, solved_prev))
        return ((coupled, solved), (coupled, solved))

    initial = (jnp.zeros_like(diagonal[0]), jnp.zeros_like(right_side[0]))
    ignored_end, (coupled_all, solved_all) = lax.scan(
        forward, initial, (lower, diagonal, upper, right_side)
    )

    def backward(following, row_blocks):
        coupled, solved = row_blocks
        current = solved - block_mul(coupled, following)
        return (current, current)

    ignored_start, result = lax.scan(
        backward, jnp.zeros_like(right_side[0]), (coupled_all, solved_all), reverse=True
    )
    return result


def stack_blocks(entries):
    stacked = jnp.stack([jnp.stack([e for e in r], 0) for r in entries], 0)
    return jnp.moveaxis(stacked, 2, 0)


def assemble(center, neighbours, fixed_charge):
    potential, concentration, permittivity = center
    blank_entry = jnp.zeros_like(potential)
    charge = fixed_charge
    for k in range(3):
        charge = charge + VALENCE[k] * concentration[k]
    residual = [-charge, blank_entry, blank_entry, blank_entry]
    jacobian = [[blank_entry] * 4 for i in range(4)]
    lower = [[blank_entry] * 4 for i in range(4)]
    upper = [[blank_entry] * 4 for i in range(4)]
    for k in range(3):
        jacobian[0][k + 1] = blank_entry - VALENCE[k]
    for nearby, inside, weight, position in neighbours:
        near_potential, near_conc, near_perm = nearby
        harmonic = 2.0 * permittivity * near_perm / (permittivity + near_perm)
        face_perm = weight * (inside * harmonic + (1.0 - inside) * permittivity)
        residual[0] = residual[0] + face_perm * (potential - near_potential)
        jacobian[0][0] = jacobian[0][0] + face_perm
        offdiag = lower if position == "lower" else upper if position == "upper" else None
        if offdiag is not None:
            offdiag[0][0] = -inside * face_perm
        for k in range(3):
            drift = VALENCE[k] * (near_potential - potential)
            face_coef = inside * weight * MOBILITY[k]
            weight_out = bernoulli(drift)
            weight_in = bernoulli(-drift)
            mean_conc = 0.5 * (concentration[k] + near_conc[k])
            residual[k + 1] = residual[k + 1] + face_coef * (
                weight_out * concentration[k] - weight_in * near_conc[k]
            )
            jacobian[k + 1][k + 1] = jacobian[k + 1][k + 1] + face_coef * weight_out
            jacobian[k + 1][0] = jacobian[k + 1][0] + face_coef * VALENCE[k] * mean_conc
            if offdiag is not None:
                offdiag[k + 1][k + 1] = -face_coef * weight_in
                offdiag[k + 1][0] = -face_coef * VALENCE[k] * mean_conc
    residual_all = jnp.moveaxis(jnp.stack([e for e in residual], 0), 1, 0)
    return (residual_all, stack_blocks(jacobian), stack_blocks(lower), stack_blocks(upper))


def split_fields(block):
    return (block[0], block[1:4], block[4])


def partition_forward(previous_vec, previous_map, first_tip, last_tip):
    identity = jnp.eye(4, dtype=first_tip.dtype).reshape((4, 4) + (1,) * (first_tip.ndim - 2))
    start_vec = first_tip[:, 0:1]
    start_left = first_tip[:, 1:5]
    start_right = first_tip[:, 5:9]
    end_vec = last_tip[:, 0:1]
    end_left = last_tip[:, 1:5]
    end_right = last_tip[:, 5:9]
    schur_block = identity - block_mul(start_left, previous_map)
    inverse = invert_small(schur_block)
    offset = block_mul(inverse, start_vec + block_mul(start_left, previous_vec))
    reach_map = block_mul(inverse, start_right)
    next_vec = end_vec + block_mul(end_left, previous_vec + block_mul(previous_map, offset))
    next_map = block_mul(end_left, block_mul(previous_map, reach_map)) + end_right
    return (next_vec, next_map, offset, reach_map)


def reduced_sweep(every_tip, zero_vec, zero_map):

    def sweep_forward(carried, tip_pair):
        previous_vec, previous_map = carried
        next_vec, next_map, offset, reach_map = partition_forward(
            previous_vec, previous_map, tip_pair[0], tip_pair[1]
        )
        return ((next_vec, next_map), (previous_vec, previous_map, offset, reach_map))

    ignored_e, (vec_all, map_all, offset_all, reach_all) = lax.scan(
        sweep_forward, (zero_vec, zero_map), every_tip
    )

    def sweep_backward(right_value, pieces):
        offset, reach_map = pieces
        return (offset + block_mul(reach_map, right_value), right_value)

    ignored_f, right_all = lax.scan(sweep_backward, zero_vec, (offset_all, reach_all), reverse=True)
    return (vec_all, map_all, offset_all, reach_all, right_all)


def on_device(potential, concentration, permittivity, fixed_charge):
    cells_wall = potential.shape[0]
    stacked = jnp.concatenate([potential[None], concentration, permittivity[None]], 0)
    walled = with_halo(stacked, (("wall", 1),), 1, False)
    planed = with_halo(stacked, (("stream", 3), ("span", 2)), 1, True)
    center = split_fields(stacked)
    wall_index = lax.axis_index("wall")
    global_row = wall_index * cells_wall + jnp.arange(cells_wall, dtype=jnp.int32)
    line_length = lax.axis_size("wall") * cells_wall
    inside_lower = (global_row > 0).astype(jnp.float32)[:, None, None]
    inside_upper = (global_row < line_length - 1).astype(jnp.float32)[:, None, None]
    neighbours = [
        (split_fields(walled[:, :-2]), inside_lower, 1.0, "lower"),
        (split_fields(walled[:, 2:]), inside_upper, 1.0, "upper"),
        (split_fields(planed[:, :, :-2, 1:-1]), 1.0, PLANE_WEIGHT, "plane"),
        (split_fields(planed[:, :, 2:, 1:-1]), 1.0, PLANE_WEIGHT, "plane"),
        (split_fields(planed[:, :, 1:-1, :-2]), 1.0, PLANE_WEIGHT, "plane"),
        (split_fields(planed[:, :, 1:-1, 2:]), 1.0, PLANE_WEIGHT, "plane"),
    ]
    residual, diagonal, lower, upper = assemble(center, neighbours, fixed_charge)
    row_ids = jnp.arange(cells_wall, dtype=jnp.int32)
    first_mask = (row_ids == 0).astype(jnp.float32)[:, None, None, None, None]
    last_mask = (row_ids == cells_wall - 1).astype(jnp.float32)[:, None, None, None, None]
    right_side = jnp.concatenate(
        [-residual[:, :, None], -lower * first_mask, -upper * last_mask], 2
    )
    solved = block_thomas(lower, diagonal, upper, right_side)
    first_tip = solved[0]
    last_tip = solved[-1]
    lines_shape = first_tip.shape[2:]
    zero_vec = jnp.zeros((4, 1) + lines_shape, jnp.float32)
    zero_map = jnp.zeros((4, 4) + lines_shape, jnp.float32)
    line_tips = jnp.stack([first_tip, last_tip], 0)[None]
    every_tip = lax.all_gather(line_tips, "wall", axis=0, tiled=True)
    vec_all, map_all, offset_all, reach_all, right_all = reduced_sweep(
        every_tip, zero_vec, zero_map
    )

    def choose_own(stacked_all):
        return lax.dynamic_index_in_dim(stacked_all, wall_index, 0, False)

    previous_vec = choose_own(vec_all)
    previous_map = choose_own(map_all)
    offset = choose_own(offset_all)
    reach_map = choose_own(reach_all)
    right_value = choose_own(right_all)
    local_first = offset + block_mul(reach_map, right_value)
    left_value = previous_vec + block_mul(previous_map, local_first)
    update = solved[:, :, 0]
    update = update + jnp.sum(solved[:, :, 1:5] * left_value[None, None, :, 0], axis=2)
    update = update + jnp.sum(solved[:, :, 5:9] * right_value[None, None, :, 0], axis=2)
    return jnp.moveaxis(update, 1, 0)


def on_any(potential, concentration, permittivity, fixed_charge):
    rows, planes, cols = potential.shape
    pair = (
        lax.axis_size("wall") == 2
        and lax.axis_size("span") % 2 == 0
        and lax.axis_size("stream") % 2 == 0
        and cols == LANES
        and rows % SUB == 0
        and planes % SUB == 0
        and rows * planes // SUB * 2 <= LANES
    )
    chosen = on_device_pair if pair else on_device
    return chosen(potential, concentration, permittivity, fixed_charge)


def solution(mesh):
    return jax.shard_map(
        on_any,
        mesh=mesh,
        in_specs=(
            P("wall", "span", "stream"),
            P(None, "wall", "span", "stream"),
            P("wall", "span", "stream"),
            P("wall", "span", "stream"),
        ),
        out_specs=P(None, "wall", "span", "stream"),
        check_vma=False,
    )
```
